32 devices in a mesh: dp: 8 (over y, x, core), seq: 4 (over z).
Axes of the slice: x: 2, y: 2, z: 4, core: 2. Of those that a mesh axis runs over, the one named last changes fastest.
Arguments:
- tokens: bfloat16 [16, 1024, 512], P('dp', 'seq'), may hold values from -6 to 6
- memory: bfloat16 [16, 1024, 512], P('dp', 'seq'), may hold values from -6 to 6
- tgt_segments: int32 [16, 1024], P('dp'), may hold values from 0 to 2, as said below
- mem_segments: int32 [16, 1024], P('dp'), may hold values from 0 to 2, as said below
- cotangent: bfloat16 [16, 1024, 512], P('dp', 'seq'), may hold values from -6 to 6
- w_qkv: bfloat16 [512, 1536], replicated, may hold values from -0.25 to 0.25
- w_self_out: bfloat16 [512, 512], replicated, may hold values from -1.5 to 1.5
- w_cross_q: bfloat16 [512, 512], replicated, may hold values from -0.25 to 0.25
- w_cross_kv: bfloat16 [512, 1024], replicated, may hold values from -0.25 to 0.25
- w_cross_out: bfloat16 [512, 512], replicated, may hold values from -1.5 to 1.5
- w_up: bfloat16 [512, 2048], replicated, may hold values from -0.25 to 0.25
- w_down: bfloat16 [2048, 512], replicated, may hold values from -0.125 to 0.125
- ln1_gain: float32 [512], replicated, may hold values from 0.25 to 1.75
- ln1_bias: float32 [512], replicated, may hold values from -1.8 to 1.8
- ln2_gain: float32 [512], replicated, may hold values from 0.25 to 1.75
- ln2_bias: float32 [512], replicated, may hold values from -1.8 to 1.8
- ln3_gain: float32 [512], replicated, may hold values from 0.25 to 1.75
- ln3_bias: float32 [512], replicated, may hold values from -1.8 to 1.8
Outputs:
- output: bfloat16 [16, 1024, 512], P('dp', 'seq')
- grad_tokens: float32 [16, 1024, 512], P('dp', 'seq')
- grad_memory: float32 [16, 1024, 512], P('dp', 'seq')
- grad_w_qkv: float32 [512, 1536], replicated
- grad_w_self_out: float32 [512, 512], replicated
- grad_w_cross_q: float32 [512, 512], replicated
- grad_w_cross_kv: float32 [512, 1024], replicated
- grad_w_cross_out: float32 [512, 512], replicated
- grad_w_up: float32 [512, 2048], replicated
- grad_w_down: float32 [2048, 512], replicated
- grad_ln1_gain: float32 [512], replicated
- grad_ln1_bias: float32 [512], replicated
- grad_ln2_gain: float32 [512], replicated
- grad_ln2_bias: float32 [512], replicated
- grad_ln3_gain: float32 [512], replicated
- grad_ln3_bias: float32 [512], replicated
The draws below stay inside these ranges and needn't reach their ends.
Inputs may be any that keep to these rules, and one draw needn't show every extreme that they name: `tgt_segments`: along a row the ids never fall and all three occur; document 1 begins within the row's first 256 positions and ends within its last 256. `mem_segments`: along a row the ids never fall and all three occur.
All inputs are finite; a program needn't handle non-finite values.
Results may differ from the reference program's by a relative error of at most 0.02.
Values may be sent and summed in bfloat16 or wider, within the bound.
No kernel may reach another device: no remote copies, remote signals or barrier semaphores. Data moves between devices by JAX's collectives and lax.ppermute only.
A program may use at most 128 MiB of HBM per device.

```python
import jax
import jax.numpy as jnp
from jax import lax

D = 512
HEADS = 8
HEAD_DIM = 64
FF = 2048
LEN = 1024
MLEN = 1024
ROWS = 16
TOK_SEQ = 256
MEM_SEQ = 256


def three_documents(key, row_total, length, edge_size, late_shift):
    first_key, second_key = jax.random.split(key)
    first_cut = jax.random.randint(first_key, (row_total, 1), 1, edge_size)
    second_cut = jax.random.randint(second_key, (row_total, 1), length - edge_size + late_shift, length)
    place = jnp.arange(length)[None, :]
    return (place >= first_cut).astype(jnp.int32) + (place >= second_cut).astype(jnp.int32)


def draw_tgt_segments(key, part):
    return three_documents(jax.random.fold_in(key, 17), ROWS, LEN, TOK_SEQ, 1)


def draw_mem_segments(key, part):
    return three_documents(jax.random.fold_in(key, 29), ROWS, MLEN, MEM_SEQ, 0)


def block_levels(own_key, extent, cuts, low, top_value):
    def one(axis_at, parts):
        draws = jax.random.uniform(jax.random.fold_in(jax.random.fold_in(own_key, 6), axis_at), (parts,), jnp.float32, low / len(cuts), top_value / len(cuts))
        return jnp.repeat(jnp.exp(draws), extent[axis_at] // parts).reshape((-1,) + (1,) * (len(extent) - axis_at - 1))

    level = one(*cuts[0])
    for cut in cuts[1:]:
        level = level * one(*cut)
    return level


def bell_draw(rng, shape, deviation, limit, cuts=(), kind=jnp.bfloat16):
    array = jax.random.normal(rng, shape, jnp.float32) * deviation
    if len(cuts) > 0:
        array = block_levels(rng, shape, cuts, -0.22, 0.18) * array
    return jnp.clip(array, min=-limit, max=limit).astype(kind)


def setup_inputs(seed: int = 0) -> dict:
    key_of = jax.random.split(jax.random.key(seed), 19)
    tokens = bell_draw(key_of[0], (ROWS, LEN, D), 1.0, 6.0, ((0, 8), (1, 4)))
    memory = bell_draw(key_of[1], (ROWS, MLEN, D), 1.0, 6.0, ((0, 8), (1, 4)))
    tgt_segments = draw_tgt_segments(jax.random.fold_in(key_of[18], 71), 0)
    mem_segments = draw_mem_segments(jax.random.fold_in(key_of[18], 71), 0)
    cotangent = bell_draw(key_of[4], (ROWS, LEN, D), 1.0, 6.0, ((0, 8), (1, 4)))
    w_qkv = bell_draw(key_of[5], (D, 3 * D), D ** -0.5, 0.25)
    w_self_out = bell_draw(key_of[6], (D, D), (D // 32) ** -0.5, 1.5)
    w_cross_q = bell_draw(key_of[7], (D, D), D ** -0.5, 0.25)
    w_cross_kv = bell_draw(key_of[8], (D, 2 * D), D ** -0.5, 0.25)
    w_cross_out = bell_draw(key_of[9], (D, D), (D // 32) ** -0.5, 1.5)
    w_up = bell_draw(key_of[10], (D, FF), D ** -0.5, 0.25)
    w_down = bell_draw(key_of[11], (FF, D), FF ** -0.5, 0.125)
    ln1_gain = jnp.clip(1.0 + 0.15 * jax.random.normal(key_of[12], (D,), jnp.float32), 0.25, 1.75)
    ln1_bias = bell_draw(key_of[13], (D,), 0.3, 1.8, (), jnp.float32)
    ln2_gain = jnp.clip(1.0 + 0.15 * jax.random.normal(key_of[14], (D,), jnp.float32), 0.25, 1.75)
    ln2_bias = bell_draw(key_of[15], (D,), 0.3, 1.8, (), jnp.float32)
    ln3_gain = jnp.clip(1.0 + 0.15 * jax.random.normal(key_of[16], (D,), jnp.float32), 0.25, 1.75)
    ln3_bias = bell_draw(key_of[17], (D,), 0.3, 1.8, (), jnp.float32)
    return dict(tokens=tokens, memory=memory, tgt_segments=tgt_segments, mem_segments=mem_segments, cotangent=cotangent, w_qkv=w_qkv, w_self_out=w_self_out, w_cross_q=w_cross_q, w_cross_kv=w_cross_kv, w_cross_out=w_cross_out, w_up=w_up, w_down=w_down, ln1_gain=ln1_gain, ln1_bias=ln1_bias, ln2_gain=ln2_gain, ln2_bias=ln2_bias, ln3_gain=ln3_gain, ln3_bias=ln3_bias)


@jax.custom_vjp
def low(v):
    return lax.optimization_barrier(v.astype(jnp.bfloat16)).astype(jnp.float32)

@jax.custom_vjp
def low_back(v):
    return v

def low_keep(v):
    return (low(v), None)

def low_pass(kept, grad):
    return (grad,)

def back_keep(v):
    return (v, None)

def back_low(kept, grad):
    return (low(grad),)
low.defvjp(low_keep, low_pass)
low_back.defvjp(back_keep, back_low)

def matmul(left, right):
    return jnp.dot(left, right, precision=lax.Precision.HIGHEST)

def normalize(values, gain, bias):
    centre = values - lax.optimization_barrier(jnp.mean(values, axis=-1, keepdims=True))
    spread = lax.optimization_barrier(jnp.mean(centre * centre, axis=-1, keepdims=True))
    return centre * lax.rsqrt(spread + 1e-05) * gain + bias

def attend(queries, key_rows, value_rows, allowed):
    q_len = queries.shape[0]
    k_len = key_rows.shape[0]
    q_heads = queries.reshape(q_len, HEADS, HEAD_DIM)
    k_heads = key_rows.reshape(k_len, HEADS, HEAD_DIM)
    v_heads = value_rows.reshape(k_len, HEADS, HEAD_DIM)
    raw_scores = jnp.einsum('qhd,khd->hqk', q_heads, k_heads, precision=lax.Precision.HIGHEST)
    scores = low_back(raw_scores * HEAD_DIM ** (-0.5))
    scores = jnp.where(allowed[None], scores, -1000000000.0)
    highest = lax.optimization_barrier(jnp.max(scores, axis=-1, keepdims=True))
    expo = jnp.exp(scores - highest)
    probs = expo / lax.optimization_barrier(jnp.sum(expo, axis=-1, keepdims=True))
    context = jnp.einsum('hqk,khd->qhd', low(probs), v_heads, precision=lax.Precision.HIGHEST)
    return low_back(low(context)).reshape(q_len, HEADS * HEAD_DIM)

def layer(params, row_tokens, row_memory, tgt_row, mem_row):
    w_qkv, w_self_out, w_cross_q, w_cross_kv, w_cross_out, w_up, w_down, ln1_gain, ln1_bias, ln2_gain, ln2_bias, ln3_gain, ln3_bias = params
    length = row_tokens.shape[0]
    place = jnp.arange(length)
    causal = (place[None, :] <= place[:, None]) & (tgt_row[:, None] == tgt_row[None, :])
    crossing = tgt_row[:, None] == mem_row[None, :]
    mixed_proj = low_back(low(matmul(row_tokens, w_qkv)))
    self_context = attend(mixed_proj[:, :D], mixed_proj[:, D:2 * D], mixed_proj[:, 2 * D:], causal)
    attended = low_back(matmul(self_context, w_self_out))
    first_norm = normalize(row_tokens + attended, ln1_gain, ln1_bias)
    cross_query = low_back(low(matmul(low(first_norm), w_cross_q)))
    memory_kv = low_back(low(matmul(row_memory, w_cross_kv)))
    cross_context = attend(cross_query, memory_kv[:, :D], memory_kv[:, D:], crossing)
    crossed = low_back(matmul(cross_context, w_cross_out))
    second_norm = normalize(first_norm + crossed, ln2_gain, ln2_bias)
    pre_act = low_back(matmul(low(second_norm), w_up))
    hidden = low(pre_act * jax.nn.sigmoid(pre_act))
    fed = low_back(matmul(hidden, w_down))
    return normalize(second_norm + fed, ln3_gain, ln3_bias)

def reference(tokens, memory, tgt_segments, mem_segments, cotangent, w_qkv, w_self_out, w_cross_q, w_cross_kv, w_cross_out, w_up, w_down, ln1_gain, ln1_bias, ln2_gain, ln2_bias, ln3_gain, ln3_bias):
    params = (w_qkv.astype(jnp.float32), w_self_out.astype(jnp.float32), w_cross_q.astype(jnp.float32), w_cross_kv.astype(jnp.float32), w_cross_out.astype(jnp.float32), w_up.astype(jnp.float32), w_down.astype(jnp.float32), ln1_gain.astype(jnp.float32), ln1_bias.astype(jnp.float32), ln2_gain.astype(jnp.float32), ln2_bias.astype(jnp.float32), ln3_gain.astype(jnp.float32), ln3_bias.astype(jnp.float32))

    def forward(params_now, token_rows, memory_rows):

        def one_row(row_item):
            return layer(params_now, row_item[0], row_item[1], row_item[2], row_item[3])
        return lax.map(jax.checkpoint(one_row), (token_rows, memory_rows, tgt_segments, mem_segments))
    outputs, pullback = jax.vjp(forward, params, tokens.astype(jnp.float32), memory.astype(jnp.float32))
    grad_params, grad_tokens, grad_memory = pullback(cotangent.astype(jnp.float32))
    return (outputs.astype(jnp.bfloat16), grad_tokens, grad_memory, grad_params[0], grad_params[1], grad_params[2], grad_params[3], grad_params[4], grad_params[5], grad_params[6], grad_params[7], grad_params[8], grad_params[9], grad_params[10], grad_params[11], grad_params[12])
```

```python
import functools

import jax
import jax.numpy as jnp
import numpy as np
from jax import lax
from jax.experimental import pallas as pl
from jax.experimental.pallas import tpu as pltpu
from jax.sharding import PartitionSpec as P

F32 = jnp.float32
BF16 = jnp.bfloat16
HEAD_DIM = 64
AUG = 2 * HEAD_DIM
QB = 256
OFF = -1e9
AXES = ("dp", "seq")
COST = 3e8
VM = pl.BlockSpec(memory_space=pltpu.VMEM)
SM = pl.BlockSpec(memory_space=pltpu.SMEM)
HB = pl.BlockSpec(memory_space=pl.ANY)


def dg(a, b, ca, cb):
    return lax.dot_general(a, b, (((ca,), (cb,)), ((), ())), preferred_element_type=F32)


class Plan:
    def __init__(self, mesh, rows, tok):
        dp, seq = mesh.shape["dp"], mesh.shape["seq"]
        self.dp, self.seq, self.rows, self.tok = dp, seq, rows, tok
        self.pair_in_dp = seq == 4
        assert rows * 2 == seq and seq in (4, 8)
        if self.pair_in_dp:
            dev = lambda k, c, h: (2 * k + h) * seq + c
            team_row = lambda h, j: 2 * h + j
            start = lambda c, h: c
            teams = dp // 2
            self.core = ("dp", 0)
            chips, line = self.bits("dp", 1, dp), self.bits("seq", 0, seq)
        else:
            dev = lambda k, c, h: k * seq + 2 * c + h
            team_row = lambda h, j: j
            start = lambda c, h: 2 * c + h
            teams = dp
            self.core = ("seq", 0)
            chips, line = self.bits("dp", 0, dp), self.bits("seq", 1, seq)
        count = dp * seq
        own = {0: (0, 3), 1: (1, 2)}
        half_of = {0: 0, 3: 0, 1: 1, 2: 1}
        todo = []
        for c in range(4):
            for h in range(2):
                for j in range(rows):
                    block = start(c, h) * tok // QB
                    todo.append(((c, h), (team_row(h, j), half_of[block]), j, start(c, h)))
        self.perms = []
        self.send_row = np.zeros((count, rows), np.int32)
        self.recv_at = np.zeros((count, rows), np.int32)
        nodes = [(c, h) for c in range(4) for h in range(2)]
        for turn in range(rows):
            match = {}

            def grow(src, seen):
                for e in todo:
                    if e[0] == src and e[1] not in seen:
                        seen.add(e[1])
                        if e[1] not in match or grow(match[e[1]][0], seen):
                            match[e[1]] = e
                            return True
                return False

            for src in nodes:
                assert grow(src, set())
            pairs = []
            for e in match.values():
                todo.remove(e)
                for k in range(teams):
                    s, d = dev(k, *e[0]), dev(k, *e[1])
                    pairs.append((s, d))
                    self.send_row[s, turn] = e[2]
                    self.recv_at[d, turn] = e[3]
            self.perms.append(sorted(pairs))
        place = np.zeros(count, np.int32)
        half, chip = np.zeros(count, np.int32), np.zeros(count, np.int32)
        sibling = np.zeros(count, np.int32)
        for k in range(teams):
            for c in range(4):
                for h in range(2):
                    d = dev(k, c, h)
                    half[d], chip[d], place[d] = h, c, 2 * c + h
                    sibling[d] = dev(k, c, 1 - h)
        self.codes = {}

        def add(name, values):
            by_place = [int(np.asarray(values)[place == p][0]) for p in range(8)]
            assert all(by_place[p] == v for p, v in zip(place, values))
            self.codes[name] = by_place

        add("half", half)
        add("lo", half)
        add("hi", 3 - half)
        if self.pair_in_dp:
            add("seg_far", (chip // 2 != half).astype(np.int32))
            add("seg_row", chip % 2)
        else:
            add("seg_far", np.zeros(count, np.int32))
            add("seg_row", chip)
        for t in range(rows):
            pos = self.recv_at[:, t] * tok
            add("own%d" % t, self.recv_at[:, t])
            add("sib%d" % t, self.recv_at[sibling, t])
            add("loc%d" % t, (np.where(pos // QB == half, 0, QB) + pos % QB) // tok)
            add("row%d" % t, self.send_row[:, t])
        far = len(chips) // 2
        self.steps = []
        for p, q in zip(chips[:far], chips[far:]):
            self.steps += [(p, q), (q, p)]
        self.stages = self.groups("dp", chips[2 * far :], dp) + self.groups("seq", line, seq)
        self.bit_names = {}
        for i, step in enumerate(self.steps):
            for side, bit in zip("ab", step):
                self.bit_names["step%d%s" % (i, side)] = (bit[0], bit[1], 1)
        self.at = {name: i for i, name in enumerate([*self.codes, *self.bit_names])}

    def scalars(self):
        dp, seq = lax.axis_index("dp"), lax.axis_index("seq")
        place = 2 * seq + (dp & 1) if self.pair_in_dp else seq
        out = {}
        for name, by_place in self.codes.items():
            code = sum(v << (3 * p) for p, v in enumerate(by_place))
            out[name] = (jnp.int32(code) >> (3 * place)) & 7
        for name, (axis, shift, mask) in self.bit_names.items():
            out[name] = ((dp if axis == "dp" else seq) >> shift) & mask
        return out

    @staticmethod
    def bits(axis, shift, size):
        return [(axis, i) for i in range(shift, size.bit_length() - 1)]


    @staticmethod
    def groups(axis, bits, size):
        out = []
        bits = [shift for _, shift in bits]
        while bits:
            now, bits = bits[:2], bits[2:]
            mask = sum(1 << b for b in now)
            rest = [i for i in range(size) if not i & mask]
            steps = [0]
            for b in now:
                steps += [v + (1 << b) for v in steps]
            out.append((axis, len(steps), [[i + v for v in steps] for i in rest]))
        return out


def trade(x, stage):
    axis, _, groups = stage
    return lax.all_to_all(x, axis, 0, 0, axis_index_groups=groups, tiled=True)


def swap(x, plan, bit):
    axis, shift = bit
    n = plan.dp if axis == "dp" else plan.seq
    return lax.ppermute(x, axis, [(i, i ^ (1 << shift)) for i in range(n)])


def norm_forward(y):
    centre = y - jnp.mean(y, axis=-1, keepdims=True)
    recip = lax.rsqrt(jnp.mean(centre * centre, axis=-1, keepdims=True) + 1e-05)
    return centre * recip, recip


def norm_back(grad, normed, recip, gain):
    d_gain = jnp.sum(grad * normed, axis=0, keepdims=True)
    d_bias = jnp.sum(grad, axis=0, keepdims=True)
    scaled = grad * gain
    d_in = recip * (
        scaled
        - jnp.mean(scaled, axis=-1, keepdims=True)
        - normed * jnp.mean(scaled * normed, axis=-1, keepdims=True)
    )
    return d_in, d_gain, d_bias


def augment(dst, x, tail):
    for h in range(x.shape[1] // HEAD_DIM):
        dst[:, h * AUG : (h + 1) * AUG] = jnp.concatenate(
            [x[:, h * HEAD_DIM : (h + 1) * HEAD_DIM], tail], axis=1
        )


def ones_tail(n):
    return (lax.broadcasted_iota(jnp.int32, (n, HEAD_DIM), 1) == 0).astype(BF16)


def head_forward(q, k, v, tri):
    s = dg(q, k, 1, 1)
    n = k.shape[0]
    if tri is not None:
        edge = s[:, n - QB :] + tri
        s = edge if n == QB else jnp.concatenate([s[:, : n - QB], edge], axis=1)
    e = jnp.exp(s - jnp.max(s, axis=1, keepdims=True)).astype(BF16)
    cv = dg(e, v, 1, 0)
    recip = 1.0 / cv[:, HEAD_DIM : HEAD_DIM + 1]
    return e, (cv[:, :HEAD_DIM] * recip).astype(BF16), recip


def gather_rows(tab, plan, parts, dst, sems, base):
    out = []
    n = plan.rows
    for i, ref in enumerate(parts):
        name = "own%d" % i if i < n else "sib%d" % (i - n)
        at = pl.multiple_of(tab[plan.at[name]] * plan.tok, plan.tok)
        cp = pltpu.make_async_copy(ref, dst.at[pl.ds(at, plan.tok)], sems.at[base + i])
        cp.start()
        out.append(cp)
    return out


def start_all(pairs, sems, base):
    out = []
    for i, (src, dst) in enumerate(pairs):
        cp = pltpu.make_async_copy(src, dst, sems.at[base + i])
        cp.start()
        out.append(cp)
    return out


def wait_all(copies):
    for cp in copies:
        cp.wait()


def call(kernel, ins, in_specs, outs, out_specs, scratch, us, mib=44, deps=()):
    first, extra = len(ins), len(deps)

    def run(*refs):
        kernel(*refs[:first], *refs[first + extra :])

    return pl.pallas_call(
        run,
        out_shape=[jax.ShapeDtypeStruct(s, d) for s, d in outs],
        in_specs=in_specs + [HB] * extra,
        out_specs=out_specs,
        scratch_shapes=scratch,
        compiler_params=pltpu.CompilerParams(vmem_limit_bytes=mib * 2**20),
        cost_estimate=pl.CostEstimate(flops=int(us * COST), bytes_accessed=2**20, transcendentals=0),
    )(*ins, *deps)


def self_forward(plan, heads, tab, *refs):
    n = plan.rows
    parts, refs = refs[: 2 * n], refs[2 * n :]
    (wqkv, wso, wcq, qf, kf, g1, b1, e_out, k_out, v_out, q_out, rl_out, c_out, n_out, r_out, cq_out) = refs[:16]
    x_s, w_s, wo_s, wc_s, k_s, v_s, e_s, sems = refs[16:]
    width = heads * HEAD_DIM
    pieces = gather_rows(tab, plan, parts, x_s, sems, 0)
    weights = start_all([(wqkv, w_s), (wso, wo_s), (wcq, wc_s)], sems, 2 * n)
    lo = pl.multiple_of(tab[plan.at["lo"]] * QB, QB)
    hi = pl.multiple_of(tab[plan.at["hi"]] * QB, QB)
    weights[0].wait()
    wait_all(pieces)
    k = dg(x_s[...], w_s[:, width : 2 * width], 1, 0).astype(BF16)
    augment(k_s, k, kf[...])
    v = dg(x_s[...], w_s[:, 2 * width :], 1, 0).astype(BF16)
    augment(v_s, v, ones_tail(v.shape[0]))
    x_own = jnp.concatenate([x_s[pl.ds(lo, QB)], x_s[pl.ds(hi, QB)]], axis=0)
    q_out[...] = (dg(x_own, w_s[:, :width], 1, 0).astype(BF16).astype(F32) * 0.125).astype(BF16)
    kv_copies = start_all([(k_s, k_out), (v_s, v_out)], sems, 2 * n + 3)
    qf_own = jnp.concatenate([qf[pl.ds(lo, QB)], qf[pl.ds(hi, QB)]], axis=0)
    tri = jnp.where(
        lax.broadcasted_iota(jnp.int32, (QB, QB), 1) <= lax.broadcasted_iota(jnp.int32, (QB, QB), 0),
        0.0,
        OFF,
    )

    def attend(core):
        sizes = (QB * (core + 1), QB * (4 - core))
        for h in range(heads):
            at = 0
            for i, keys in enumerate(sizes):
                rows = slice(i * QB, (i + 1) * QB)
                cols = slice(h * HEAD_DIM, (h + 1) * HEAD_DIM)
                q = jnp.concatenate([q_out[rows, cols], qf_own[rows]], axis=1)
                wide = slice(h * AUG, (h + 1) * AUG)
                e, c, recip = head_forward(q, k_s[:keys, wide], v_s[:keys, wide], tri)
                e_s[h, :, at : at + keys] = e
                c_out[rows, cols] = c
                rl_out[rows, h : h + 1] = recip
                at += keys
            pltpu.make_async_copy(e_s.at[h], e_out.at[h], sems.at[2 * n + 5 + h]).start()

    for core in range(2):
        pl.when(tab[plan.at["half"]] == core)(functools.partial(attend, core))
    wait_all(weights[1:])
    y = x_own.astype(F32) + dg(c_out[...], wo_s[...], 1, 0)
    normed, recip = norm_forward(y)
    n_out[...] = normed
    r_out[...] = recip
    z = (normed * g1[...] + b1[...]).astype(BF16)
    cq_out[...] = (dg(z, wc_s[...], 1, 0).astype(BF16).astype(F32) * 0.125).astype(BF16)
    wait_all(kv_copies)
    for h in range(heads):
        pltpu.make_async_copy(e_s.at[h], e_out.at[h], sems.at[2 * n + 5 + h]).wait()


def cross_forward(plan, heads, tab, *refs):
    n = plan.rows
    parts, refs = refs[: 2 * n], refs[2 * n :]
    (wckv, wco, cq, n1, qf, kf, g1, b1, e_out, k_out, v_out, rl_out, c_out, n_out, r_out) = refs[:15]
    m_s, w_s, wo_s, k_s, v_s, e_s, sems = refs[15:]
    width = heads * HEAD_DIM
    pieces = gather_rows(tab, plan, parts, m_s, sems, 0)
    weights = start_all([(wckv, w_s), (wco, wo_s)], sems, 2 * n)
    lo = pl.multiple_of(tab[plan.at["lo"]] * QB, QB)
    hi = pl.multiple_of(tab[plan.at["hi"]] * QB, QB)
    qf_own = jnp.concatenate([qf[pl.ds(lo, QB)], qf[pl.ds(hi, QB)]], axis=0)
    weights[0].wait()
    wait_all(pieces)
    k = dg(m_s[...], w_s[:, :width], 1, 0).astype(BF16)
    augment(k_s, k, kf[...])
    v = dg(m_s[...], w_s[:, width:], 1, 0).astype(BF16)
    augment(v_s, v, ones_tail(v.shape[0]))
    kv_copies = start_all([(k_s, k_out), (v_s, v_out)], sems, 2 * n + 3)
    copies = []
    for h in range(heads):
        for i in range(2):
            rows = slice(i * QB, (i + 1) * QB)
            cols = slice(h * HEAD_DIM, (h + 1) * HEAD_DIM)
            q = jnp.concatenate([cq[rows, cols], qf_own[rows]], axis=1)
            wide = slice(h * AUG, (h + 1) * AUG)
            e, c, recip = head_forward(q, k_s[:, wide], v_s[:, wide], None)
            e_s[h, rows] = e
            c_out[rows, cols] = c
            rl_out[rows, h : h + 1] = recip
        copies += start_all([(e_s.at[h], e_out.at[h])], sems, 2 * n + 5 + h)
    weights[1].wait()
    y = n1[...] * g1[...] + b1[...] + dg(c_out[...], wo_s[...], 1, 0)
    normed, recip = norm_forward(y)
    n_out[...] = normed
    r_out[...] = recip
    wait_all(kv_copies + copies)


def feed(plan, tab, *refs):
    n = plan.rows
    parts, refs = refs[:n], refs[n:]
    (wup, wdown, n2, g2, b2, g3, b3) = refs[:7]
    outs, refs = refs[7 : 7 + n], refs[7 + n :]
    f_send, f_keep, du_out, dy_out, small_out = refs[:5]
    g_s, wu_s, wd_s, h_s, d_s, o_s, fs_s, fk_s, sems = refs[5:]
    width = n2.shape[1]
    ff = wup.shape[1]
    half = ff // 2
    weights = start_all([(wup, wu_s), (wdown, wd_s)], sems, n)
    grads = []
    for t in range(n):
        at = pl.multiple_of(tab[plan.at["loc%d" % t]] * plan.tok, plan.tok)
        grads += start_all([(parts[t], g_s.at[pl.ds(at, plan.tok)])], sems, t)
    z2 = n2[...] * g2[...] + b2[...]
    z2b = z2.astype(BF16)
    fed = jnp.zeros(z2.shape, F32)
    wait_all(weights)
    for i in range(0, ff, width):
        cols = slice(i, i + width)
        u = dg(z2b, wu_s[:, cols], 1, 0)
        sig = 1.0 / (1.0 + jnp.exp(-u))
        h_s[:, cols] = (u * sig).astype(BF16)
        d_s[:, cols] = (sig * (1.0 + u * (1.0 - sig))).astype(BF16)
        fed += dg(h_s[:, cols], wd_s[cols, :], 1, 0)
    n3, r3 = norm_forward(z2 + fed)
    o_s[...] = (n3 * g3[...] + b3[...]).astype(BF16)
    out_copies = []
    for t in range(n):
        at = pl.multiple_of(tab[plan.at["loc%d" % t]] * plan.tok, plan.tok)
        out_copies += start_all([(o_s.at[pl.ds(at, plan.tok)], outs[t])], sems, n + 2 + t)
    wait_all(grads)
    dy3, dg3, db3 = norm_back(g_s[...].astype(F32), n3, r3, g3[...])
    dy_out[...] = dy3
    small_out[...] = jnp.concatenate([dg3, db3, jnp.zeros((6, width), F32)], axis=0)
    dfb = dy3.astype(BF16)
    mine = tab[plan.at["half"]]
    sides = ((fs_s, 1 - mine), (fk_s, mine))
    for dst, side in sides:
        at = pl.multiple_of(side * half, half)
        dst[:half] = dg(h_s[:, pl.ds(at, half)], dfb, 0, 0).astype(BF16)
    for i in range(0, ff, width):
        cols = slice(i, i + width)
        d_s[:, cols] = (dg(dfb, wd_s[cols, :], 1, 1) * d_s[:, cols].astype(F32)).astype(BF16)
    f_copies = start_all([(d_s, du_out)], sems, 2 * n + 4)
    for s, (dst, side) in enumerate(sides):
        for i in range(half // width):
            at = pl.multiple_of(side * half + i * width, width)
            rows = slice(half + i * width, half + (i + 1) * width)
            dst[rows] = dg(z2b, d_s[:, pl.ds(at, width)], 0, 0).astype(BF16)
        f_copies += start_all([(dst, (f_send, f_keep)[s])], sems, 2 * n + 2 + s)
    wait_all(out_copies + f_copies)


def feed_inputs(du, wup, dy3, n2, r2, g2, small_in, dy_out, small_out):
    dz2 = dy3[...] + dg(du[...], wup[...], 1, 1)
    dy2, dg2, db2 = norm_back(dz2, n2[...], r2[...], g2[...])
    dy_out[...] = dy2
    small_out[...] = jnp.concatenate([dg2, db2, small_in[:6]], axis=0)


def context_grad(dy, w, c, rl, first, heads, dc_s, dd_s):
    group = slice(first * HEAD_DIM, (first + heads) * HEAD_DIM)
    dc = dg(dy[...].astype(BF16), w[group], 1, 1)
    cf = c[:, group].astype(F32)
    for h in range(heads):
        cols = slice(h * HEAD_DIM, (h + 1) * HEAD_DIM)
        part = dc[:, cols] * rl[:, first + h : first + h + 1]
        dc_s[:, cols] = part.astype(BF16)
        dd_s[:, h : h + 1] = jnp.sum(part * cf[:, cols], axis=1, keepdims=True)
    return group


def cross_heads(first, heads, *refs):
    (e_in, k_in, v_in, wo, dy, c, rl, q) = refs[:8]
    kv_out, dq_out = refs[8:10]
    e_s, k_s, v_s, dc_s, dd_s, ds_s, sems = refs[10:]
    wide = pl.ds(first * AUG, heads * AUG)
    copies = start_all([(v_in.at[:, wide], v_s), (k_in.at[:, wide], k_s)], sems, 0)
    e_copies = start_all([(e_in.at[first + h], e_s.at[h]) for h in range(heads)], sems, 2)
    group = context_grad(dy, wo, c, rl, first, heads, dc_s, dd_s)
    dct = dc_s[...].T
    qt = q[:, group].T
    half = heads * HEAD_DIM
    wait_all(copies)
    for h in range(heads):
        cols = slice(h * HEAD_DIM, (h + 1) * HEAD_DIM)
        wide = slice(h * AUG, h * AUG + HEAD_DIM)
        e_copies[h].wait()
        for i in range(2):
            rows = slice(i * QB, (i + 1) * QB)
            dp = dg(dc_s[rows, cols], v_s[:, wide], 1, 1)
            ds_s[rows] = (e_s[h, rows].astype(F32) * (dp - dd_s[rows, h : h + 1])).astype(BF16)
        kv_out[half + h * HEAD_DIM : half + (h + 1) * HEAD_DIM] = dg(dct[cols], e_s[h], 1, 0).astype(BF16)
        kv_out[cols] = dg(qt[cols], ds_s[...], 1, 0).astype(BF16)
        dq_out[:, cols] = (dg(ds_s[...], k_s[:, wide], 1, 0) * 0.125).astype(BF16)


def self_heads(plan, first, heads, tab, *refs):
    (e_in, k_in, v_in, wo, dy, c, rl, q) = refs[:8]
    kv_out, dq_out = refs[8:10]
    e_s, k_s, v_s, dc_s, dd_s, sems = refs[10:]
    wide = pl.ds(first * AUG, heads * AUG)
    copies = start_all([(v_in.at[:, wide], v_s), (k_in.at[:, wide], k_s)], sems, 0)
    e_copies = start_all([(e_in.at[first + h], e_s.at[h]) for h in range(heads)], sems, 2)
    group = context_grad(dy, wo, c, rl, first, heads, dc_s, dd_s)
    dct = dc_s[...].T
    qt = q[:, group].T
    half = heads * HEAD_DIM
    wait_all(copies + e_copies)

    def attend(core):
        n_lo, n_hi = QB * (core + 1), QB * (4 - core)
        total = k_s.shape[0]
        for h in range(heads):
            cols = slice(h * HEAD_DIM, (h + 1) * HEAD_DIM)
            wide = slice(h * AUG, h * AUG + HEAD_DIM)
            sums = []
            at = 0
            for i, keys in enumerate((n_lo, n_hi)):
                rows = slice(i * QB, (i + 1) * QB)
                e = e_s[h, :, at : at + keys]
                dp = dg(dc_s[rows, cols], v_s[:keys, wide], 1, 1)
                ds = (e.astype(F32) * (dp - dd_s[rows, h : h + 1])).astype(BF16)
                dq_out[rows, cols] = (dg(ds, k_s[:keys, wide], 1, 0) * 0.125).astype(BF16)
                sums.append((dg(qt[cols, rows], ds, 1, 0), dg(dct[cols, rows], e, 1, 0)))
                at += keys
            for j in range(2):
                small, large = sums[0][j], sums[1][j]
                at = j * half + h * HEAD_DIM
                rows = slice(at, at + HEAD_DIM)
                kv_out[rows, :n_lo] = (small + large[:, :n_lo]).astype(BF16)
                kv_out[rows, n_lo:n_hi] = large[:, n_lo:].astype(BF16)
                if n_hi < total:
                    kv_out[rows, n_hi:] = jnp.zeros((HEAD_DIM, total - n_hi), BF16)

    for core in range(2):
        pl.when(tab[plan.at["half"]] == core)(functools.partial(attend, core))


def stack_heads(parts, dst):
    half = parts[0].shape[0] // 2
    for j in range(2):
        for i, p in enumerate(parts):
            at = (j * len(parts) + i) * half
            dst[at : at + half] = p[j * half : (j + 1) * half]


def share_rows(plan, tab, src, send, keep):
    n, tok = plan.rows, plan.tok
    for t in range(n):
        for name, dst in (("sib%d", send), ("own%d", keep)):
            at = pl.multiple_of(tab[plan.at[name % t]] * tok, tok)
            dst[t * tok : (t + 1) * tok] = src[pl.ds(at, tok)].astype(BF16)


def cross_dense(plan, groups, tab, *refs):
    n = plan.rows
    parts, refs = refs[: 2 * n], refs[2 * n :]
    kvs, refs = refs[:groups], refs[groups:]
    dqs, refs = refs[:groups], refs[groups:]
    (wckv, wcq, dy2, c2, n1, r1, g1, b1, c1, small_in) = refs[:10]
    c_send, c_keep, m_send, m_keep, dy_out = refs[10:15]
    m_s, w_s, wq_s, kv_s, f_s, z_s, sems = refs[15:]
    width = dy2.shape[1]
    step = width // 2
    pieces = gather_rows(tab, plan, parts, m_s, sems, 0)
    weights = start_all([(wckv, w_s), (wcq, wq_s)], sems, 2 * n)
    mine = tab[plan.at["half"]]
    stack_heads(kvs, kv_s)
    da2 = dy2[...].astype(BF16)
    dqb = jnp.concatenate([v[...] for v in dqs], axis=1)
    wait_all(weights)
    dz1 = dy2[...] + dg(dqb, wq_s[...], 1, 1)
    dy1, dg1, db1 = norm_back(dz1, n1[...], r1[...], g1[...])
    dy_out[...] = dy1
    da1 = dy1.astype(BF16)
    z_s[...] = (n1[...] * g1[...] + b1[...]).astype(BF16)
    small = jnp.concatenate([dg1, db1, small_in[:6]], axis=0)
    wait_all(pieces)
    for dst, side in ((c_send, 1 - mine), (c_keep, mine)):
        at = pl.multiple_of(side * step, step)
        ckv = dg(m_s[:, pl.ds(at, step)], kv_s[...], 0, 1).astype(BF16)
        dst[:step] = ckv[:, :width]
        dst[step : 2 * step] = ckv[:, width:]
        dst[2 * step : 3 * step] = dg(z_s[:, pl.ds(at, step)], dqb, 0, 0).astype(BF16)
        dst[3 * step : 4 * step] = dg(c2[:, pl.ds(at, step)], da2, 0, 0).astype(BF16)
        dst[4 * step : 5 * step] = dg(c1[:, pl.ds(at, step)], da1, 0, 0).astype(BF16)
        dst[5 * step : 5 * step + 8] = jnp.where(side == 0, small, 0.0).astype(BF16)
        dst[5 * step + 8 :] = jnp.zeros((step - 8, width), BF16)
    f_s[...] = dg(kv_s[...], w_s[...], 0, 1)
    share_rows(plan, tab, f_s, m_send, m_keep)


def self_weights(plan, groups, tab, *refs):
    n = plan.rows
    parts, refs = refs[: 2 * n], refs[2 * n :]
    kvs, refs = refs[:groups], refs[groups:]
    dqs, refs = refs[:groups], refs[groups:]
    s_send, s_keep, x_s, kv_s, xo_s, sems = refs
    pieces = gather_rows(tab, plan, parts, x_s, sems, 0)
    lo = pl.multiple_of(tab[plan.at["lo"]] * QB, QB)
    hi = pl.multiple_of(tab[plan.at["hi"]] * QB, QB)
    width = x_s.shape[1]
    step = width // 2
    mine = tab[plan.at["half"]]
    stack_heads(kvs, kv_s)
    dqb = jnp.concatenate([v[...] for v in dqs], axis=1)
    wait_all(pieces)
    xo_s[:QB] = x_s[pl.ds(lo, QB)]
    xo_s[QB:] = x_s[pl.ds(hi, QB)]
    for dst, side in ((s_send, 1 - mine), (s_keep, mine)):
        at = pl.multiple_of(side * step, step)
        dst[:step] = dg(xo_s[:, pl.ds(at, step)], dqb, 0, 0).astype(BF16)
        kv = dg(x_s[:, pl.ds(at, step)], kv_s[...], 0, 1).astype(BF16)
        dst[step : 2 * step] = kv[:, :width]
        dst[2 * step :] = kv[:, width:]


def self_inputs(plan, groups, tab, *refs):
    kvs, refs = refs[:groups], refs[groups:]
    dqs, refs = refs[:groups], refs[groups:]
    w, dy1, x_send, x_keep, kv_s, f_s = refs
    lo = pl.multiple_of(tab[plan.at["lo"]] * QB, QB)
    hi = pl.multiple_of(tab[plan.at["hi"]] * QB, QB)
    width = dy1.shape[1]
    stack_heads(kvs, kv_s)
    dqb = jnp.concatenate([v[...] for v in dqs], axis=1)
    f_s[...] = dg(kv_s[...], w[:, width:], 0, 1)
    dx = dy1[...] + dg(dqb, w[:, :width], 1, 1)
    f_s[pl.ds(lo, QB)] += dx[:QB]
    f_s[pl.ds(hi, QB)] += dx[QB:]
    share_rows(plan, tab, f_s, x_send, x_keep)


def halves(refs):
    if len(refs) == 2:
        return refs
    half = refs[0].shape[0] // 2
    return refs[0].at[:half], refs[0].at[half:]


def halve_kernel(cols, came, tab, keep, *refs):
    got, (kept, *sends) = halves(refs[:came]), refs[came:]
    half = keep.shape[0] // 2
    size = half // 2
    for i in range(2):
        mine = tab[cols[i]]
        for dst, block in ((kept.at[i * size : (i + 1) * size], mine), (sends[i], 1 - mine)):
            at = pl.multiple_of(block * size, size)
            base = pl.multiple_of(i * half + block * size, size)
            dst[...] = (keep[pl.ds(base, size)].astype(F32) + got[i][pl.ds(at, size)].astype(F32)).astype(BF16)


def join_kernel(cols, tab, own, *refs):
    got, out = halves(refs[:-1]), refs[-1]
    size = own.shape[0] // 2
    for i in range(2):
        mine = tab[cols[i]]
        for src, block in ((own.at[i * size : (i + 1) * size], mine), (got[i], 1 - mine)):
            at = pl.multiple_of(2 * i * size + block * size, size)
            out[pl.ds(at, size)] = src[...]


def sum_kernel(count, *refs):
    parts, out = refs[:-1], refs[-1]
    if len(parts) == 1:
        blocks = parts[0].shape[0]
        total = parts[0][0].astype(F32)
        for i in range(1, blocks):
            total += parts[0][i].astype(F32)
        total = total.astype(BF16)
        if count:
            for i in range(count):
                out[i] = total
        else:
            out[...] = total
    else:
        half = out.shape[0] // 2
        for i, got in enumerate(halves(parts[1:])):
            rows = slice(i * half, (i + 1) * half)
            out[rows] = (parts[0][rows].astype(F32) + got[...].astype(F32)).astype(BF16)


def copy_kernel(src, out):
    for i in range(out.shape[0]):
        out[i] = src[...]


class Chunk:
    def __init__(self, plan, tab, send, keep):
        self.plan, self.tab = plan, tab
        self.rows, self.width = keep.shape
        pieces = 16 * 2 ** len(plan.steps)
        for _, n, _ in plan.stages:
            pieces *= n
        padded = -(-self.rows // pieces) * pieces
        if padded != self.rows:
            send, keep = (jnp.pad(v, ((0, padded - self.rows), (0, 0))) for v in (send, keep))
        self.kept, self.got = keep, [swap(send, plan, plan.core)]

    def small(self, kernel, ins, outs, deps):
        lead = [SM] if ins[0] is self.tab else []
        return call(
            kernel,
            ins,
            lead + [VM] * (len(ins) - len(lead)),
            [(shape, BF16) for shape in outs],
            [VM] * len(outs),
            [],
            2,
            24,
            deps=deps,
        )

    def cols(self, i):
        return [self.plan.at["step%d%s" % (i, side)] for side in "ab"]

    def move(self, arrays, i):
        return [swap(v, self.plan, bit) for v, bit in zip(arrays, self.plan.steps[i])]

    def halve(self, i, deps=()):
        rows = self.kept.shape[0]
        shapes = [(n, self.width) for n in (rows // 2, rows // 4, rows // 4)]
        kernel = functools.partial(halve_kernel, self.cols(i), len(self.got))
        self.kept, *sends = self.small(kernel, [self.tab, self.kept, *self.got], shapes, deps)
        self.got = self.move(sends, i)
        return self.kept

    def total(self, copies=0, deps=()):
        ins = [self.blocks] if self.got is None else [self.kept, *self.got]
        shape = ins[0].shape[-2:]
        if copies:
            shape = (copies,) + shape
        return self.small(functools.partial(sum_kernel, copies), ins, [shape], deps)[0]

    def scatter(self, i, deps=()):
        total = self.total(0, deps)
        n = self.plan.stages[i][1]
        self.blocks, self.got = trade(total.reshape(n, -1, self.width), self.plan.stages[i]), None
        return total

    def turn(self, deps=()):
        stage = self.plan.stages[-1]
        total = self.total(stage[1], deps)
        self.blocks = trade(total, stage)
        return total

    def gather(self, i, deps=()):
        stage = self.plan.stages[i]
        whole = self.blocks.reshape(-1, self.width)
        copies = self.small(copy_kernel, [whole], [(stage[1],) + whole.shape], deps)[0]
        self.blocks = trade(copies, stage)
        return copies

    def spread(self, i):
        self.own = self.blocks.reshape(-1, self.width) if self.blocks is not None else self.own
        self.blocks = None
        half = self.own.shape[0] // 2
        self.got = self.move([self.own[:half], self.own[half:]], i)

    def join(self, i, deps=()):
        kernel = functools.partial(join_kernel, self.cols(i))
        rows = self.own.shape[0]
        self.own = self.small(kernel, [self.tab, self.own, *self.got], [(2 * rows, self.width)], deps)[0]
        return self.own

    def finish(self, steps):
        for i in reversed(range(steps)):
            self.spread(i)
            self.join(i)
        return self.own, swap(self.own, self.plan, self.plan.core)


def feed_final(plan, tab, own, far, down, up):
    mine = tab[plan.at["half"]]
    width = own.shape[1]
    half = down.shape[0] // 2
    for src, side in ((own, mine), (far, 1 - mine)):
        down[pl.ds(pl.multiple_of(side * half, half), half)] = src[:half].astype(F32)
        for i in range(half // width):
            at = pl.multiple_of(side * half + i * width, width)
            rows = slice(half + i * width, half + (i + 1) * width)
            up[:, pl.ds(at, width)] = src[rows].astype(F32)


def cross_final(plan, tab, own, far, ckv, cq, co, so, small):
    mine = tab[plan.at["half"]]
    width = own.shape[1]
    step = width // 2
    for src, side in ((own, mine), (far, 1 - mine)):
        at = pl.ds(pl.multiple_of(side * step, step), step)
        ckv[at, :width] = src[:step].astype(F32)
        ckv[at, width:] = src[step : 2 * step].astype(F32)
        for i, dst in enumerate((cq, co, so)):
            dst[at] = src[(2 + i) * step : (3 + i) * step].astype(F32)
    tail = slice(5 * step, 5 * step + 8)
    small[...] = own[tail].astype(F32) + far[tail].astype(F32)


def self_final(plan, tab, own, far, qkv):
    mine = tab[plan.at["half"]]
    width = own.shape[1]
    step = width // 2
    for src, side in ((own, mine), (far, 1 - mine)):
        at = pl.ds(pl.multiple_of(side * step, step), step)
        for i in range(3):
            qkv[at, i * width : (i + 1) * width] = src[i * step : (i + 1) * step].astype(F32)


def finish(kernel, plan, tab, pair, outs):
    return call(
        functools.partial(kernel, plan),
        [tab, *pair],
        [SM, VM, VM],
        [(s, F32) for s in outs],
        [VM] * len(outs),
        [],
        5,
        32,
    )


def row_blocks(x, plan, scalar):
    return [
        lax.dynamic_index_in_dim(x, scalar("row%d" % t), 0, keepdims=False) for t in range(plan.rows)
    ]


def to_rows(blocks, plan):
    return [lax.ppermute(b, AXES, plan.perms[t]) for t, b in enumerate(blocks)]


def send_back(parts, plan):
    return [
        lax.ppermute(p, AXES, [(d, s) for s, d in plan.perms[t]]) for t, p in enumerate(parts)
    ]


def place_rows(parts, plan, scalar, dtype):
    out = jnp.zeros((plan.rows, plan.tok, parts[0].shape[-1]), dtype)
    for t, p in enumerate(parts):
        out = lax.dynamic_update_index_in_dim(out, p.astype(dtype), scalar("row%d" % t), 0)
    return out


def body(plan, tokens, memory, tgt_seg, mem_seg, cotangent, w_qkv, w_so, w_cq, w_ckv, w_co, w_up, w_down, *norms):
    n, tok, width = tokens.shape
    length = tgt_seg.shape[1]
    heads = width // HEAD_DIM
    ff = w_up.shape[1]
    own = length // 2
    g1, b1, g2, b2, g3, b3 = (v.reshape(1, width) for v in norms)
    known = plan.scalars()
    scalar = lambda name: known[name]
    tab = jnp.stack([known[name] for name in plan.at])

    segs = jnp.stack([tgt_seg, mem_seg])
    if plan.pair_in_dp:
        far = swap(segs, plan, plan.core)
        segs = jnp.where(scalar("seg_far") == 1, far, segs)
    segs = lax.dynamic_index_in_dim(segs, scalar("seg_row"), 1, keepdims=False)
    lane = jnp.arange(HEAD_DIM)[None, :]
    qf = (segs[0][:, None] == lane).astype(BF16)
    kf, mf = (jnp.where((s[:, None] != lane) & (lane < 3), OFF, 0.0).astype(BF16) for s in segs)

    def both(parts):
        return parts + [swap(p, plan, plan.core) for p in parts]

    x_own = to_rows(row_blocks(tokens, plan, scalar), plan)
    x_parts = both(x_own)
    blocks, x_own = lax.optimization_barrier((row_blocks(memory, plan, scalar), x_own))
    m_own = to_rows(blocks, plan)

    vec = lambda r, c, d=F32: ((r, c), d)
    wide = heads * AUG
    dma = pltpu.SemaphoreType.DMA
    vs = lambda r, c, d=BF16: pltpu.VMEM((r, c), d)
    slots = 2 * n + 16
    e1, k1, v1, q1, rl1, c1, n1, r1, cq = call(
        functools.partial(self_forward, plan, heads),
        [tab, *x_parts, w_qkv, w_so, w_cq, qf, kf, g1, b1],
        [SM] + [HB] * (2 * n + 3) + [VM] * 4,
        [
            ((heads, QB, 5 * QB), BF16),
            vec(length, wide, BF16),
            vec(length, wide, BF16),
            vec(own, width, BF16),
            vec(own, heads),
            vec(own, width, BF16),
            vec(own, width),
            vec(own, 1),
            vec(own, width, BF16),
        ],
        [HB] * 3 + [VM] * 6,
        [
            vs(length, width),
            vs(width, 3 * width),
            vs(width, width),
            vs(width, width),
            vs(length, wide),
            vs(length, wide),
            pltpu.VMEM((heads, QB, 5 * QB), BF16),
            dma((slots,)),
        ],
        14,
    )
    m_own, cq = lax.optimization_barrier((m_own, cq))
    m_parts = both(m_own)
    blocks, cq = lax.optimization_barrier((row_blocks(cotangent, plan, scalar), cq))
    g_parts = to_rows(blocks, plan)
    e2, k2, v2, rl2, c2, n2, r2 = call(
        functools.partial(cross_forward, plan, heads),
        [tab, *m_parts, w_ckv, w_co, cq, n1, qf, mf, g1, b1],
        [SM] + [HB] * (2 * n + 2) + [VM] * 6,
        [
            ((heads, own, length), BF16),
            vec(length, wide, BF16),
            vec(length, wide, BF16),
            vec(own, heads),
            vec(own, width, BF16),
            vec(own, width),
            vec(own, 1),
        ],
        [HB] * 3 + [VM] * 4,
        [
            vs(length, width),
            vs(width, 2 * width),
            vs(width, width),
            vs(length, wide),
            vs(length, wide),
            pltpu.VMEM((heads, own, length), BF16),
            dma((slots,)),
        ],
        15,
    )
    feed_out = call(
        functools.partial(feed, plan),
        [tab, *g_parts, w_up, w_down, n2, g2, b2, g3, b3],
        [SM] + [HB] * (n + 2) + [VM] * 5,
        [vec(tok, width, BF16)] * n
        + [vec(ff, width, BF16), vec(ff, width, BF16), vec(own, ff, BF16), vec(own, width), vec(8, width)],
        [HB] * (n + 3) + [VM] * 2,
        [
            vs(own, width),
            vs(width, ff),
            vs(ff, width),
            vs(own, ff),
            vs(own, ff),
            vs(own, width),
            vs(ff, width),
            vs(ff, width),
            dma((slots,)),
        ],
        12,
    )
    f_send, f_keep, du, dy3, small = feed_out[n:]
    f = Chunk(plan, tab, f_send, f_keep)
    dy2, small = call(
        feed_inputs, [du, w_up, dy3, n2, r2, g2, small], [VM] * 7, [vec(own, width), vec(8, width)], [VM] * 2, [], 4
    )
    steps, stages = len(plan.steps), len(plan.stages)
    kept = f.halve(0, [dy2])
    groups = 2
    some = heads // groups

    def backward_heads(i, kernel, lead, e, k, v, w, dy, c, rl, q, extra, us, deps):
        cols = some * HEAD_DIM
        return call(
            functools.partial(kernel, i * some, some),
            [*lead, e, k, v, w, dy, c, rl, q],
            [SM] * len(lead) + [HB] * 3 + [VM] * 5,
            [vec(2 * cols, length, BF16), vec(own, cols, BF16)],
            [VM] * 2,
            [
                pltpu.VMEM((some,) + e.shape[1:], BF16),
                vs(length, some * AUG),
                vs(length, some * AUG),
                vs(own, cols),
                vs(own, some, F32),
            ]
            + extra
            + [dma((slots,))],
            us,
            deps=deps,
        )

    cross_part = lambda i, deps: backward_heads(
        i, cross_heads, [], e2, k2, v2, w_co, dy2, c2, rl2, cq, [vs(own, length)], 9, deps
    )
    kv_a, dq_a = cross_part(0, [kept])
    for i in range(1, steps):
        kept = f.halve(i, [dq_a])
    kv_b, dq_b = cross_part(1, [kept, dq_a])
    kept = f.scatter(0, [dq_b])
    c_send, c_keep, m_send, m_keep, dy1 = call(
        functools.partial(cross_dense, plan, groups),
        [tab, *m_parts, kv_a, kv_b, dq_a, dq_b, w_ckv, w_cq, dy2, c2, n1, r1, g1, b1, c1, small],
        [SM] + [HB] * (2 * n) + [VM] * 4 + [HB] * 2 + [VM] * 8,
        [vec(3 * width, width, BF16)] * 2 + [vec(own, width, BF16)] * 2 + [vec(own, width)],
        [VM] * 5,
        [
            vs(length, width),
            vs(width, 2 * width),
            vs(width, width),
            vs(2 * width, length),
            vs(length, width, F32),
            vs(own, width),
            dma((slots,)),
        ],
        11,
        deps=[kept],
    )
    for i in range(1, stages):
        f.scatter(i)
    kept = f.turn([dy1])
    c = Chunk(plan, tab, c_send, c_keep)
    m_far = swap(m_send, plan, plan.core)
    self_part = lambda i, deps: backward_heads(
        i, functools.partial(self_heads, plan), [tab], e1, k1, v1, w_so, dy1, c1, rl1, q1, [], 7, deps
    )
    kv_c, dq_c = self_part(0, [kept])
    kept = c.halve(0, [dq_c])
    kv_d, dq_d = self_part(1, [kept, dq_c])
    for i in reversed(range(stages - 1)):
        f.gather(i)
    f.spread(steps - 1)
    if steps > 1:
        kept = f.join(steps - 1, [dq_d])
    s_send, s_keep = call(
        functools.partial(self_weights, plan, groups),
        [tab, *x_parts, kv_c, kv_d, dq_c, dq_d],
        [SM] + [HB] * (2 * n) + [VM] * 4,
        [vec(3 * width // 2, width, BF16)] * 2,
        [VM] * 2,
        [vs(length, width), vs(2 * width, length), vs(own, width), dma((slots,))],
        4,
        deps=[kept],
    )
    s = Chunk(plan, tab, s_send, s_keep)
    x_send, x_keep = call(
        functools.partial(self_inputs, plan, groups),
        [tab, kv_c, kv_d, dq_c, dq_d, w_qkv, dy1],
        [SM] + [VM] * 6,
        [vec(own, width, BF16)] * 2,
        [VM] * 2,
        [vs(2 * width, length), vs(length, width, F32)],
        4,
        deps=[s_keep],
    )
    s.halve(0, [x_keep])
    x_far = swap(x_send, plan, plan.core)
    f_pair = f.finish(steps - 1)
    for i in range(1, steps):
        c.halve(i)
        s.halve(i)
    for i in range(stages):
        c.scatter(i)
        s.scatter(i)
    for chunk in (c, s):
        chunk.turn()
        for i in reversed(range(stages - 1)):
            chunk.gather(i)
    c_pair, s_pair = c.finish(steps), s.finish(steps)
    out_back = send_back(lax.optimization_barrier((feed_out[:n], s_keep))[0], plan)
    output = place_rows(out_back, plan, scalar, BF16)

    def give_back(keep, far):
        total = (keep.astype(F32) + far.astype(F32)).astype(BF16)
        parts = [total[t * tok : (t + 1) * tok] for t in range(n)]
        return place_rows(send_back(parts, plan), plan, scalar, F32)

    grad_memory = give_back(m_keep, m_far)
    grad_tokens = give_back(x_keep, x_far)
    down, up = finish(feed_final, plan, tab, f_pair, [(ff, width), (width, ff)])
    square = (width, width)
    ckv, d_cq, d_co, d_so, tiny = finish(
        cross_final, plan, tab, c_pair, [(width, 2 * width), square, square, square, (8, width)]
    )
    (qkv,) = finish(self_final, plan, tab, s_pair, [(width, 3 * width)])
    return (output, grad_tokens, grad_memory, qkv, d_so, d_cq, ckv, d_co, up, down) + tuple(
        tiny[i] for i in range(6)
    )


def solution(mesh):
    def whole(*args):
        rows = args[0].shape[0] // mesh.shape["dp"]
        tok = args[0].shape[1] // mesh.shape["seq"]
        plan = Plan(mesh, rows, tok)
        split, copied = P("dp", "seq", None), P()
        return jax.shard_map(
            functools.partial(body, plan),
            mesh=mesh,
            in_specs=(split, split, P("dp", None), P("dp", None), split) + (copied,) * 13,
            out_specs=(split,) * 3 + (copied,) * 13,
            check_vma=False,
        )(*args)

    return whole
```

```python
import functools

import jax
import jax.numpy as jnp
import numpy as np
from jax import lax
from jax.experimental import pallas as pl
from jax.experimental.pallas import tpu as pltpu
from jax.sharding import PartitionSpec as P

F32 = jnp.float32
BF16 = jnp.bfloat16
HEAD_DIM = 64
AUG = 2 * HEAD_DIM
QB = 256
OFF = -1e9
AXES = ("dp", "seq")
COST = 3e8
VM = pl.BlockSpec(memory_space=pltpu.VMEM)
SM = pl.BlockSpec(memory_space=pltpu.SMEM)
HB = pl.BlockSpec(memory_space=pltpu.HBM)
ANY = pl.BlockSpec(memory_space=pl.ANY)


def dg(a, b, ca, cb):
    return lax.dot_general(a, b, (((ca,), (cb,)), ((), ())), preferred_element_type=F32)


class Plan:
    def __init__(self, mesh, rows, tok):
        dp, seq = mesh.shape["dp"], mesh.shape["seq"]
        self.dp, self.seq, self.rows, self.tok = dp, seq, rows, tok
        self.pair_in_dp = seq == 4
        assert rows * 2 == seq and seq in (4, 8)
        if self.pair_in_dp:
            dev = lambda k, c, h: (2 * k + h) * seq + c
            team_row = lambda h, j: 2 * h + j
            start = lambda c, h: c
            teams = dp // 2
            self.core = ("dp", 0)
            chips, line = self.bits("dp", 1, dp), self.bits("seq", 0, seq)
        else:
            dev = lambda k, c, h: k * seq + 2 * c + h
            team_row = lambda h, j: j
            start = lambda c, h: 2 * c + h
            teams = dp
            self.core = ("seq", 0)
            chips, line = self.bits("dp", 0, dp), self.bits("seq", 1, seq)
        count = dp * seq
        own = {0: (0, 3), 1: (1, 2)}
        half_of = {0: 0, 3: 0, 1: 1, 2: 1}
        todo = []
        for c in range(4):
            for h in range(2):
                for j in range(rows):
                    block = start(c, h) * tok // QB
                    todo.append(((c, h), (team_row(h, j), half_of[block]), j, start(c, h)))
        self.perms = []
        self.send_row = np.zeros((count, rows), np.int32)
        self.recv_at = np.zeros((count, rows), np.int32)
        nodes = [(c, h) for c in range(4) for h in range(2)]
        for turn in range(rows):
            match = {}

            def grow(src, seen):
                for e in todo:
                    if e[0] == src and e[1] not in seen:
                        seen.add(e[1])
                        if e[1] not in match or grow(match[e[1]][0], seen):
                            match[e[1]] = e
                            return True
                return False

            for src in nodes:
                assert grow(src, set())
            pairs = []
            for e in match.values():
                todo.remove(e)
                for k in range(teams):
                    s, d = dev(k, *e[0]), dev(k, *e[1])
                    pairs.append((s, d))
                    self.send_row[s, turn] = e[2]
                    self.recv_at[d, turn] = e[3]
            self.perms.append(sorted(pairs))
        place = np.zeros(count, np.int32)
        half, chip = np.zeros(count, np.int32), np.zeros(count, np.int32)
        sibling = np.zeros(count, np.int32)
        for k in range(teams):
            for c in range(4):
                for h in range(2):
                    d = dev(k, c, h)
                    half[d], chip[d], place[d] = h, c, 2 * c + h
                    sibling[d] = dev(k, c, 1 - h)
        self.codes = {}

        def add(name, values):
            by_place = [int(np.asarray(values)[place == p][0]) for p in range(8)]
            assert all(by_place[p] == v for p, v in zip(place, values))
            self.codes[name] = by_place

        add("half", half)
        add("lo", half)
        add("hi", 3 - half)
        if self.pair_in_dp:
            add("seg_far", (chip // 2 != half).astype(np.int32))
            add("seg_row", chip % 2)
        else:
            add("seg_far", np.zeros(count, np.int32))
            add("seg_row", chip)
        for t in range(rows):
            pos = self.recv_at[:, t] * tok
            add("own%d" % t, self.recv_at[:, t])
            add("sib%d" % t, self.recv_at[sibling, t])
            add("loc%d" % t, (np.where(pos // QB == half, 0, QB) + pos % QB) // tok)
            add("row%d" % t, self.send_row[:, t])
        far = len(chips) // 2
        self.steps = []
        for p, q in zip(chips[:far], chips[far:]):
            self.steps += [(p, q), (q, p)]
        near = [b for p, q in zip(chips[:far], chips[far:]) for b in (p, q)]
        self.near = self.groups("dp", sorted(near), dp)
        self.stages = self.groups("dp", chips[2 * far :], dp) + self.groups("seq", line, seq)
        self.bit_names = {}
        for i, step in enumerate(self.steps):
            for side, bit in zip("ab", step):
                self.bit_names["step%d%s" % (i, side)] = (bit[0], bit[1], 1)
        for i, (axis, shifts, _) in enumerate(self.near):
            self.bit_names["near%d" % i] = (axis, shifts[0], 2 ** len(shifts) - 1)
        for i, (axis, shifts, _) in enumerate(self.stages):
            self.bit_names["far%d" % i] = (axis, shifts[0], 2 ** len(shifts) - 1)
        self.at = {name: i for i, name in enumerate([*self.codes, *self.bit_names])}

    def padded(self, rows):
        unit = 16 * 2 ** len(self.steps)
        for _, bits, _ in self.stages:
            unit *= 2 ** len(bits)
        return -(-rows // unit) * unit

    def scalars(self):
        dp, seq = lax.axis_index("dp"), lax.axis_index("seq")
        place = 2 * seq + (dp & 1) if self.pair_in_dp else seq
        out = {}
        for name, by_place in self.codes.items():
            code = sum(v << (3 * p) for p, v in enumerate(by_place))
            out[name] = (jnp.int32(code) >> (3 * place)) & 7
        for name, (axis, shift, mask) in self.bit_names.items():
            out[name] = ((dp if axis == "dp" else seq) >> shift) & mask
        return out

    @staticmethod
    def bits(axis, shift, size):
        return [(axis, i) for i in range(shift, size.bit_length() - 1)]


    @staticmethod
    def groups(axis, bits, size):
        out = []
        bits = [shift for _, shift in bits]
        while bits:
            now, bits = bits[:2], bits[2:]
            mask = sum(1 << b for b in now)
            rest = [i for i in range(size) if not i & mask]
            steps = [0]
            for b in now:
                steps += [v + (1 << b) for v in steps]
            out.append((axis, now, [[i + v for v in steps] for i in rest]))
        return out


def meet(x, stage, r):
    axis, _, groups = stage
    pairs = [(g[k], g[k ^ r]) for g in groups for k in range(len(g))]
    return lax.ppermute(x, axis, pairs)


def swap(x, plan, bit):
    axis, shift = bit
    n = plan.dp if axis == "dp" else plan.seq
    return lax.ppermute(x, axis, [(i, i ^ (1 << shift)) for i in range(n)])


def norm_forward(y):
    centre = y - jnp.mean(y, axis=-1, keepdims=True)
    recip = lax.rsqrt(jnp.mean(centre * centre, axis=-1, keepdims=True) + 1e-05)
    return centre * recip, recip


def norm_back(grad, normed, recip, gain):
    d_gain = jnp.sum(grad * normed, axis=0, keepdims=True)
    d_bias = jnp.sum(grad, axis=0, keepdims=True)
    scaled = grad * gain
    d_in = recip * (
        scaled
        - jnp.mean(scaled, axis=-1, keepdims=True)
        - normed * jnp.mean(scaled * normed, axis=-1, keepdims=True)
    )
    return d_in, d_gain, d_bias


def augment(dst, x, tail):
    for h in range(x.shape[1] // HEAD_DIM):
        dst[:, h * AUG : (h + 1) * AUG] = jnp.concatenate(
            [x[:, h * HEAD_DIM : (h + 1) * HEAD_DIM], tail], axis=1
        )


def ones_tail(n):
    return (lax.broadcasted_iota(jnp.int32, (n, HEAD_DIM), 1) == 0).astype(BF16)


def head_forward(q, k, v, tri):
    s = dg(q, k, 1, 1)
    n = k.shape[0]
    if tri is not None:
        edge = s[:, n - QB :] + tri
        s = edge if n == QB else jnp.concatenate([s[:, : n - QB], edge], axis=1)
    e = jnp.exp(s - jnp.max(s, axis=1, keepdims=True)).astype(BF16)
    cv = dg(e, v, 1, 0)
    recip = 1.0 / cv[:, HEAD_DIM : HEAD_DIM + 1]
    return e, (cv[:, :HEAD_DIM] * recip).astype(BF16), recip


class Load:
    def __init__(self, src, dst, sem):
        self.dst, self.copy = dst, pltpu.make_async_copy(src, dst, sem)
        self.copy.start()
        self.here = False

    @property
    def r(self):
        if not self.here:
            self.copy.wait()
            self.here = True
        return self.dst


class Store:
    def __init__(self, src, dst, sem):
        self.r, self.copy, self.sent = src, pltpu.make_async_copy(src, dst, sem), False

    def send(self):
        self.copy.start()
        self.sent = True

    def done(self):
        if not self.sent:
            self.send()
        self.copy.wait()


def gather_rows(tab, plan, names, parts, dst, sems):
    out = []
    for i, (name, ref) in enumerate(zip(names, parts)):
        at = pl.multiple_of(tab[plan.at[name]] * plan.tok, plan.tok)
        out.append(Load(ref, dst.at[pl.ds(at, plan.tok)], sems.at[i]))
    return out


def row_names(plan):
    return ["own%d" % t for t in range(plan.rows)] + ["sib%d" % t for t in range(plan.rows)]


def arrive(loads):
    for v in loads:
        v.r


def big(kernel, tab, raw, ins, outs, scratch, us, raw_outs=(), deps=(), mib=44, free=(), raw_spec=HB):
    n_raw, n_in, n_dep, n_out, n_ro = len(raw), len(ins), len(deps), len(outs), len(raw_outs)

    def run(tab, *refs):
        raws, refs = refs[:n_raw], refs[n_raw:]
        srcs, refs = refs[:n_in], refs[n_in + n_dep :]
        dsts, refs = refs[:n_out], refs[n_out:]
        raw_dsts, refs = refs[:n_ro], refs[n_ro:]
        in_room, refs = refs[:n_in], refs[n_in:]
        out_room, refs = refs[:n_out], refs[n_out:]
        sems, refs = refs[0], refs[1:]
        loads = [Load(s, d, sems.at[i]) for i, (s, d) in enumerate(zip(srcs, in_room))]
        stores = [Store(s, d, sems.at[n_in + i]) for i, (s, d) in enumerate(zip(out_room, dsts))]
        kernel(tab, raws, loads, stores, raw_dsts, *refs)
        arrive(loads)
        for v in stores:
            v.done()

    room = [pltpu.VMEM(v.shape, v.dtype) for v in ins] + [pltpu.VMEM(s, d) for s, d in outs]
    return pl.pallas_call(
        run,
        out_shape=[jax.ShapeDtypeStruct(s, d) for s, d in [*outs, *raw_outs]],
        in_specs=[SM] + [raw_spec] * n_raw + [HB] * n_in + [ANY] * n_dep,
        out_specs=[ANY if i in free else HB for i in range(n_out)] + [HB] * n_ro,
        scratch_shapes=room + [pltpu.SemaphoreType.DMA((n_in + n_out,))] + scratch,
        compiler_params=pltpu.CompilerParams(vmem_limit_bytes=mib * 2**20),
        cost_estimate=pl.CostEstimate(flops=int(us * COST), bytes_accessed=2**20, transcendentals=0),
    )(tab, *raw, *ins, *deps)


def small(kernel, tab, ins, outs, deps=(), mib=16):
    n_in, n_dep = len(ins), len(deps)

    def run(tab, *refs):
        kernel(tab, refs[:n_in], refs[n_in + n_dep :])

    return pl.pallas_call(
        run,
        out_shape=[jax.ShapeDtypeStruct(s, d) for s, d in outs],
        in_specs=[SM] + [VM] * n_in + [ANY] * n_dep,
        out_specs=[VM] * len(outs),
        compiler_params=pltpu.CompilerParams(vmem_limit_bytes=mib * 2**20),
        cost_estimate=pl.CostEstimate(flops=int(2 * COST), bytes_accessed=2**20, transcendentals=0),
    )(tab, *ins, *deps)


def own_rows(plan, tab, ref):
    lo = pl.multiple_of(tab[plan.at["lo"]] * QB, QB)
    hi = pl.multiple_of(tab[plan.at["hi"]] * QB, QB)
    return jnp.concatenate([ref[pl.ds(lo, QB)], ref[pl.ds(hi, QB)]], axis=0)


def head_cols(h):
    return slice(h * HEAD_DIM, (h + 1) * HEAD_DIM)


def self_forward(plan, heads, tab, raw, ins, outs, raw_outs, x_s, e_s, sems, e_sems):
    wqkv, qf, kf, wso, g1, b1, wcq = ins
    q_out, k_out, v_out, rl_out, c_out, n_out, r_out, cq_out = outs
    pieces = gather_rows(tab, plan, row_names(plan), raw, x_s, sems)
    width = heads * HEAD_DIM
    w = wqkv.r
    arrive(pieces)
    k = dg(x_s[...], w[:, width : 2 * width], 1, 0).astype(BF16)
    augment(k_out.r, k, kf.r[...])
    k_out.send()
    v = dg(x_s[...], w[:, 2 * width :], 1, 0).astype(BF16)
    augment(v_out.r, v, ones_tail(v.shape[0]))
    v_out.send()
    x_own = own_rows(plan, tab, x_s)
    q_out.r[...] = (dg(x_own, w[:, :width], 1, 0).astype(BF16).astype(F32) * 0.125).astype(BF16)
    q_out.send()
    qf_own = own_rows(plan, tab, qf.r)
    tri = jnp.where(
        lax.broadcasted_iota(jnp.int32, (QB, QB), 1) <= lax.broadcasted_iota(jnp.int32, (QB, QB), 0),
        0.0,
        OFF,
    )

    def attend(core):
        sizes = (QB * (core + 1), QB * (4 - core))
        for h in range(heads):
            at = 0
            for i, keys in enumerate(sizes):
                rows = slice(i * QB, (i + 1) * QB)
                q = jnp.concatenate([q_out.r[rows, head_cols(h)], qf_own[rows]], axis=1)
                wide = slice(h * AUG, (h + 1) * AUG)
                e, c, recip = head_forward(q, k_out.r[:keys, wide], v_out.r[:keys, wide], tri)
                e_s[h, :, at : at + keys] = e
                c_out.r[rows, head_cols(h)] = c
                rl_out.r[rows, h : h + 1] = recip
                at += keys
            pltpu.make_async_copy(e_s.at[h], raw_outs[0].at[h], e_sems.at[h]).start()

    for core in range(2):
        pl.when(tab[plan.at["half"]] == core)(functools.partial(attend, core))
    rl_out.send()
    c_out.send()
    y = x_own.astype(F32) + dg(c_out.r[...], wso.r[...], 1, 0)
    normed, recip = norm_forward(y)
    n_out.r[...] = normed
    n_out.send()
    r_out.r[...] = recip
    r_out.send()
    z = (normed * g1.r[...] + b1.r[...]).astype(BF16)
    cq_out.r[...] = (dg(z, wcq.r[...], 1, 0).astype(BF16).astype(F32) * 0.125).astype(BF16)
    for h in range(heads):
        pltpu.make_async_copy(e_s.at[h], raw_outs[0].at[h], e_sems.at[h]).wait()


def cross_forward(plan, heads, tab, raw, ins, outs, raw_outs, m_s, e_s, sems, e_sems):
    wckv, qf, kf, cq, wco, n1, g1, b1 = ins
    k_out, v_out, rl_out, c_out, n_out, r_out = outs
    pieces = gather_rows(tab, plan, row_names(plan), raw, m_s, sems)
    width = heads * HEAD_DIM
    w = wckv.r
    arrive(pieces)
    k = dg(m_s[...], w[:, :width], 1, 0).astype(BF16)
    augment(k_out.r, k, kf.r[...])
    k_out.send()
    v = dg(m_s[...], w[:, width:], 1, 0).astype(BF16)
    augment(v_out.r, v, ones_tail(v.shape[0]))
    v_out.send()
    qf_own = own_rows(plan, tab, qf.r)
    copies = []
    for h in range(heads):
        for i in range(2):
            rows = slice(i * QB, (i + 1) * QB)
            q = jnp.concatenate([cq.r[rows, head_cols(h)], qf_own[rows]], axis=1)
            wide = slice(h * AUG, (h + 1) * AUG)
            e, c, recip = head_forward(q, k_out.r[:, wide], v_out.r[:, wide], None)
            e_s[h, rows] = e
            c_out.r[rows, head_cols(h)] = c
            rl_out.r[rows, h : h + 1] = recip
        copies.append(pltpu.make_async_copy(e_s.at[h], raw_outs[0].at[h], e_sems.at[h]))
        copies[-1].start()
    rl_out.send()
    c_out.send()
    y = n1.r[...] * g1.r[...] + b1.r[...] + dg(c_out.r[...], wco.r[...], 1, 0)
    normed, recip = norm_forward(y)
    n_out.r[...] = normed
    r_out.r[...] = recip
    for cp in copies:
        cp.wait()


def feed(plan, tab, raw, ins, outs, raw_outs, g_s, h_s, sems):
    n2, g2, b2, wup, wdown, g3, b3 = ins
    f_send, f_keep, du_out, dy_out, small_out, *o_out = outs
    n, tok = plan.rows, plan.tok
    grads = gather_rows(tab, plan, ["loc%d" % t for t in range(n)], raw, g_s, sems)
    z2 = n2.r[...] * g2.r[...] + b2.r[...]
    z2b = z2.astype(BF16)
    width = z2.shape[1]
    ff = wup.dst.shape[1]
    half = ff // 2
    fed = jnp.zeros(z2.shape, F32)
    d = du_out.r
    for i in range(0, ff, width):
        cols = slice(i, i + width)
        u = dg(z2b, wup.r[:, cols], 1, 0)
        sig = 1.0 / (1.0 + jnp.exp(-u))
        h_s[:, cols] = (u * sig).astype(BF16)
        d[:, cols] = (sig * (1.0 + u * (1.0 - sig))).astype(BF16)
        fed += dg(h_s[:, cols], wdown.r[cols, :], 1, 0)
    n3, r3 = norm_forward(z2 + fed)
    arrive(grads)
    dy3, dg3, db3 = norm_back(g_s[...].astype(F32), n3, r3, g3.r[...])
    g_s[...] = (n3 * g3.r[...] + b3.r[...]).astype(BF16)
    for t in range(n):
        at = pl.multiple_of(tab[plan.at["loc%d" % t]] * tok, tok)
        o_out[t].r[...] = g_s[pl.ds(at, tok)]
        o_out[t].send()
    dy_out.r[...] = dy3
    dy_out.send()
    small_out.r[...] = jnp.concatenate([dg3, db3, jnp.zeros((6, width), F32)], axis=0)
    dfb = dy3.astype(BF16)
    mine = tab[plan.at["half"]]
    sides = ((f_send, 1 - mine), (f_keep, mine))
    for dst, side in sides:
        at = pl.multiple_of(side * half, half)
        dst.r[:half] = dg(h_s[:, pl.ds(at, half)], dfb, 0, 0).astype(BF16)
    for i in range(0, ff, width):
        cols = slice(i, i + width)
        d[:, cols] = (dg(dfb, wdown.r[cols, :], 1, 1) * d[:, cols].astype(F32)).astype(BF16)
    du_out.send()
    for dst, side in sides:
        for i in range(half // width):
            at = pl.multiple_of(side * half + i * width, width)
            rows = slice(half + i * width, half + (i + 1) * width)
            dst.r[rows] = dg(z2b, d[:, pl.ds(at, width)], 0, 0).astype(BF16)
        dst.send()


def feed_inputs(tab, raw, ins, outs, raw_outs):
    du, wup, dy3, n2, r2, g2, small_in = ins
    dy_out, small_out = outs
    dz2 = dy3.r[...] + dg(du.r[...], wup.r[...], 1, 1)
    dy2, dg2, db2 = norm_back(dz2, n2.r[...], r2.r[...], g2.r[...])
    dy_out.r[...] = dy2
    small_out.r[...] = jnp.concatenate([dg2, db2, small_in.r[:6]], axis=0)


def context_grad(dy, w, c, rl, first, heads, dc_s, dd_s):
    group = slice(first * HEAD_DIM, (first + heads) * HEAD_DIM)
    dc = dg(dy[...].astype(BF16), w[group], 1, 1)
    cf = c[:, group].astype(F32)
    for h in range(heads):
        part = dc[:, head_cols(h)] * rl[:, first + h : first + h + 1]
        dc_s[:, head_cols(h)] = part.astype(BF16)
        dd_s[:, h : h + 1] = jnp.sum(part * cf[:, head_cols(h)], axis=1, keepdims=True)
    return group


def head_loads(first, heads, raw, e_s, k_s, v_s, sems):
    wide = pl.ds(first * AUG, heads * AUG)
    e_in, k_in, v_in = raw
    v = Load(v_in.at[:, wide], v_s, sems.at[0])
    e = [Load(e_in.at[first + h], e_s.at[h], sems.at[2 + h]) for h in range(heads)]
    return v, Load(k_in.at[:, wide], k_s, sems.at[1]), e


def cross_heads(first, heads, tab, raw, ins, outs, raw_outs, e_s, k_s, v_s, dc_s, dd_s, sems, ds_s):
    dy, wo, c, rl, q = ins
    kv_out, dq_out = outs
    v, k, e = head_loads(first, heads, raw, e_s, k_s, v_s, sems)
    group = context_grad(dy.r, wo.r, c.r, rl.r, first, heads, dc_s, dd_s)
    dct = dc_s[...].T
    qt = q.r[:, group].T
    half = heads * HEAD_DIM
    for h in range(heads):
        cols = head_cols(h)
        wide = slice(h * AUG, h * AUG + HEAD_DIM)
        for i in range(2):
            rows = slice(i * QB, (i + 1) * QB)
            dp = dg(dc_s[rows, cols], v.r[:, wide], 1, 1)
            e[h].r
            ds_s[rows] = (e_s[h, rows].astype(F32) * (dp - dd_s[rows, h : h + 1])).astype(BF16)
        kv_out.r[half + h * HEAD_DIM : half + (h + 1) * HEAD_DIM] = dg(dct[cols], e_s[h], 1, 0).astype(BF16)
        kv_out.r[cols] = dg(qt[cols], ds_s[...], 1, 0).astype(BF16)
        dq_out.r[:, cols] = (dg(ds_s[...], k.r[:, wide], 1, 0) * 0.125).astype(BF16)


def self_heads(plan, first, heads, tab, raw, ins, outs, raw_outs, e_s, k_s, v_s, dc_s, dd_s, sems):
    dy, wo, c, rl, q = ins
    kv_out, dq_out = outs
    v, k, e = head_loads(first, heads, raw, e_s, k_s, v_s, sems)
    group = context_grad(dy.r, wo.r, c.r, rl.r, first, heads, dc_s, dd_s)
    dct = dc_s[...].T
    qt = q.r[:, group].T
    half = heads * HEAD_DIM
    arrive([v, k] + e)

    def attend(core):
        n_lo, n_hi = QB * (core + 1), QB * (4 - core)
        total = k_s.shape[0]
        for h in range(heads):
            cols = head_cols(h)
            wide = slice(h * AUG, h * AUG + HEAD_DIM)
            sums = []
            at = 0
            for i, keys in enumerate((n_lo, n_hi)):
                rows = slice(i * QB, (i + 1) * QB)
                eh = e_s[h, :, at : at + keys]
                dp = dg(dc_s[rows, cols], v_s[:keys, wide], 1, 1)
                ds = (eh.astype(F32) * (dp - dd_s[rows, h : h + 1])).astype(BF16)
                dq_out.r[rows, cols] = (dg(ds, k_s[:keys, wide], 1, 0) * 0.125).astype(BF16)
                sums.append((dg(qt[cols, rows], ds, 1, 0), dg(dct[cols, rows], eh, 1, 0)))
                at += keys
            for j in range(2):
                low, high = sums[0][j], sums[1][j]
                at = j * half + h * HEAD_DIM
                rows = slice(at, at + HEAD_DIM)
                kv_out.r[rows, :n_lo] = (low + high[:, :n_lo]).astype(BF16)
                kv_out.r[rows, n_lo:n_hi] = high[:, n_lo:].astype(BF16)
                if n_hi < total:
                    kv_out.r[rows, n_hi:] = jnp.zeros((HEAD_DIM, total - n_hi), BF16)

    for core in range(2):
        pl.when(tab[plan.at["half"]] == core)(functools.partial(attend, core))


def stack_heads(parts, dst):
    at = 0
    for j in range(2):
        for p in parts:
            half = p.shape[0] // 2
            dst[at : at + half] = p[j * half : (j + 1) * half]
            at += half


def share_rows(plan, tab, src, send, base, keep):
    n, tok = plan.rows, plan.tok
    for t in range(n):
        for name, dst, at in (("sib%d", send, base), ("own%d", keep, 0)):
            row = pl.multiple_of(tab[plan.at[name % t]] * tok, tok)
            dst[at + t * tok : at + (t + 1) * tok] = src[pl.ds(row, tok)].astype(BF16)


def cross_dense(plan, groups, padded, tab, raw, ins, outs, raw_outs, m_s, kv_s, f_s, z_s, sems):
    dqs, ins = ins[:groups], ins[groups:]
    wcq, dy2, n1, r1, g1, b1, small_in = ins[:7]
    kvs, (c2, c1, wckv) = ins[7 : 7 + groups], ins[7 + groups :]
    dy_out, c_send, c_keep, m_keep = outs
    pieces = gather_rows(tab, plan, row_names(plan), raw, m_s, sems)
    mine = tab[plan.at["half"]]
    dqb = jnp.concatenate([v.r[...] for v in dqs], axis=1)
    dz1 = dy2.r[...] + dg(dqb, wcq.r[...], 1, 1)
    dy1, dg1, db1 = norm_back(dz1, n1.r[...], r1.r[...], g1.r[...])
    width = dy1.shape[1]
    step = width // 2
    dy_out.r[...] = dy1
    dy_out.send()
    da1 = dy1.astype(BF16)
    da2 = dy2.r[...].astype(BF16)
    z_s[...] = (n1.r[...] * g1.r[...] + b1.r[...]).astype(BF16)
    tiny = jnp.concatenate([dg1, db1, small_in.r[:6]], axis=0)
    stack_heads([v.r for v in kvs], kv_s)
    f_s[...] = dg(kv_s[...], wckv.r[...], 0, 1)
    share_rows(plan, tab, f_s, c_send.r, padded, m_keep.r)
    m_keep.send()
    arrive(pieces)
    for store, side in ((c_send, 1 - mine), (c_keep, mine)):
        dst = store.r
        at = pl.multiple_of(side * step, step)
        ckv = dg(m_s[:, pl.ds(at, step)], kv_s[...], 0, 1).astype(BF16)
        dst[:step] = ckv[:, :width]
        dst[step : 2 * step] = ckv[:, width:]
        dst[2 * step : 3 * step] = dg(z_s[:, pl.ds(at, step)], dqb, 0, 0).astype(BF16)
        dst[3 * step : 4 * step] = dg(c2.r[:, pl.ds(at, step)], da2, 0, 0).astype(BF16)
        dst[4 * step : 5 * step] = dg(c1.r[:, pl.ds(at, step)], da1, 0, 0).astype(BF16)
        dst[5 * step : 5 * step + 8] = jnp.where(side == 0, tiny, 0.0).astype(BF16)
        dst[5 * step + 8 : padded] = jnp.zeros((padded - 5 * step - 8, width), BF16)
        store.send()


def self_dense(plan, groups, padded, tab, raw, ins, outs, raw_outs, x_s, kv_s, xo_s, f_s, sems):
    kvs, dqs, (wqkv, dy1) = ins[:groups], ins[groups : 2 * groups], ins[2 * groups :]
    s_send, s_keep, x_keep = outs
    pieces = gather_rows(tab, plan, row_names(plan), raw, x_s, sems)
    lo = pl.multiple_of(tab[plan.at["lo"]] * QB, QB)
    hi = pl.multiple_of(tab[plan.at["hi"]] * QB, QB)
    width = x_s.shape[1]
    step = width // 2
    mine = tab[plan.at["half"]]
    stack_heads([v.r for v in kvs], kv_s)
    dqb = jnp.concatenate([v.r[...] for v in dqs], axis=1)
    arrive(pieces)
    xo_s[:QB] = x_s[pl.ds(lo, QB)]
    xo_s[QB:] = x_s[pl.ds(hi, QB)]
    for store, side in ((s_keep, mine), (s_send, 1 - mine)):
        dst = store.r
        at = pl.multiple_of(side * step, step)
        dst[:step] = dg(xo_s[:, pl.ds(at, step)], dqb, 0, 0).astype(BF16)
        kv = dg(x_s[:, pl.ds(at, step)], kv_s[...], 0, 1).astype(BF16)
        dst[step : 2 * step] = kv[:, :width]
        dst[2 * step : 3 * step] = kv[:, width:]
        if padded > 3 * step:
            dst[3 * step : padded] = jnp.zeros((padded - 3 * step, width), BF16)
    s_keep.send()
    w = wqkv.r
    f_s[...] = dg(kv_s[...], w[:, width:], 0, 1)
    dx = dy1.r[...] + dg(dqb, w[:, :width], 1, 1)
    f_s[pl.ds(lo, QB)] += dx[:QB]
    f_s[pl.ds(hi, QB)] += dx[QB:]
    share_rows(plan, tab, f_s, s_send.r, padded, x_keep.r)


def halve_kernel(cols, tab, ins, outs):
    keep, got = ins[0], ins[1:]
    kept, sends = outs[0], outs[1:]
    half = keep.shape[0] // 2
    size = half // 2
    for i in range(2):
        src, base = (got[0], i * half) if len(got) == 1 else (got[i], 0)
        mine = tab[cols[i]]
        for dst, block in ((kept.at[i * size : (i + 1) * size], mine), (sends[i], 1 - mine)):
            at = pl.multiple_of(i * half + block * size, size)
            there = pl.multiple_of(base + block * size, size)
            dst[...] = (keep[pl.ds(at, size)].astype(F32) + src[pl.ds(there, size)].astype(F32)).astype(BF16)


def split_kernel(col, tab, ins, outs):
    size, me = outs[0].shape[0], tab[col]
    for r, dst in enumerate(outs):
        at = pl.multiple_of((me ^ r) * size, size)
        total = ins[0][pl.ds(at, size)].astype(F32)
        for p in ins[1:]:
            total += p[pl.ds(at, size)].astype(F32)
        dst[...] = total.astype(BF16)


def block_kernel(kinds, names, tab, ins, outs):
    parts = []
    for kind, count in kinds:
        parts.append((kind, ins[:count], ins[0].shape[0]))
        ins = ins[count:]
    me = tab[names] if len(outs) > 1 else 0
    at = 0
    for kind, arrays, rows in parts:
        share = rows // len(outs)
        for r, dst in enumerate(outs):
            cuts = [(0, share, None)]
            if len(outs) > 1:
                start = pl.multiple_of((me ^ r) * share, share)
            else:
                start = 0
            if kind == "halves":
                half = rows // 2
                if len(outs) == 1:
                    cuts = [(0, half, arrays[1]), (half, half, arrays[2])]
                    for base, size, src in cuts:
                        total = arrays[0][base : base + size].astype(F32) + src[...].astype(F32)
                        dst[at + base : at + base + size] = total.astype(BF16)
                    continue
                inner = pl.multiple_of(lax.rem(start, half), share)
                in_b = start >= half
                for flag, src in ((False, arrays[1]), (True, arrays[2])):

                    @pl.when(in_b == flag)
                    def _(src=src, dst=dst, start=start, inner=inner, share=share, at=at):
                        total = arrays[0][pl.ds(start, share)].astype(F32) + src[pl.ds(inner, share)].astype(F32)
                        dst[at : at + share] = total.astype(BF16)

                continue
            total = arrays[0][pl.ds(start, share)].astype(F32)
            for p in arrays[1:]:
                total += p[pl.ds(start, share)].astype(F32)
            dst[at : at + share] = total.astype(BF16)
        at += rows // len(outs)


def unblock_kernel(rows, name, tab, ins, outs):
    me, out = tab[name], outs[0]
    at = to = 0
    for n in rows:
        for r, src in enumerate(ins):
            out[pl.ds(pl.multiple_of(to + (me ^ r) * n, n), n)] = src[at : at + n]
        at += n
        to += n * len(ins)


class Halving:
    def __init__(self, plan, tab, keep, got):
        self.plan, self.tab, self.kept, self.got = plan, tab, keep, [got]

    def halve(self, i, deps=()):
        rows, width = self.kept.shape
        shapes = [((n, width), BF16) for n in (rows // 2, rows // 4, rows // 4)]
        cols = [self.plan.at["step%d%s" % (i, side)] for side in "ab"]
        out = small(functools.partial(halve_kernel, cols), self.tab, [self.kept, *self.got], shapes, deps)
        self.kept = out[0]
        self.got = [swap(v, self.plan, bit) for v, bit in zip(out[1:], self.plan.steps[i])]
        return self.kept

    kind = ("halves", 3)


class Direct:
    def __init__(self, plan, tab, rows, keep, got):
        self.plan, self.tab, self.rows, self.kept, self.got = plan, tab, rows, keep, [got]

    def split(self, i, deps=()):
        stage = self.plan.near[i]
        n = 2 ** len(stage[1])
        self.rows //= n
        shapes = [((self.rows, self.kept.shape[1]), BF16)] * n
        kernel = functools.partial(split_kernel, self.plan.at["near%d" % i])
        out = small(kernel, self.tab, [self.kept, *self.got], shapes, deps)
        self.kept, self.got = out[0], [meet(out[r], stage, r) for r in range(1, n)]
        return self.kept

    @property
    def kind(self):
        return ("sum", 1 + len(self.got))


class Far:
    def __init__(self, plan, tab, chunks):
        self.plan, self.tab = plan, tab
        self.rows = [c.kept.shape[0] for c in chunks]
        self.width = chunks[0].kept.shape[1]
        self.kinds = [c.kind for c in chunks]
        self.parts = [v for c in chunks for v in (c.kept, *c.got)]

    def cut(self, n, name, deps):
        self.rows = [v // n for v in self.rows]
        kernel = functools.partial(block_kernel, self.kinds, name)
        self.kinds = [("sum", n)]
        return small(kernel, self.tab, self.parts, [((sum(self.rows), self.width), BF16)] * n, deps)

    def total(self, deps=()):
        return self.cut(1, 0, deps)[0]

    def scatter(self, i, deps=()):
        stage = self.plan.stages[i]
        n = 2 ** len(stage[1])
        out = self.cut(n, self.plan.at["far%d" % i], deps)
        self.parts = [out[0]] + [meet(out[r], stage, r) for r in range(1, n)]
        return out[0]

    def gather(self, i, own, deps=()):
        stage = self.plan.stages[i]
        n = 2 ** len(stage[1])
        ins = [own] + [meet(own, stage, r) for r in range(1, n)]
        kernel = functools.partial(unblock_kernel, self.rows, self.plan.at["far%d" % i])
        self.rows = [v * n for v in self.rows]
        return small(kernel, self.tab, ins, [((sum(self.rows), self.width), BF16)], deps)[0]

    def around(self, deps=()):
        stages = len(self.plan.stages)
        for i in range(stages):
            self.scatter(i, deps)
        own = self.total()
        for i in reversed(range(1, stages)):
            own = self.gather(i, own)
        return own


def near_parts(plan, own):
    out = [((), own)]
    for stage in plan.near:
        n = 2 ** len(stage[1])
        out = [(r + (k,), v if k == 0 else meet(v, stage, k)) for k in range(n) for r, v in out]
    return out


def both_cores(plan, parts):
    return [(r, side, v if side == 0 else swap(v, plan, plan.core)) for side in range(2) for r, v in parts]


def halving_at(plan, tab, diff, rows, i):
    size = rows // 2
    at = i * size
    for j in range(len(plan.steps)):
        size //= 2
        axis, shift = plan.steps[j][i]
        flip = 0
        for (_, shifts, _), d in zip(plan.near, diff):
            if shift in shifts:
                flip = (d >> shifts.index(shift)) & 1
        at = at + (tab[plan.at["step%d%s" % (j, "ab"[i])]] ^ flip) * size
    return at, size


def direct_at(plan, tab, diff, rows):
    at, size = 0, rows
    for j, ((_, shifts, _), d) in enumerate(zip(plan.near, diff)):
        size >>= len(shifts)
        at = at + (tab[plan.at["near%d" % j]] ^ d) * size
    return at, size


def feed_final(plan, diffs, tab, raw, ins, outs, raw_outs):
    down, up, mark = outs
    mark.r[...] = jnp.zeros(mark.r.shape, F32)
    mine = tab[plan.at["half"]]
    half = down.r.shape[0] // 2
    width = down.r.shape[1]
    for (diff, far), load in zip(diffs, ins):
        side = mine ^ far
        at, size = halving_at(plan, tab, diff, 2 * half, 0)
        src = load.r
        down.r[pl.ds(pl.multiple_of(side * half + at, size), size)] = src[:size].astype(F32)
        at, size = halving_at(plan, tab, diff, 2 * half, 1)
        at = at - half
        row = pl.multiple_of(lax.rem(at, width), size)
        col = pl.multiple_of(side * half + (at - row), width)
        up.r[pl.ds(row, size), pl.ds(col, width)] = src[size:].astype(F32)


def rest_final(plan, diffs, c_rows, s_rows, tab, raw, ins, outs, raw_outs, c_s, s_s):
    qkv, ckv, cq, co, so, tiny = outs
    width = qkv.r.shape[0]
    step = width // 2
    for (diff, far), load in zip(diffs, ins):
        src = load.r
        base = 0
        for i in range(2):
            at, size = halving_at(plan, tab, diff, c_rows, i)
            c_s[far, pl.ds(pl.multiple_of(at, size), size)] = src[base : base + size]
            base += size
        at, size = direct_at(plan, tab, diff, s_rows)
        s_s[far, pl.ds(pl.multiple_of(at, size), size)] = src[base : base + size]
    mine = tab[plan.at["half"]]
    places = [pl.ds(pl.multiple_of((mine ^ far) * step, step), step) for far in range(2)]
    for i in range(3):
        for far, at in enumerate(places):
            qkv.r[at, i * width : (i + 1) * width] = s_s[far, i * step : (i + 1) * step].astype(F32)
    qkv.send()
    for i in range(2):
        for far, at in enumerate(places):
            ckv.r[at, i * width : (i + 1) * width] = c_s[far, i * step : (i + 1) * step].astype(F32)
    ckv.send()
    for i, dst in enumerate((cq, co, so)):
        for far, at in enumerate(places):
            dst.r[at] = c_s[far, (2 + i) * step : (3 + i) * step].astype(F32)
        dst.send()
    tail = slice(5 * step, 5 * step + 8)
    tiny.r[...] = c_s[0, tail].astype(F32) + c_s[1, tail].astype(F32)


def row_blocks(x, plan, scalar):
    return [lax.dynamic_index_in_dim(x, scalar("row%d" % t), 0, keepdims=False) for t in range(plan.rows)]


def to_rows(blocks, plan):
    return [lax.ppermute(b, AXES, plan.perms[t]) for t, b in enumerate(blocks)]


def send_back(parts, plan):
    return [lax.ppermute(p, AXES, [(d, s) for s, d in plan.perms[t]]) for t, p in enumerate(parts)]


def give_kernel(plan, rows, tab, ins, outs):
    keep, got = ins
    tok = plan.tok
    for t, dst in enumerate(outs):
        came = got[rows + t * tok : rows + (t + 1) * tok].astype(F32)
        dst[...] = (keep[t * tok : (t + 1) * tok].astype(F32) + came).astype(BF16)


def take_kernel(plan, tab, raw, ins, outs, raw_outs):
    *arrays, mark = outs
    for i, dst in enumerate(arrays):
        for t in range(plan.rows):
            dst.r[tab[plan.at["row%d" % t]]] = ins[i * plan.rows + t].r[...].astype(dst.r.dtype)
    mark.r[...] = jnp.zeros(mark.r.shape, F32)


def body(plan, tokens, memory, tgt_seg, mem_seg, cotangent, w_qkv, w_so, w_cq, w_ckv, w_co, w_up, w_down, *norms):
    n, tok, width = tokens.shape
    length = tgt_seg.shape[1]
    heads = width // HEAD_DIM
    ff = w_up.shape[1]
    own = length // 2
    g1, b1, g2, b2, g3, b3 = (v.reshape(1, width) for v in norms)
    known = plan.scalars()
    scalar = lambda name: known[name]
    tab = jnp.stack([known[name] for name in plan.at])

    segs = jnp.stack([tgt_seg, mem_seg])
    if plan.pair_in_dp:
        far = swap(segs, plan, plan.core)
        segs = jnp.where(scalar("seg_far") == 1, far, segs)
    segs = lax.dynamic_index_in_dim(segs, scalar("seg_row"), 1, keepdims=False)
    lane = jnp.arange(HEAD_DIM)[None, :]
    qf = (segs[0][:, None] == lane).astype(BF16)
    kf, mf = (jnp.where((s[:, None] != lane) & (lane < 3), OFF, 0.0).astype(BF16) for s in segs)

    def both(parts):
        return parts + [swap(p, plan, plan.core) for p in parts]

    x_own = to_rows(row_blocks(tokens, plan, scalar), plan)
    x_parts = both(x_own)
    blocks, x_own = lax.optimization_barrier((row_blocks(memory, plan, scalar), x_own))
    m_own = to_rows(blocks, plan)
    blocks, x_parts = lax.optimization_barrier((row_blocks(cotangent, plan, scalar), x_parts))
    g_parts = to_rows(blocks, plan)

    arr = lambda r, c, d=F32: ((r, c), d)
    low = lambda r, c: ((r, c), BF16)
    vs = lambda r, c, d=BF16: pltpu.VMEM((r, c), d)
    sem = lambda k: pltpu.SemaphoreType.DMA((k,))
    wide = heads * AUG
    e_self, e_cross = (heads, QB, 5 * QB), (heads, own, length)

    q1, k1, v1, rl1, c1, n1, r1, cq, e1 = big(
        functools.partial(self_forward, plan, heads),
        tab,
        x_parts,
        [w_qkv, qf, kf, w_so, g1, b1, w_cq],
        [
            low(own, width),
            low(length, wide),
            low(length, wide),
            arr(own, heads),
            low(own, width),
            arr(own, width),
            arr(own, 1),
            low(own, width),
        ],
        [vs(length, width), pltpu.VMEM(e_self, BF16), sem(2 * n), sem(heads)],
        14,
        raw_outs=[(e_self, BF16)],
    )
    m_own, cq = lax.optimization_barrier((m_own, cq))
    m_parts = both(m_own)
    k2, v2, rl2, c2, n2, r2, e2 = big(
        functools.partial(cross_forward, plan, heads),
        tab,
        m_parts,
        [w_ckv, qf, mf, cq, w_co, n1, g1, b1],
        [low(length, wide), low(length, wide), arr(own, heads), low(own, width), arr(own, width), arr(own, 1)],
        [vs(length, width), pltpu.VMEM(e_cross, BF16), sem(2 * n), sem(heads)],
        15,
        raw_outs=[(e_cross, BF16)],
    )
    f_send, f_keep, du, dy3, tiny, *o_rows = big(
        functools.partial(feed, plan),
        tab,
        g_parts,
        [n2, g2, b2, w_up, w_down, g3, b3],
        [low(ff, width), low(ff, width), low(own, ff), arr(own, width), arr(8, width)]
        + [low(tok, width)] * n,
        [vs(own, width), vs(own, ff), sem(n)],
        12,
    )
    f = Halving(plan, tab, f_keep, swap(f_send, plan, plan.core))
    dy2, tiny = big(
        feed_inputs, tab, [], [du, w_up, dy3, n2, r2, g2, tiny], [arr(own, width), arr(8, width)], [], 4, mib=20
    )
    steps = len(plan.steps)
    kept = f.halve(0, [dy2])
    groups = 2
    some = heads // groups
    cols = some * HEAD_DIM

    def backward(i, kernel, raw, ins, extra, us, deps):
        return big(
            functools.partial(kernel, i * some, some),
            tab,
            raw,
            ins,
            [low(2 * cols, length), low(own, cols)],
            [
                pltpu.VMEM((some,) + raw[0].shape[1:], BF16),
                vs(length, some * AUG),
                vs(length, some * AUG),
                vs(own, cols),
                vs(own, some, F32),
                sem(2 + some),
            ]
            + extra,
            us,
            deps=deps,
            raw_spec=HB,
        )

    cross_part = lambda i, deps: backward(
        i, cross_heads, [e2, k2, v2], [dy2, w_co, c2, rl2, cq], [vs(own, length)], 9, deps
    )
    kv_a, dq_a = cross_part(0, [kept])
    for i in range(1, steps):
        kept = f.halve(i, [dq_a])
    out_back = send_back(o_rows, plan)
    kv_b, dq_b = cross_part(1, [kept, dq_a])
    f = Far(plan, tab, [f])
    kept = f.scatter(0, [dq_b])
    c_rows, s_rows = plan.padded(3 * width), plan.padded(3 * width // 2)
    dy1, c_send, c_keep, m_keep = big(
        functools.partial(cross_dense, plan, groups, c_rows),
        tab,
        m_parts,
        [dq_a, dq_b, w_cq, dy2, n1, r1, g1, b1, tiny, kv_a, kv_b, c2, c1, w_ckv],
        [arr(own, width), low(c_rows + own, width), low(c_rows, width), low(own, width)],
        [vs(length, width), vs(2 * width, length), vs(length, width, F32), vs(own, width), sem(2 * n)],
        11,
        deps=[kept, *out_back],
    )
    for i in range(1, len(plan.stages)):
        f.scatter(i, [dy1])
    f_own = f.total([dy1])
    for i in reversed(range(1, len(plan.stages))):
        f_own = f.gather(i, f_own)
    c_send, f_own = lax.optimization_barrier((c_send, f_own))
    c_got = swap(c_send, plan, plan.core)
    c = Halving(plan, tab, c_keep, c_got)
    self_part = lambda i, deps: backward(
        i, functools.partial(self_heads, plan), [e1, k1, v1], [dy1, w_so, c1, rl1, q1], [], 7, deps
    )
    kv_c, dq_c = self_part(0, [f_own])
    f_own = f.gather(0, f_own, [dq_c])
    f_near = near_parts(plan, f_own)
    turns = small(functools.partial(give_kernel, plan, c_rows), tab, [m_keep, c_got], [low(tok, width)] * n, [f_own])
    m_back = send_back(turns, plan)
    kv_d, dq_d = self_part(1, [dq_c, f_own])
    c.halve(0, [dq_d])
    s_send, s_keep, x_keep = big(
        functools.partial(self_dense, plan, groups, s_rows),
        tab,
        x_parts,
        [kv_c, kv_d, dq_c, dq_d, w_qkv, dy1],
        [low(s_rows + own, width), low(s_rows, width), low(own, width)],
        [vs(length, width), vs(2 * width, length), vs(own, width), vs(length, width, F32), sem(2 * n)],
        7,
        deps=[v for _, v in f_near] + [*m_back, c.kept],
    )
    s_got = swap(s_send, plan, plan.core)
    s = Direct(plan, tab, s_rows, s_keep, s_got)
    for i in range(len(plan.near)):
        s.split(i)
    f_all = both_cores(plan, f_near)
    for i in range(1, steps):
        c.halve(i, [s.kept] + [v for _, far, v in f_all if far])
    turns = small(functools.partial(give_kernel, plan, s_rows), tab, [x_keep, s_got], [low(tok, width)] * n, [s.kept])
    x_back = send_back(turns, plan)
    rest = Far(plan, tab, [c, s])
    rest_own = rest.around(x_back)

    def finish(kernel, arrays, outs, scratch, more=(), deps=()):
        diffs = [(diff, far) for diff, far, _ in arrays]
        return big(
            functools.partial(kernel, plan, diffs, *more), tab, [], [v for _, _, v in arrays], outs, scratch, 5, deps=deps
        )

    output, grad_memory, grad_tokens, mark = big(
        functools.partial(take_kernel, plan),
        tab,
        [],
        [*out_back, *m_back, *x_back],
        [((n, tok, width), BF16), ((n, tok, width), F32), ((n, tok, width), F32), arr(8, 128)],
        [],
        3,
    )
    down, up, late = finish(feed_final, f_all, [arr(ff, width), arr(width, ff), arr(8, 128)], [])
    rest_own = rest.gather(0, rest_own, [mark, late])
    all_rest = both_cores(plan, near_parts(plan, rest_own))
    qkv, ckv, d_cq, d_co, d_so, tiny = finish(
        rest_final,
        all_rest,
        [arr(width, 3 * width), arr(width, 2 * width)] + [arr(width, width)] * 3 + [arr(8, width)],
        [pltpu.VMEM((2, c_rows, width), BF16), pltpu.VMEM((2, s_rows, width), BF16)],
        (c_rows, s_rows),
    )
    return (output, grad_tokens, grad_memory, qkv, d_so, d_cq, ckv, d_co, up, down) + tuple(
        tiny[i] for i in range(6)
    )


def solution(mesh):
    def whole(*args):
        rows = args[0].shape[0] // mesh.shape["dp"]
        tok = args[0].shape[1] // mesh.shape["seq"]
        plan = Plan(mesh, rows, tok)
        split, copied = P("dp", "seq", None), P()
        return jax.shard_map(
            functools.partial(body, plan),
            mesh=mesh,
            in_specs=(split, split, P("dp", None), P("dp", None), split) + (copied,) * 13,
            out_specs=(split,) * 3 + (copied,) * 13,
            check_vma=False,
        )(*args)

    return whole
```

```python
import functools

import jax
import jax.numpy as jnp
import numpy as np
from jax import lax
from jax.experimental import pallas as pl
from jax.experimental.pallas import tpu as pltpu
from jax.sharding import PartitionSpec as P

F32 = jnp.float32
BF16 = jnp.bfloat16
HEAD_DIM = 64
AUG = 2 * HEAD_DIM
QB = 256
OFF = -1e9
AXES = ("dp", "seq")
COST = 3e8
VM = pl.BlockSpec(memory_space=pltpu.VMEM)
SM = pl.BlockSpec(memory_space=pltpu.SMEM)
HB = pl.BlockSpec(memory_space=pltpu.HBM)
ANY = pl.BlockSpec(memory_space=pl.ANY)


def dg(a, b, ca, cb):
    return lax.dot_general(a, b, (((ca,), (cb,)), ((), ())), preferred_element_type=F32)


class Plan:
    def __init__(self, mesh, rows, tok):
        dp, seq = mesh.shape["dp"], mesh.shape["seq"]
        self.dp, self.seq, self.rows, self.tok = dp, seq, rows, tok
        self.pair_in_dp = seq == 4
        assert rows * 2 == seq and seq in (4, 8)
        if self.pair_in_dp:
            dev = lambda k, c, h: (2 * k + h) * seq + c
            team_row = lambda h, j: 2 * h + j
            start = lambda c, h: c
            teams = dp // 2
            self.core = ("dp", 0)
            chips, line = self.bits("dp", 1, dp), self.bits("seq", 0, seq)
        else:
            dev = lambda k, c, h: k * seq + 2 * c + h
            team_row = lambda h, j: j
            start = lambda c, h: 2 * c + h
            teams = dp
            self.core = ("seq", 0)
            chips, line = self.bits("dp", 0, dp), self.bits("seq", 1, seq)
        count = dp * seq
        own = {0: (0, 3), 1: (1, 2)}
        half_of = {0: 0, 3: 0, 1: 1, 2: 1}
        todo = []
        for c in range(4):
            for h in range(2):
                for j in range(rows):
                    block = start(c, h) * tok // QB
                    todo.append(((c, h), (team_row(h, j), half_of[block]), j, start(c, h)))
        self.perms = []
        self.send_row = np.zeros((count, rows), np.int32)
        self.recv_at = np.zeros((count, rows), np.int32)
        nodes = [(c, h) for c in range(4) for h in range(2)]
        for turn in range(rows):
            match = {}

            def grow(src, seen):
                for e in todo:
                    if e[0] == src and e[1] not in seen:
                        seen.add(e[1])
                        if e[1] not in match or grow(match[e[1]][0], seen):
                            match[e[1]] = e
                            return True
                return False

            for src in nodes:
                assert grow(src, set())
            pairs = []
            for e in match.values():
                todo.remove(e)
                for k in range(teams):
                    s, d = dev(k, *e[0]), dev(k, *e[1])
                    pairs.append((s, d))
                    self.send_row[s, turn] = e[2]
                    self.recv_at[d, turn] = e[3]
            self.perms.append(sorted(pairs))
        place = np.zeros(count, np.int32)
        half, chip = np.zeros(count, np.int32), np.zeros(count, np.int32)
        sibling = np.zeros(count, np.int32)
        for k in range(teams):
            for c in range(4):
                for h in range(2):
                    d = dev(k, c, h)
                    half[d], chip[d], place[d] = h, c, 2 * c + h
                    sibling[d] = dev(k, c, 1 - h)
        self.codes = {}

        def add(name, values):
            by_place = [int(np.asarray(values)[place == p][0]) for p in range(8)]
            assert all(by_place[p] == v for p, v in zip(place, values))
            self.codes[name] = by_place

        add("half", half)
        add("lo", half)
        add("hi", 3 - half)
        if self.pair_in_dp:
            add("seg_far", (chip // 2 != half).astype(np.int32))
            add("seg_row", chip % 2)
        else:
            add("seg_far", np.zeros(count, np.int32))
            add("seg_row", chip)
        for t in range(rows):
            pos = self.recv_at[:, t] * tok
            add("own%d" % t, self.recv_at[:, t])
            add("sib%d" % t, self.recv_at[sibling, t])
            add("loc%d" % t, (np.where(pos // QB == half, 0, QB) + pos % QB) // tok)
            add("row%d" % t, self.send_row[:, t])
        far = len(chips) // 2
        self.steps = []
        for p, q in zip(chips[:far], chips[far:]):
            self.steps += [(p, q), (q, p)]
        near = [b for p, q in zip(chips[:far], chips[far:]) for b in (p, q)]
        self.near = self.groups("dp", sorted(near), dp)
        self.stages = self.groups("dp", chips[2 * far :], dp) + self.groups("seq", line, seq)
        self.bit_names = {}
        for i, step in enumerate(self.steps):
            for side, bit in zip("ab", step):
                self.bit_names["step%d%s" % (i, side)] = (bit[0], bit[1], 1)
        for i, (axis, shifts, _) in enumerate(self.near):
            self.bit_names["near%d" % i] = (axis, shifts[0], 2 ** len(shifts) - 1)
        for i, (axis, shifts, _) in enumerate(self.stages):
            self.bit_names["far%d" % i] = (axis, shifts[0], 2 ** len(shifts) - 1)
        self.at = {name: i for i, name in enumerate([*self.codes, *self.bit_names])}

    def padded(self, rows):
        unit = 16 * 2 ** len(self.steps)
        for _, bits, _ in self.stages:
            unit *= 2 ** len(bits)
        return -(-rows // unit) * unit

    def scalars(self):
        dp, seq = lax.axis_index("dp"), lax.axis_index("seq")
        place = 2 * seq + (dp & 1) if self.pair_in_dp else seq
        out = {}
        for name, by_place in self.codes.items():
            code = sum(v << (3 * p) for p, v in enumerate(by_place))
            out[name] = (jnp.int32(code) >> (3 * place)) & 7
        for name, (axis, shift, mask) in self.bit_names.items():
            out[name] = ((dp if axis == "dp" else seq) >> shift) & mask
        return out

    @staticmethod
    def bits(axis, shift, size):
        return [(axis, i) for i in range(shift, size.bit_length() - 1)]


    @staticmethod
    def groups(axis, bits, size):
        out = []
        bits = [shift for _, shift in bits]
        while bits:
            now, bits = bits[:2], bits[2:]
            mask = sum(1 << b for b in now)
            rest = [i for i in range(size) if not i & mask]
            steps = [0]
            for b in now:
                steps += [v + (1 << b) for v in steps]
            out.append((axis, now, [[i + v for v in steps] for i in rest]))
        return out


def meet(x, stage, r):
    axis, _, groups = stage
    pairs = [(g[k], g[k ^ r]) for g in groups for k in range(len(g))]
    return lax.ppermute(x, axis, pairs)


def swap(x, plan, bit):
    axis, shift = bit
    n = plan.dp if axis == "dp" else plan.seq
    return lax.ppermute(x, axis, [(i, i ^ (1 << shift)) for i in range(n)])


def norm_forward(y):
    centre = y - jnp.mean(y, axis=-1, keepdims=True)
    recip = lax.rsqrt(jnp.mean(centre * centre, axis=-1, keepdims=True) + 1e-05)
    return centre * recip, recip


def norm_back(grad, normed, recip, gain):
    d_gain = jnp.sum(grad * normed, axis=0, keepdims=True)
    d_bias = jnp.sum(grad, axis=0, keepdims=True)
    scaled = grad * gain
    d_in = recip * (
        scaled
        - jnp.mean(scaled, axis=-1, keepdims=True)
        - normed * jnp.mean(scaled * normed, axis=-1, keepdims=True)
    )
    return d_in, d_gain, d_bias


def augment(dst, x, tail):
    for h in range(x.shape[1] // HEAD_DIM):
        dst[:, h * AUG : (h + 1) * AUG] = jnp.concatenate(
            [x[:, h * HEAD_DIM : (h + 1) * HEAD_DIM], tail], axis=1
        )


def ones_tail(n):
    return (lax.broadcasted_iota(jnp.int32, (n, HEAD_DIM), 1) == 0).astype(BF16)


def head_forward(q, k, v, tri):
    s = dg(q, k, 1, 1)
    n = k.shape[0]
    if tri is not None:
        edge = s[:, n - QB :] + tri
        s = edge if n == QB else jnp.concatenate([s[:, : n - QB], edge], axis=1)
    e = jnp.exp(s - jnp.max(s, axis=1, keepdims=True)).astype(BF16)
    cv = dg(e, v, 1, 0)
    recip = 1.0 / cv[:, HEAD_DIM : HEAD_DIM + 1]
    return e, (cv[:, :HEAD_DIM] * recip).astype(BF16), recip


class Load:
    def __init__(self, src, dst, sem):
        self.dst, self.copy = dst, pltpu.make_async_copy(src, dst, sem)
        self.copy.start()
        self.here = False

    @property
    def r(self):
        if not self.here:
            self.copy.wait()
            self.here = True
        return self.dst


class Store:
    def __init__(self, src, dst, sem):
        self.r, self.copy, self.sent = src, pltpu.make_async_copy(src, dst, sem), False

    def send(self):
        self.copy.start()
        self.sent = True

    def done(self):
        if not self.sent:
            self.send()
        self.copy.wait()


def gather_rows(tab, plan, names, parts, dst, sems):
    out = []
    for i, (name, ref) in enumerate(zip(names, parts)):
        at = pl.multiple_of(tab[plan.at[name]] * plan.tok, plan.tok)
        out.append(Load(ref, dst.at[pl.ds(at, plan.tok)], sems.at[i]))
    return out


def row_names(plan):
    return ["own%d" % t for t in range(plan.rows)] + ["sib%d" % t for t in range(plan.rows)]


def arrive(loads):
    for v in loads:
        v.r


def big(kernel, tab, raw, ins, outs, scratch, us, raw_outs=(), deps=(), mib=44, free=(), raw_spec=HB):
    n_raw, n_in, n_dep, n_out, n_ro = len(raw), len(ins), len(deps), len(outs), len(raw_outs)

    def run(tab, *refs):
        raws, refs = refs[:n_raw], refs[n_raw:]
        srcs, refs = refs[:n_in], refs[n_in + n_dep :]
        dsts, refs = refs[:n_out], refs[n_out:]
        raw_dsts, refs = refs[:n_ro], refs[n_ro:]
        in_room, refs = refs[:n_in], refs[n_in:]
        out_room, refs = refs[:n_out], refs[n_out:]
        sems, refs = refs[0], refs[1:]
        loads = [Load(s, d, sems.at[i]) for i, (s, d) in enumerate(zip(srcs, in_room))]
        stores = [Store(s, d, sems.at[n_in + i]) for i, (s, d) in enumerate(zip(out_room, dsts))]
        kernel(tab, raws, loads, stores, raw_dsts, *refs)
        arrive(loads)
        for v in stores:
            v.done()

    room = [pltpu.VMEM(v.shape, v.dtype) for v in ins] + [pltpu.VMEM(s, d) for s, d in outs]
    return pl.pallas_call(
        run,
        out_shape=[jax.ShapeDtypeStruct(s, d) for s, d in [*outs, *raw_outs]],
        in_specs=[SM] + [raw_spec] * n_raw + [HB] * n_in + [ANY] * n_dep,
        out_specs=[ANY if i in free else HB for i in range(n_out)] + [HB] * n_ro,
        scratch_shapes=room + [pltpu.SemaphoreType.DMA((n_in + n_out,))] + scratch,
        compiler_params=pltpu.CompilerParams(vmem_limit_bytes=mib * 2**20),
        cost_estimate=pl.CostEstimate(flops=int(us * COST), bytes_accessed=2**20, transcendentals=0),
    )(tab, *raw, *ins, *deps)


def small(kernel, tab, ins, outs, deps=(), mib=16):
    n_in, n_dep = len(ins), len(deps)

    def run(tab, *refs):
        kernel(tab, refs[:n_in], refs[n_in + n_dep :])

    return pl.pallas_call(
        run,
        out_shape=[jax.ShapeDtypeStruct(s, d) for s, d in outs],
        in_specs=[SM] + [VM] * n_in + [ANY] * n_dep,
        out_specs=[VM] * len(outs),
        compiler_params=pltpu.CompilerParams(vmem_limit_bytes=mib * 2**20),
        cost_estimate=pl.CostEstimate(flops=int(2 * COST), bytes_accessed=2**20, transcendentals=0),
    )(tab, *ins, *deps)


def own_rows(plan, tab, ref):
    lo = pl.multiple_of(tab[plan.at["lo"]] * QB, QB)
    hi = pl.multiple_of(tab[plan.at["hi"]] * QB, QB)
    return jnp.concatenate([ref[pl.ds(lo, QB)], ref[pl.ds(hi, QB)]], axis=0)


def head_cols(h):
    return slice(h * HEAD_DIM, (h + 1) * HEAD_DIM)


def self_forward(plan, heads, tab, raw, ins, outs, raw_outs, x_s, e_s, sems, e_sems):
    wqkv, qf, kf, wso, g1, b1, wcq = ins
    q_out, k_out, v_out, rl_out, c_out, n_out, r_out, cq_out = outs
    pieces = gather_rows(tab, plan, row_names(plan), raw, x_s, sems)
    width = heads * HEAD_DIM
    w = wqkv.r
    arrive(pieces)
    k = dg(x_s[...], w[:, width : 2 * width], 1, 0).astype(BF16)
    augment(k_out.r, k, kf.r[...])
    k_out.send()
    v = dg(x_s[...], w[:, 2 * width :], 1, 0).astype(BF16)
    augment(v_out.r, v, ones_tail(v.shape[0]))
    v_out.send()
    x_own = own_rows(plan, tab, x_s)
    q_out.r[...] = (dg(x_own, w[:, :width], 1, 0).astype(BF16).astype(F32) * 0.125).astype(BF16)
    q_out.send()
    qf_own = own_rows(plan, tab, qf.r)
    tri = jnp.where(
        lax.broadcasted_iota(jnp.int32, (QB, QB), 1) <= lax.broadcasted_iota(jnp.int32, (QB, QB), 0),
        0.0,
        OFF,
    )

    def attend(core):
        sizes = (QB * (core + 1), QB * (4 - core))
        for h in range(heads):
            at = 0
            for i, keys in enumerate(sizes):
                rows = slice(i * QB, (i + 1) * QB)
                q = jnp.concatenate([q_out.r[rows, head_cols(h)], qf_own[rows]], axis=1)
                wide = slice(h * AUG, (h + 1) * AUG)
                e, c, recip = head_forward(q, k_out.r[:keys, wide], v_out.r[:keys, wide], tri)
                e_s[h, :, at : at + keys] = e
                c_out.r[rows, head_cols(h)] = c
                rl_out.r[rows, h : h + 1] = recip
                at += keys
            pltpu.make_async_copy(e_s.at[h], raw_outs[0].at[h], e_sems.at[h]).start()

    for core in range(2):
        pl.when(tab[plan.at["half"]] == core)(functools.partial(attend, core))
    rl_out.send()
    c_out.send()
    y = x_own.astype(F32) + dg(c_out.r[...], wso.r[...], 1, 0)
    normed, recip = norm_forward(y)
    n_out.r[...] = normed
    n_out.send()
    r_out.r[...] = recip
    r_out.send()
    z = (normed * g1.r[...] + b1.r[...]).astype(BF16)
    cq_out.r[...] = (dg(z, wcq.r[...], 1, 0).astype(BF16).astype(F32) * 0.125).astype(BF16)
    for h in range(heads):
        pltpu.make_async_copy(e_s.at[h], raw_outs[0].at[h], e_sems.at[h]).wait()


def cross_forward(plan, heads, tab, raw, ins, outs, raw_outs, m_s, e_s, sems, e_sems):
    wckv, qf, kf, cq, wco, n1, g1, b1 = ins
    k_out, v_out, rl_out, c_out, n_out, r_out = outs
    pieces = gather_rows(tab, plan, row_names(plan), raw, m_s, sems)
    width = heads * HEAD_DIM
    w = wckv.r
    arrive(pieces)
    k = dg(m_s[...], w[:, :width], 1, 0).astype(BF16)
    augment(k_out.r, k, kf.r[...])
    k_out.send()
    v = dg(m_s[...], w[:, width:], 1, 0).astype(BF16)
    augment(v_out.r, v, ones_tail(v.shape[0]))
    v_out.send()
    qf_own = own_rows(plan, tab, qf.r)
    copies = []
    for h in range(heads):
        for i in range(2):
            rows = slice(i * QB, (i + 1) * QB)
            q = jnp.concatenate([cq.r[rows, head_cols(h)], qf_own[rows]], axis=1)
            wide = slice(h * AUG, (h + 1) * AUG)
            e, c, recip = head_forward(q, k_out.r[:, wide], v_out.r[:, wide], None)
            e_s[h, rows] = e
            c_out.r[rows, head_cols(h)] = c
            rl_out.r[rows, h : h + 1] = recip
        copies.append(pltpu.make_async_copy(e_s.at[h], raw_outs[0].at[h], e_sems.at[h]))
        copies[-1].start()
    rl_out.send()
    c_out.send()
    y = n1.r[...] * g1.r[...] + b1.r[...] + dg(c_out.r[...], wco.r[...], 1, 0)
    normed, recip = norm_forward(y)
    n_out.r[...] = normed
    r_out.r[...] = recip
    for cp in copies:
        cp.wait()


def feed(plan, tab, raw, ins, outs, raw_outs, g_s, h_s, sems):
    n2, g2, b2, wup, wdown, g3, b3 = ins
    f_send, f_keep, du_out, dy_out, small_out, *o_out = outs
    n, tok = plan.rows, plan.tok
    grads = gather_rows(tab, plan, ["loc%d" % t for t in range(n)], raw, g_s, sems)
    z2 = n2.r[...] * g2.r[...] + b2.r[...]
    z2b = z2.astype(BF16)
    width = z2.shape[1]
    ff = wup.dst.shape[1]
    half = ff // 2
    fed = jnp.zeros(z2.shape, F32)
    d = du_out.r
    for i in range(0, ff, width):
        cols = slice(i, i + width)
        u = dg(z2b, wup.r[:, cols], 1, 0)
        sig = 1.0 / (1.0 + jnp.exp(-u))
        h_s[:, cols] = (u * sig).astype(BF16)
        d[:, cols] = (sig * (1.0 + u * (1.0 - sig))).astype(BF16)
        fed += dg(h_s[:, cols], wdown.r[cols, :], 1, 0)
    n3, r3 = norm_forward(z2 + fed)
    arrive(grads)
    dy3, dg3, db3 = norm_back(g_s[...].astype(F32), n3, r3, g3.r[...])
    g_s[...] = (n3 * g3.r[...] + b3.r[...]).astype(BF16)
    for t in range(n):
        at = pl.multiple_of(tab[plan.at["loc%d" % t]] * tok, tok)
        o_out[t].r[...] = g_s[pl.ds(at, tok)]
        o_out[t].send()
    dy_out.r[...] = dy3
    dy_out.send()
    small_out.r[...] = jnp.concatenate([dg3, db3, jnp.zeros((6, width), F32)], axis=0)
    dfb = dy3.astype(BF16)
    mine = tab[plan.at["half"]]
    sides = ((f_send, 1 - mine), (f_keep, mine))
    for dst, side in sides:
        at = pl.multiple_of(side * half, half)
        dst.r[:half] = dg(h_s[:, pl.ds(at, half)], dfb, 0, 0).astype(BF16)
    for i in range(0, ff, width):
        cols = slice(i, i + width)
        d[:, cols] = (dg(dfb, wdown.r[cols, :], 1, 1) * d[:, cols].astype(F32)).astype(BF16)
    du_out.send()
    for dst, side in sides:
        for i in range(half // width):
            at = pl.multiple_of(side * half + i * width, width)
            rows = slice(half + i * width, half + (i + 1) * width)
            dst.r[rows] = dg(z2b, d[:, pl.ds(at, width)], 0, 0).astype(BF16)
        dst.send()


def feed_inputs(tab, raw, ins, outs, raw_outs):
    du, wup, dy3, n2, r2, g2, small_in = ins
    dy_out, small_out = outs
    dz2 = dy3.r[...] + dg(du.r[...], wup.r[...], 1, 1)
    dy2, dg2, db2 = norm_back(dz2, n2.r[...], r2.r[...], g2.r[...])
    dy_out.r[...] = dy2
    small_out.r[...] = jnp.concatenate([dg2, db2, small_in.r[:6]], axis=0)


def context_grad(dy, w, c, rl, first, heads, dc_s, dd_s):
    group = slice(first * HEAD_DIM, (first + heads) * HEAD_DIM)
    dc = dg(dy[...].astype(BF16), w[group], 1, 1)
    cf = c[:, group].astype(F32)
    for h in range(heads):
        part = dc[:, head_cols(h)] * rl[:, first + h : first + h + 1]
        dc_s[:, head_cols(h)] = part.astype(BF16)
        dd_s[:, h : h + 1] = jnp.sum(part * cf[:, head_cols(h)], axis=1, keepdims=True)
    return group


def head_loads(first, heads, raw, e_s, k_s, v_s, sems):
    wide = pl.ds(first * AUG, heads * AUG)
    e_in, k_in, v_in = raw
    v = Load(v_in.at[:, wide], v_s, sems.at[0])
    e = [Load(e_in.at[first + h], e_s.at[h], sems.at[2 + h]) for h in range(heads)]
    return v, Load(k_in.at[:, wide], k_s, sems.at[1]), e


def cross_heads(first, heads, tab, raw, ins, outs, raw_outs, e_s, k_s, v_s, dc_s, dd_s, sems, ds_s):
    dy, wo, c, rl, q = ins
    kv_out, dq_out = outs
    v, k, e = head_loads(first, heads, raw, e_s, k_s, v_s, sems)
    group = context_grad(dy.r, wo.r, c.r, rl.r, first, heads, dc_s, dd_s)
    dct = dc_s[...].T
    qt = q.r[:, group].T
    half = heads * HEAD_DIM
    for h in range(heads):
        cols = head_cols(h)
        wide = slice(h * AUG, h * AUG + HEAD_DIM)
        for i in range(2):
            rows = slice(i * QB, (i + 1) * QB)
            dp = dg(dc_s[rows, cols], v.r[:, wide], 1, 1)
            e[h].r
            ds_s[rows] = (e_s[h, rows].astype(F32) * (dp - dd_s[rows, h : h + 1])).astype(BF16)
        kv_out.r[half + h * HEAD_DIM : half + (h + 1) * HEAD_DIM] = dg(dct[cols], e_s[h], 1, 0).astype(BF16)
        kv_out.r[cols] = dg(qt[cols], ds_s[...], 1, 0).astype(BF16)
        dq_out.r[:, cols] = (dg(ds_s[...], k.r[:, wide], 1, 0) * 0.125).astype(BF16)


def self_heads(plan, first, heads, tab, raw, ins, outs, raw_outs, e_s, k_s, v_s, dc_s, dd_s, sems):
    dy, wo, c, rl, q = ins
    kv_out, dq_out = outs
    v, k, e = head_loads(first, heads, raw, e_s, k_s, v_s, sems)
    group = context_grad(dy.r, wo.r, c.r, rl.r, first, heads, dc_s, dd_s)
    dct = dc_s[...].T
    qt = q.r[:, group].T
    half = heads * HEAD_DIM
    arrive([v, k] + e)

    def attend(core):
        n_lo, n_hi = QB * (core + 1), QB * (4 - core)
        total = k_s.shape[0]
        for h in range(heads):
            cols = head_cols(h)
            wide = slice(h * AUG, h * AUG + HEAD_DIM)
            sums = []
            at = 0
            for i, keys in enumerate((n_lo, n_hi)):
                rows = slice(i * QB, (i + 1) * QB)
                eh = e_s[h, :, at : at + keys]
                dp = dg(dc_s[rows, cols], v_s[:keys, wide], 1, 1)
                ds = (eh.astype(F32) * (dp - dd_s[rows, h : h + 1])).astype(BF16)
                dq_out.r[rows, cols] = (dg(ds, k_s[:keys, wide], 1, 0) * 0.125).astype(BF16)
                sums.append((dg(qt[cols, rows], ds, 1, 0), dg(dct[cols, rows], eh, 1, 0)))
                at += keys
            for j in range(2):
                low, high = sums[0][j], sums[1][j]
                at = j * half + h * HEAD_DIM
                rows = slice(at, at + HEAD_DIM)
                kv_out.r[rows, :n_lo] = (low + high[:, :n_lo]).astype(BF16)
                kv_out.r[rows, n_lo:n_hi] = high[:, n_lo:].astype(BF16)
                if n_hi < total:
                    kv_out.r[rows, n_hi:] = jnp.zeros((HEAD_DIM, total - n_hi), BF16)

    for core in range(2):
        pl.when(tab[plan.at["half"]] == core)(functools.partial(attend, core))


def stack_heads(parts, dst):
    at = 0
    for j in range(2):
        for p in parts:
            half = p.shape[0] // 2
            dst[at : at + half] = p[j * half : (j + 1) * half]
            at += half


def share_rows(plan, tab, src, send, base, keep):
    n, tok = plan.rows, plan.tok
    for t in range(n):
        for name, dst, at in (("sib%d", send, base), ("own%d", keep, 0)):
            row = pl.multiple_of(tab[plan.at[name % t]] * tok, tok)
            dst[at + t * tok : at + (t + 1) * tok] = src[pl.ds(row, tok)].astype(BF16)


def cross_dense(plan, groups, padded, tab, raw, ins, outs, raw_outs, m_s, kv_s, f_s, z_s, sems):
    dqs, ins = ins[:groups], ins[groups:]
    wcq, dy2, n1, r1, g1, b1, small_in = ins[:7]
    kvs, (c2, c1, wckv) = ins[7 : 7 + groups], ins[7 + groups :]
    dy_out, c_send, c_keep, m_keep = outs
    pieces = gather_rows(tab, plan, row_names(plan), raw, m_s, sems)
    mine = tab[plan.at["half"]]
    dqb = jnp.concatenate([v.r[...] for v in dqs], axis=1)
    dz1 = dy2.r[...] + dg(dqb, wcq.r[...], 1, 1)
    dy1, dg1, db1 = norm_back(dz1, n1.r[...], r1.r[...], g1.r[...])
    width = dy1.shape[1]
    step = width // 2
    dy_out.r[...] = dy1
    dy_out.send()
    da1 = dy1.astype(BF16)
    da2 = dy2.r[...].astype(BF16)
    z_s[...] = (n1.r[...] * g1.r[...] + b1.r[...]).astype(BF16)
    tiny = jnp.concatenate([dg1, db1, small_in.r[:6]], axis=0)
    stack_heads([v.r for v in kvs], kv_s)
    f_s[...] = dg(kv_s[...], wckv.r[...], 0, 1)
    share_rows(plan, tab, f_s, c_send.r, padded, m_keep.r)
    m_keep.send()
    arrive(pieces)
    for store, side in ((c_send, 1 - mine), (c_keep, mine)):
        dst = store.r
        at = pl.multiple_of(side * step, step)
        ckv = dg(m_s[:, pl.ds(at, step)], kv_s[...], 0, 1).astype(BF16)
        dst[:step] = ckv[:, :width]
        dst[step : 2 * step] = ckv[:, width:]
        dst[2 * step : 3 * step] = dg(z_s[:, pl.ds(at, step)], dqb, 0, 0).astype(BF16)
        dst[3 * step : 4 * step] = dg(c2.r[:, pl.ds(at, step)], da2, 0, 0).astype(BF16)
        dst[4 * step : 5 * step] = dg(c1.r[:, pl.ds(at, step)], da1, 0, 0).astype(BF16)
        dst[5 * step : 5 * step + 8] = jnp.where(side == 0, tiny, 0.0).astype(BF16)
        dst[5 * step + 8 : padded] = jnp.zeros((padded - 5 * step - 8, width), BF16)
        store.send()


def self_dense(plan, groups, padded, tab, raw, ins, outs, raw_outs, x_s, kv_s, xo_s, f_s, sems):
    kvs, dqs, (wqkv, dy1) = ins[:groups], ins[groups : 2 * groups], ins[2 * groups :]
    s_send, s_keep, x_keep = outs
    pieces = gather_rows(tab, plan, row_names(plan), raw, x_s, sems)
    lo = pl.multiple_of(tab[plan.at["lo"]] * QB, QB)
    hi = pl.multiple_of(tab[plan.at["hi"]] * QB, QB)
    width = x_s.shape[1]
    step = width // 2
    mine = tab[plan.at["half"]]
    stack_heads([v.r for v in kvs], kv_s)
    dqb = jnp.concatenate([v.r[...] for v in dqs], axis=1)
    arrive(pieces)
    xo_s[:QB] = x_s[pl.ds(lo, QB)]
    xo_s[QB:] = x_s[pl.ds(hi, QB)]
    for store, side in ((s_keep, mine), (s_send, 1 - mine)):
        dst = store.r
        at = pl.multiple_of(side * step, step)
        dst[:step] = dg(xo_s[:, pl.ds(at, step)], dqb, 0, 0).astype(BF16)
        kv = dg(x_s[:, pl.ds(at, step)], kv_s[...], 0, 1).astype(BF16)
        dst[step : 2 * step] = kv[:, :width]
        dst[2 * step : 3 * step] = kv[:, width:]
        if padded > 3 * step:
            dst[3 * step : padded] = jnp.zeros((padded - 3 * step, width), BF16)
    s_keep.send()
    w = wqkv.r
    f_s[...] = dg(kv_s[...], w[:, width:], 0, 1)
    dx = dy1.r[...] + dg(dqb, w[:, :width], 1, 1)
    f_s[pl.ds(lo, QB)] += dx[:QB]
    f_s[pl.ds(hi, QB)] += dx[QB:]
    share_rows(plan, tab, f_s, s_send.r, padded, x_keep.r)


def halve_kernel(cols, tab, ins, outs):
    keep, got = ins[0], ins[1:]
    kept, sends = outs[0], outs[1:]
    half = keep.shape[0] // 2
    size = half // 2
    for i in range(2):
        src, base = (got[0], i * half) if len(got) == 1 else (got[i], 0)
        mine = tab[cols[i]]
        for dst, block in ((kept.at[i * size : (i + 1) * size], mine), (sends[i], 1 - mine)):
            at = pl.multiple_of(i * half + block * size, size)
            there = pl.multiple_of(base + block * size, size)
            dst[...] = (keep[pl.ds(at, size)].astype(F32) + src[pl.ds(there, size)].astype(F32)).astype(BF16)


def split_kernel(col, tab, ins, outs):
    size, me = outs[0].shape[0], tab[col]
    for r, dst in enumerate(outs):
        at = pl.multiple_of((me ^ r) * size, size)
        total = ins[0][pl.ds(at, size)].astype(F32)
        for p in ins[1:]:
            total += p[pl.ds(at, size)].astype(F32)
        dst[...] = total.astype(BF16)


def block_kernel(kinds, names, tab, ins, outs):
    parts = []
    for kind, count in kinds:
        parts.append((kind, ins[:count], ins[0].shape[0]))
        ins = ins[count:]
    me = tab[names] if len(outs) > 1 else 0
    at = 0
    for kind, arrays, rows in parts:
        share = rows // len(outs)
        for r, dst in enumerate(outs):
            cuts = [(0, share, None)]
            if len(outs) > 1:
                start = pl.multiple_of((me ^ r) * share, share)
            else:
                start = 0
            if kind == "halves":
                half = rows // 2
                if len(outs) == 1:
                    cuts = [(0, half, arrays[1]), (half, half, arrays[2])]
                    for base, size, src in cuts:
                        total = arrays[0][base : base + size].astype(F32) + src[...].astype(F32)
                        dst[at + base : at + base + size] = total.astype(BF16)
                    continue
                inner = pl.multiple_of(lax.rem(start, half), share)
                in_b = start >= half
                for flag, src in ((False, arrays[1]), (True, arrays[2])):

                    @pl.when(in_b == flag)
                    def _(src=src, dst=dst, start=start, inner=inner, share=share, at=at):
                        total = arrays[0][pl.ds(start, share)].astype(F32) + src[pl.ds(inner, share)].astype(F32)
                        dst[at : at + share] = total.astype(BF16)

                continue
            total = arrays[0][pl.ds(start, share)].astype(F32)
            for p in arrays[1:]:
                total += p[pl.ds(start, share)].astype(F32)
            dst[at : at + share] = total.astype(BF16)
        at += rows // len(outs)


def unblock_kernel(rows, name, tab, ins, outs):
    me, out = tab[name], outs[0]
    at = to = 0
    for n in rows:
        for r, src in enumerate(ins):
            out[pl.ds(pl.multiple_of(to + (me ^ r) * n, n), n)] = src[at : at + n]
        at += n
        to += n * len(ins)


class Halving:
    def __init__(self, plan, tab, keep, got):
        self.plan, self.tab, self.kept, self.got = plan, tab, keep, [got]

    def halve(self, i, deps=()):
        rows, width = self.kept.shape
        shapes = [((n, width), BF16) for n in (rows // 2, rows // 4, rows // 4)]
        cols = [self.plan.at["step%d%s" % (i, side)] for side in "ab"]
        out = small(functools.partial(halve_kernel, cols), self.tab, [self.kept, *self.got], shapes, deps)
        self.kept = out[0]
        self.got = [swap(v, self.plan, bit) for v, bit in zip(out[1:], self.plan.steps[i])]
        return self.kept

    kind = ("halves", 3)


class Direct:
    def __init__(self, plan, tab, rows, keep, got):
        self.plan, self.tab, self.rows, self.kept, self.got = plan, tab, rows, keep, [got]

    def split(self, i, deps=()):
        stage = self.plan.near[i]
        n = 2 ** len(stage[1])
        self.rows //= n
        shapes = [((self.rows, self.kept.shape[1]), BF16)] * n
        kernel = functools.partial(split_kernel, self.plan.at["near%d" % i])
        out = small(kernel, self.tab, [self.kept, *self.got], shapes, deps)
        self.kept, self.got = out[0], [meet(out[r], stage, r) for r in range(1, n)]
        return self.kept

    @property
    def kind(self):
        return ("sum", 1 + len(self.got))


class Far:
    def __init__(self, plan, tab, chunks):
        self.plan, self.tab = plan, tab
        self.rows = [c.kept.shape[0] for c in chunks]
        self.width = chunks[0].kept.shape[1]
        self.kinds = [c.kind for c in chunks]
        self.parts = [v for c in chunks for v in (c.kept, *c.got)]

    def cut(self, n, name, deps):
        self.rows = [v // n for v in self.rows]
        kernel = functools.partial(block_kernel, self.kinds, name)
        self.kinds = [("sum", n)]
        return small(kernel, self.tab, self.parts, [((sum(self.rows), self.width), BF16)] * n, deps)

    def total(self, deps=()):
        return self.cut(1, 0, deps)[0]

    def scatter(self, i, deps=()):
        stage = self.plan.stages[i]
        n = 2 ** len(stage[1])
        out = self.cut(n, self.plan.at["far%d" % i], deps)
        self.parts = [out[0]] + [meet(out[r], stage, r) for r in range(1, n)]
        return out[0]

    def gather(self, i, own, deps=()):
        stage = self.plan.stages[i]
        n = 2 ** len(stage[1])
        ins = [own] + [meet(own, stage, r) for r in range(1, n)]
        kernel = functools.partial(unblock_kernel, self.rows, self.plan.at["far%d" % i])
        self.rows = [v * n for v in self.rows]
        return small(kernel, self.tab, ins, [((sum(self.rows), self.width), BF16)], deps)[0]


def halves_kernel(tab, ins, outs):
    half = ins[0].shape[0] // 2
    for i, dst in enumerate(outs):
        dst[...] = ins[0][i * half : (i + 1) * half]


def join_kernel(cols, tab, ins, outs):
    own, *got = ins
    size = own.shape[0] // 2
    for i in range(2):
        mine = tab[cols[i]]
        for src, block in ((own.at[i * size : (i + 1) * size], mine), (got[i], 1 - mine)):
            at = pl.multiple_of(block * size, size)
            value = src[...]
            outs[1 + i][pl.ds(at, size)] = value
            outs[0][pl.ds(pl.multiple_of(2 * i * size + at, size), size)] = value


class Doubling:
    def __init__(self, plan, tab, own, deps):
        self.plan, self.tab, self.own = plan, tab, own
        rows, self.width = own.shape
        self.apart = small(halves_kernel, tab, [own], [((rows // 2, self.width), BF16)] * 2, deps)
        self.move(len(plan.steps) - 1)

    def move(self, i):
        self.got = [swap(v, self.plan, bit) for v, bit in zip(self.apart, self.plan.steps[i])]

    def join(self, i, deps=()):
        cols = [self.plan.at["step%d%s" % (i, side)] for side in "ab"]
        rows = self.own.shape[0]
        shapes = [((n, self.width), BF16) for n in (2 * rows, rows, rows)]
        self.own, *self.apart = small(
            functools.partial(join_kernel, cols), self.tab, [self.own, *self.got], shapes, deps
        )
        self.move(i - 1)

    def both(self, after):
        mine, _ = lax.optimization_barrier(([self.own, *self.got], after))
        return mine + [swap(v, self.plan, self.plan.core) for v in mine]


def near_parts(plan, own):
    out = [((), own)]
    for stage in plan.near:
        n = 2 ** len(stage[1])
        out = [(r + (k,), v if k == 0 else meet(v, stage, k)) for k in range(n) for r, v in out]
    return out


def both_cores(plan, parts):
    return [(r, side, v if side == 0 else swap(v, plan, plan.core)) for side in range(2) for r, v in parts]


def halving_at(plan, tab, diff, rows, i):
    size = rows // 2
    at = i * size
    for j in range(len(plan.steps)):
        size //= 2
        axis, shift = plan.steps[j][i]
        flip = 0
        for (_, shifts, _), d in zip(plan.near, diff):
            if shift in shifts:
                flip = (d >> shifts.index(shift)) & 1
        at = at + (tab[plan.at["step%d%s" % (j, "ab"[i])]] ^ flip) * size
    return at, size


def direct_at(plan, tab, diff, rows):
    at, size = 0, rows
    for j, ((_, shifts, _), d) in enumerate(zip(plan.near, diff)):
        size >>= len(shifts)
        at = at + (tab[plan.at["near%d" % j]] ^ d) * size
    return at, size


def feed_final(plan, tab, raw, ins, outs, raw_outs):
    down, up, mark = outs
    mark.r[...] = jnp.zeros(mark.r.shape, F32)
    mine = tab[plan.at["half"]]
    bits = [tab[plan.at["step0" + side]] for side in "ab"]
    half = down.r.shape[0] // 2
    size = half // 2

    def put(far, flip, a, b):
        side = mine ^ far
        at = pl.multiple_of(side * half + (bits[0] ^ flip) * size, size)
        down.r[pl.ds(at, size)] = a.astype(F32)
        at = pl.multiple_of(side * half + (bits[1] ^ flip) * size, size)
        up.r[:, pl.ds(at, size)] = b.astype(F32)

    for far in range(2):
        own, a, b = ins[3 * far : 3 * far + 3]
        put(far, 0, own.r[:size], own.r[size:])
        put(far, 1, a.r[...], b.r[...])


def rest_final(plan, diffs, c_rows, s_rows, tab, raw, ins, outs, raw_outs, c_s, s_s):
    qkv, ckv, cq, co, so, tiny = outs
    width = qkv.r.shape[0]
    step = width // 2
    for (diff, far), load in zip(diffs, ins):
        src = load.r
        base = 0
        for i in range(2):
            at, size = halving_at(plan, tab, diff, c_rows, i)
            c_s[far, pl.ds(pl.multiple_of(at, size), size)] = src[base : base + size]
            base += size
        at, size = direct_at(plan, tab, diff, s_rows)
        s_s[far, pl.ds(pl.multiple_of(at, size), size)] = src[base : base + size]
    mine = tab[plan.at["half"]]
    places = [pl.ds(pl.multiple_of((mine ^ far) * step, step), step) for far in range(2)]
    for i in range(3):
        for far, at in enumerate(places):
            qkv.r[at, i * width : (i + 1) * width] = s_s[far, i * step : (i + 1) * step].astype(F32)
    qkv.send()
    for i in range(2):
        for far, at in enumerate(places):
            ckv.r[at, i * width : (i + 1) * width] = c_s[far, i * step : (i + 1) * step].astype(F32)
    ckv.send()
    for i, dst in enumerate((cq, co, so)):
        for far, at in enumerate(places):
            dst.r[at] = c_s[far, (2 + i) * step : (3 + i) * step].astype(F32)
        dst.send()
    tail = slice(5 * step, 5 * step + 8)
    tiny.r[...] = c_s[0, tail].astype(F32) + c_s[1, tail].astype(F32)


def row_blocks(x, plan, scalar):
    return [lax.dynamic_index_in_dim(x, scalar("row%d" % t), 0, keepdims=False) for t in range(plan.rows)]


def to_rows(blocks, plan):
    return [lax.ppermute(b, AXES, plan.perms[t]) for t, b in enumerate(blocks)]


def send_back(parts, plan):
    return [lax.ppermute(p, AXES, [(d, s) for s, d in plan.perms[t]]) for t, p in enumerate(parts)]


def give_kernel(plan, tab, raw, ins, outs, raw_outs):
    tok = plan.tok
    for t, dst in enumerate(outs):
        rows = slice(t * tok, (t + 1) * tok)
        for i in range(2):
            keep, got = ins[2 * i : 2 * i + 2]
            base = got.dst.shape[0] - plan.rows * tok
            came = got.r[base + t * tok : base + (t + 1) * tok].astype(F32)
            dst.r[i * tok : (i + 1) * tok] = (keep.r[rows].astype(F32) + came).astype(BF16)
        dst.send()


def take_kernel(plan, tab, raw, ins, outs, raw_outs):
    *arrays, mark = outs
    tok = plan.tok
    for t, load in enumerate(ins):
        row = tab[plan.at["row%d" % t]]
        for i, dst in enumerate(arrays):
            dst.r[row] = load.r[i * tok : (i + 1) * tok].astype(dst.r.dtype)
    mark.r[...] = jnp.zeros(mark.r.shape, F32)


def body(plan, tokens, memory, tgt_seg, mem_seg, cotangent, w_qkv, w_so, w_cq, w_ckv, w_co, w_up, w_down, *norms):
    n, tok, width = tokens.shape
    length = tgt_seg.shape[1]
    heads = width // HEAD_DIM
    ff = w_up.shape[1]
    own = length // 2
    g1, b1, g2, b2, g3, b3 = (v.reshape(1, width) for v in norms)
    known = plan.scalars()
    scalar = lambda name: known[name]
    tab = jnp.stack([known[name] for name in plan.at])

    segs = jnp.stack([tgt_seg, mem_seg])
    if plan.pair_in_dp:
        far = swap(segs, plan, plan.core)
        segs = jnp.where(scalar("seg_far") == 1, far, segs)
    segs = lax.dynamic_index_in_dim(segs, scalar("seg_row"), 1, keepdims=False)
    lane = jnp.arange(HEAD_DIM)[None, :]
    qf = (segs[0][:, None] == lane).astype(BF16)
    kf, mf = (jnp.where((s[:, None] != lane) & (lane < 3), OFF, 0.0).astype(BF16) for s in segs)

    def both(parts):
        return parts + [swap(p, plan, plan.core) for p in parts]

    x_own = to_rows(row_blocks(tokens, plan, scalar), plan)
    x_parts = both(x_own)
    blocks, x_own = lax.optimization_barrier((row_blocks(memory, plan, scalar), x_own))
    m_own = to_rows(blocks, plan)
    blocks, x_parts = lax.optimization_barrier((row_blocks(cotangent, plan, scalar), x_parts))
    g_parts = to_rows(blocks, plan)

    arr = lambda r, c, d=F32: ((r, c), d)
    low = lambda r, c: ((r, c), BF16)
    vs = lambda r, c, d=BF16: pltpu.VMEM((r, c), d)
    sem = lambda k: pltpu.SemaphoreType.DMA((k,))
    wide = heads * AUG
    e_self, e_cross = (heads, QB, 5 * QB), (heads, own, length)

    q1, k1, v1, rl1, c1, n1, r1, cq, e1 = big(
        functools.partial(self_forward, plan, heads),
        tab,
        x_parts,
        [w_qkv, qf, kf, w_so, g1, b1, w_cq],
        [
            low(own, width),
            low(length, wide),
            low(length, wide),
            arr(own, heads),
            low(own, width),
            arr(own, width),
            arr(own, 1),
            low(own, width),
        ],
        [vs(length, width), pltpu.VMEM(e_self, BF16), sem(2 * n), sem(heads)],
        14,
        raw_outs=[(e_self, BF16)],
    )
    m_own, cq = lax.optimization_barrier((m_own, cq))
    m_parts = both(m_own)
    k2, v2, rl2, c2, n2, r2, e2 = big(
        functools.partial(cross_forward, plan, heads),
        tab,
        m_parts,
        [w_ckv, qf, mf, cq, w_co, n1, g1, b1],
        [low(length, wide), low(length, wide), arr(own, heads), low(own, width), arr(own, width), arr(own, 1)],
        [vs(length, width), pltpu.VMEM(e_cross, BF16), sem(2 * n), sem(heads)],
        15,
        raw_outs=[(e_cross, BF16)],
    )
    f_send, f_keep, du, dy3, tiny, *o_rows = big(
        functools.partial(feed, plan),
        tab,
        g_parts,
        [n2, g2, b2, w_up, w_down, g3, b3],
        [low(ff, width), low(ff, width), low(own, ff), arr(own, width), arr(8, width)]
        + [low(tok, width)] * n,
        [vs(own, width), vs(own, ff), sem(n)],
        12,
    )
    f = Halving(plan, tab, f_keep, swap(f_send, plan, plan.core))
    dy2, tiny = big(
        feed_inputs, tab, [], [du, w_up, dy3, n2, r2, g2, tiny], [arr(own, width), arr(8, width)], [], 4, mib=20
    )
    steps = len(plan.steps)
    kept = f.halve(0, [dy2])
    groups = 2
    some = heads // groups

    def backward(first, some, kernel, raw, ins, extra, us, deps):
        cols = some * HEAD_DIM
        return big(
            functools.partial(kernel, first, some),
            tab,
            raw,
            ins,
            [low(2 * cols, length), low(own, cols)],
            [
                pltpu.VMEM((some,) + raw[0].shape[1:], BF16),
                vs(length, some * AUG),
                vs(length, some * AUG),
                vs(own, cols),
                vs(own, some, F32),
                sem(2 + some),
            ]
            + extra,
            us,
            deps=deps,
            raw_spec=HB,
        )

    cross_part = lambda i, deps: backward(
        i * some, some, cross_heads, [e2, k2, v2], [dy2, w_co, c2, rl2, cq], [vs(own, length)], 9, deps
    )
    kv_a, dq_a = cross_part(0, [kept])
    for i in range(1, steps):
        kept = f.halve(i, [dq_a])
    out_back = send_back(o_rows, plan)
    kv_b, dq_b = cross_part(1, [kept, dq_a])
    f = Far(plan, tab, [f])
    kept = f.scatter(0, [dq_b])
    c_rows, s_rows = plan.padded(3 * width), plan.padded(3 * width // 2)
    dy1, c_send, c_keep, m_keep = big(
        functools.partial(cross_dense, plan, groups, c_rows),
        tab,
        m_parts,
        [dq_a, dq_b, w_cq, dy2, n1, r1, g1, b1, tiny, kv_a, kv_b, c2, c1, w_ckv],
        [arr(own, width), low(c_rows + own, width), low(c_rows, width), low(own, width)],
        [vs(length, width), vs(2 * width, length), vs(length, width, F32), vs(own, width), sem(2 * n)],
        11,
        deps=[kept, *out_back],
    )
    for i in range(1, len(plan.stages)):
        f.scatter(i, [dy1])
    f_own = f.total([dy1])
    for i in reversed(range(1, len(plan.stages))):
        f_own = f.gather(i, f_own)
    c_send, f_own = lax.optimization_barrier((c_send, f_own))
    c_got = swap(c_send, plan, plan.core)
    c = Halving(plan, tab, c_keep, c_got)
    kept = c.halve(0)
    kv_c, dq_c = backward(
        0, heads, functools.partial(self_heads, plan), [e1, k1, v1], [dy1, w_so, c1, rl1, q1], [], 13, [f_own, kept]
    )
    f_own = f.gather(0, f_own, [dq_c])
    for i in range(1, steps):
        kept = c.halve(i, [dq_c])
    s_send, s_keep, x_keep = big(
        functools.partial(self_dense, plan, 1, s_rows),
        tab,
        x_parts,
        [kv_c, dq_c, w_qkv, dy1],
        [low(s_rows + own, width), low(s_rows, width), low(own, width)],
        [vs(length, width), vs(2 * width, length), vs(own, width), vs(length, width, F32), sem(2 * n)],
        7,
        deps=[f_own, kept],
    )
    s_got = swap(s_send, plan, plan.core)
    s = Direct(plan, tab, s_rows, s_keep, s_got)
    for i in range(len(plan.near)):
        s.split(i)
    rest = Far(plan, tab, [c, s])
    for i in range(len(plan.stages)):
        kept = rest.scatter(i)
    f = Doubling(plan, tab, f_own, [kept])
    rest_own = rest.total()
    for i in reversed(range(1, steps)):
        f.join(i, [rest_own])
    for i in reversed(range(1, len(plan.stages))):
        rest_own = rest.gather(i, rest_own)

    def finish(kernel, arrays, outs, scratch, more=(), deps=()):
        diffs = [(diff, far) for diff, far, _ in arrays]
        return big(
            functools.partial(kernel, plan, diffs, *more), tab, [], [v for _, _, v in arrays], outs, scratch, 5, deps=deps
        )

    def take(parts, kinds):
        outs = [((n, tok, width), d) for d in kinds] + [arr(8, 128)]
        return big(functools.partial(take_kernel, plan), tab, [], parts, outs, [], 2)

    output, mark = take(out_back, [BF16])
    rest_own = rest.gather(0, rest_own, [mark, *f.got])
    rest_near = near_parts(plan, rest_own)
    turns = big(
        functools.partial(give_kernel, plan),
        tab,
        [],
        [m_keep, c_got, x_keep, s_got],
        [low(2 * tok, width)] * n,
        [],
        2,
        deps=[rest_own],
    )
    back = send_back(turns, plan)
    down, up, late = big(
        functools.partial(feed_final, plan),
        tab,
        [],
        f.both(turns[0]),
        [arr(ff, width), arr(width, ff), arr(8, 128)],
        [],
        5,
    )
    arrays, late, back = lax.optimization_barrier(([v for _, v in rest_near], late, back))
    all_rest = both_cores(plan, [(d, v) for (d, _), v in zip(rest_near, arrays)])
    grad_memory, grad_tokens, mark = take(back, [F32, F32])
    qkv, ckv, d_cq, d_co, d_so, tiny = finish(
        rest_final,
        all_rest,
        [arr(width, 3 * width), arr(width, 2 * width)] + [arr(width, width)] * 3 + [arr(8, width)],
        [pltpu.VMEM((2, c_rows, width), BF16), pltpu.VMEM((2, s_rows, width), BF16)],
        (c_rows, s_rows),
        [late],
    )
    return (output, grad_tokens, grad_memory, qkv, d_so, d_cq, ckv, d_co, up, down) + tuple(
        tiny[i] for i in range(6)
    )


def solution(mesh):
    def whole(*args):
        rows = args[0].shape[0] // mesh.shape["dp"]
        tok = args[0].shape[1] // mesh.shape["seq"]
        plan = Plan(mesh, rows, tok)
        split, copied = P("dp", "seq", None), P()
        return jax.shard_map(
            functools.partial(body, plan),
            mesh=mesh,
            in_specs=(split, split, P("dp", None), P("dp", None), split) + (copied,) * 13,
            out_specs=(split,) * 3 + (copied,) * 13,
            check_vma=False,
        )(*args)

    return whole
```

```python
import functools

import jax
import jax.numpy as jnp
import numpy as np
from jax import lax
from jax.experimental import pallas as pl
from jax.experimental.pallas import tpu as pltpu
from jax.sharding import PartitionSpec as P

F32 = jnp.float32
BF16 = jnp.bfloat16
HEAD_DIM = 64
AUG = 2 * HEAD_DIM
QB = 256
OFF = -1e9
AXES = ("dp", "seq")
COST = 3e8
VM = pl.BlockSpec(memory_space=pltpu.VMEM)
SM = pl.BlockSpec(memory_space=pltpu.SMEM)
HB = pl.BlockSpec(memory_space=pltpu.HBM)
ANY = pl.BlockSpec(memory_space=pl.ANY)


def dg(a, b, ca, cb):
    return lax.dot_general(a, b, (((ca,), (cb,)), ((), ())), preferred_element_type=F32)


class Plan:
    def __init__(self, mesh, rows, tok):
        dp, seq = mesh.shape["dp"], mesh.shape["seq"]
        self.dp, self.seq, self.rows, self.tok = dp, seq, rows, tok
        self.pair_in_dp = seq == 4
        assert rows * 2 == seq and seq in (4, 8)
        if self.pair_in_dp:
            dev = lambda k, c, h: (2 * k + h) * seq + c
            team_row = lambda h, j: 2 * h + j
            start = lambda c, h: c
            teams = dp // 2
            self.core = ("dp", 0)
            chips, line = self.bits("dp", 1, dp), self.bits("seq", 0, seq)
        else:
            dev = lambda k, c, h: k * seq + 2 * c + h
            team_row = lambda h, j: j
            start = lambda c, h: 2 * c + h
            teams = dp
            self.core = ("seq", 0)
            chips, line = self.bits("dp", 0, dp), self.bits("seq", 1, seq)
        count = dp * seq
        own = {0: (0, 3), 1: (1, 2)}
        half_of = {0: 0, 3: 0, 1: 1, 2: 1}
        todo = []
        for c in range(4):
            for h in range(2):
                for j in range(rows):
                    block = start(c, h) * tok // QB
                    todo.append(((c, h), (team_row(h, j), half_of[block]), j, start(c, h)))
        self.perms = []
        self.send_row = np.zeros((count, rows), np.int32)
        self.recv_at = np.zeros((count, rows), np.int32)
        nodes = [(c, h) for c in range(4) for h in range(2)]
        for turn in range(rows):
            match = {}

            def grow(src, seen):
                for e in todo:
                    if e[0] == src and e[1] not in seen:
                        seen.add(e[1])
                        if e[1] not in match or grow(match[e[1]][0], seen):
                            match[e[1]] = e
                            return True
                return False

            for src in nodes:
                assert grow(src, set())
            pairs = []
            for e in match.values():
                todo.remove(e)
                for k in range(teams):
                    s, d = dev(k, *e[0]), dev(k, *e[1])
                    pairs.append((s, d))
                    self.send_row[s, turn] = e[2]
                    self.recv_at[d, turn] = e[3]
            self.perms.append(sorted(pairs))
        place = np.zeros(count, np.int32)
        half, chip = np.zeros(count, np.int32), np.zeros(count, np.int32)
        sibling = np.zeros(count, np.int32)
        for k in range(teams):
            for c in range(4):
                for h in range(2):
                    d = dev(k, c, h)
                    half[d], chip[d], place[d] = h, c, 2 * c + h
                    sibling[d] = dev(k, c, 1 - h)
        self.codes = {}

        def add(name, values):
            by_place = [int(np.asarray(values)[place == p][0]) for p in range(8)]
            assert all(by_place[p] == v for p, v in zip(place, values))
            self.codes[name] = by_place

        add("half", half)
        add("lo", half)
        add("hi", 3 - half)
        if self.pair_in_dp:
            add("seg_far", (chip // 2 != half).astype(np.int32))
            add("seg_row", chip % 2)
        else:
            add("seg_far", np.zeros(count, np.int32))
            add("seg_row", chip)
        for t in range(rows):
            pos = self.recv_at[:, t] * tok
            add("own%d" % t, self.recv_at[:, t])
            add("sib%d" % t, self.recv_at[sibling, t])
            add("loc%d" % t, (np.where(pos // QB == half, 0, QB) + pos % QB) // tok)
            add("row%d" % t, self.send_row[:, t])
        far = len(chips) // 2
        self.steps = []
        for p, q in zip(chips[:far], chips[far:]):
            self.steps += [(p, q), (q, p)]
        near = [b for p, q in zip(chips[:far], chips[far:]) for b in (p, q)]
        self.near = self.groups("dp", sorted(near), dp)
        self.stages = self.groups("dp", chips[2 * far :], dp) + self.groups("seq", line, seq)
        self.bit_names = {}
        for i, step in enumerate(self.steps):
            for side, bit in zip("ab", step):
                self.bit_names["step%d%s" % (i, side)] = (bit[0], bit[1], 1)
        for i, (axis, shifts, _) in enumerate(self.near):
            self.bit_names["near%d" % i] = (axis, shifts[0], 2 ** len(shifts) - 1)
        for i, (axis, shifts, _) in enumerate(self.stages):
            self.bit_names["far%d" % i] = (axis, shifts[0], 2 ** len(shifts) - 1)
        self.at = {name: i for i, name in enumerate([*self.codes, *self.bit_names])}

    def padded(self, rows):
        unit = 16 * 2 ** len(self.steps)
        for _, bits, _ in self.stages:
            unit *= 2 ** len(bits)
        return -(-rows // unit) * unit

    def scalars(self):
        dp, seq = lax.axis_index("dp"), lax.axis_index("seq")
        place = 2 * seq + (dp & 1) if self.pair_in_dp else seq
        out = {}
        for name, by_place in self.codes.items():
            code = sum(v << (3 * p) for p, v in enumerate(by_place))
            out[name] = (jnp.int32(code) >> (3 * place)) & 7
        for name, (axis, shift, mask) in self.bit_names.items():
            out[name] = ((dp if axis == "dp" else seq) >> shift) & mask
        return out

    @staticmethod
    def bits(axis, shift, size):
        return [(axis, i) for i in range(shift, size.bit_length() - 1)]


    @staticmethod
    def groups(axis, bits, size):
        out = []
        bits = [shift for _, shift in bits]
        while bits:
            now, bits = bits[:2], bits[2:]
            mask = sum(1 << b for b in now)
            rest = [i for i in range(size) if not i & mask]
            steps = [0]
            for b in now:
                steps += [v + (1 << b) for v in steps]
            out.append((axis, now, [[i + v for v in steps] for i in rest]))
        return out


def meet(x, stage, r):
    axis, _, groups = stage
    pairs = [(g[k], g[k ^ r]) for g in groups for k in range(len(g))]
    return lax.ppermute(x, axis, pairs)


def swap(x, plan, bit):
    axis, shift = bit
    n = plan.dp if axis == "dp" else plan.seq
    return lax.ppermute(x, axis, [(i, i ^ (1 << shift)) for i in range(n)])


def norm_forward(y):
    centre = y - jnp.mean(y, axis=-1, keepdims=True)
    recip = lax.rsqrt(jnp.mean(centre * centre, axis=-1, keepdims=True) + 1e-05)
    return centre * recip, recip


def norm_back(grad, normed, recip, gain):
    d_gain = jnp.sum(grad * normed, axis=0, keepdims=True)
    d_bias = jnp.sum(grad, axis=0, keepdims=True)
    scaled = grad * gain
    d_in = recip * (
        scaled
        - jnp.mean(scaled, axis=-1, keepdims=True)
        - normed * jnp.mean(scaled * normed, axis=-1, keepdims=True)
    )
    return d_in, d_gain, d_bias


def augment(dst, x, tail):
    for h in range(x.shape[1] // HEAD_DIM):
        dst[:, h * AUG : (h + 1) * AUG] = jnp.concatenate(
            [x[:, h * HEAD_DIM : (h + 1) * HEAD_DIM], tail], axis=1
        )


def ones_tail(n):
    return (lax.broadcasted_iota(jnp.int32, (n, HEAD_DIM), 1) == 0).astype(BF16)


def head_forward(q, k, v, tri):
    s = dg(q, k, 1, 1)
    n = k.shape[0]
    if tri is not None:
        edge = s[:, n - QB :] + tri
        s = edge if n == QB else jnp.concatenate([s[:, : n - QB], edge], axis=1)
    e = jnp.exp(s - jnp.max(s, axis=1, keepdims=True)).astype(BF16)
    cv = dg(e, v, 1, 0)
    recip = 1.0 / cv[:, HEAD_DIM : HEAD_DIM + 1]
    return e, (cv[:, :HEAD_DIM] * recip).astype(BF16), recip


class Load:
    def __init__(self, src, dst, sem):
        self.dst, self.copy = dst, pltpu.make_async_copy(src, dst, sem)
        self.copy.start()
        self.here = False

    @property
    def r(self):
        if not self.here:
            self.copy.wait()
            self.here = True
        return self.dst


class Store:
    def __init__(self, src, dst, sem):
        self.r, self.copy, self.sent = src, pltpu.make_async_copy(src, dst, sem), False

    def send(self):
        self.copy.start()
        self.sent = True

    def done(self):
        if not self.sent:
            self.send()
        self.copy.wait()


def gather_rows(tab, plan, names, parts, dst, sems):
    out = []
    for i, (name, ref) in enumerate(zip(names, parts)):
        at = pl.multiple_of(tab[plan.at[name]] * plan.tok, plan.tok)
        out.append(Load(ref, dst.at[pl.ds(at, plan.tok)], sems.at[i]))
    return out


def row_names(plan):
    return ["own%d" % t for t in range(plan.rows)] + ["sib%d" % t for t in range(plan.rows)]


def arrive(loads):
    for v in loads:
        v.r


def big(kernel, tab, raw, ins, outs, scratch, us, raw_outs=(), deps=(), mib=44, free=(), raw_spec=HB):
    n_raw, n_in, n_dep, n_out, n_ro = len(raw), len(ins), len(deps), len(outs), len(raw_outs)

    def run(tab, *refs):
        raws, refs = refs[:n_raw], refs[n_raw:]
        srcs, refs = refs[:n_in], refs[n_in + n_dep :]
        dsts, refs = refs[:n_out], refs[n_out:]
        raw_dsts, refs = refs[:n_ro], refs[n_ro:]
        in_room, refs = refs[:n_in], refs[n_in:]
        out_room, refs = refs[:n_out], refs[n_out:]
        sems, refs = refs[0], refs[1:]
        loads = [Load(s, d, sems.at[i]) for i, (s, d) in enumerate(zip(srcs, in_room))]
        stores = [Store(s, d, sems.at[n_in + i]) for i, (s, d) in enumerate(zip(out_room, dsts))]
        kernel(tab, raws, loads, stores, raw_dsts, *refs)
        arrive(loads)
        for v in stores:
            v.done()

    room = [pltpu.VMEM(v.shape, v.dtype) for v in ins] + [pltpu.VMEM(s, d) for s, d in outs]
    return pl.pallas_call(
        run,
        out_shape=[jax.ShapeDtypeStruct(s, d) for s, d in [*outs, *raw_outs]],
        in_specs=[SM] + [raw_spec] * n_raw + [HB] * n_in + [ANY] * n_dep,
        out_specs=[ANY if i in free else HB for i in range(n_out)] + [HB] * n_ro,
        scratch_shapes=room + [pltpu.SemaphoreType.DMA((n_in + n_out,))] + scratch,
        compiler_params=pltpu.CompilerParams(vmem_limit_bytes=mib * 2**20),
        cost_estimate=pl.CostEstimate(flops=int(us * COST), bytes_accessed=2**20, transcendentals=0),
    )(tab, *raw, *ins, *deps)


def small(kernel, tab, ins, outs, deps=(), mib=16):
    n_in, n_dep = len(ins), len(deps)

    def run(tab, *refs):
        kernel(tab, refs[:n_in], refs[n_in + n_dep :])

    return pl.pallas_call(
        run,
        out_shape=[jax.ShapeDtypeStruct(s, d) for s, d in outs],
        in_specs=[SM] + [VM] * n_in + [ANY] * n_dep,
        out_specs=[VM] * len(outs),
        compiler_params=pltpu.CompilerParams(vmem_limit_bytes=mib * 2**20),
        cost_estimate=pl.CostEstimate(flops=int(2 * COST), bytes_accessed=2**20, transcendentals=0),
    )(tab, *ins, *deps)


def own_rows(plan, tab, ref):
    lo = pl.multiple_of(tab[plan.at["lo"]] * QB, QB)
    hi = pl.multiple_of(tab[plan.at["hi"]] * QB, QB)
    return jnp.concatenate([ref[pl.ds(lo, QB)], ref[pl.ds(hi, QB)]], axis=0)


def head_cols(h):
    return slice(h * HEAD_DIM, (h + 1) * HEAD_DIM)


def self_forward(plan, heads, tab, raw, ins, outs, raw_outs, x_s, e_s, sems, e_sems):
    wqkv, qf, kf, wso, g1, b1, wcq = ins
    q_out, k_out, v_out, rl_out, c_out, n_out, r_out, cq_out = outs
    pieces = gather_rows(tab, plan, row_names(plan), raw, x_s, sems)
    width = heads * HEAD_DIM
    w = wqkv.r
    arrive(pieces)
    k = dg(x_s[...], w[:, width : 2 * width], 1, 0).astype(BF16)
    augment(k_out.r, k, kf.r[...])
    k_out.send()
    v = dg(x_s[...], w[:, 2 * width :], 1, 0).astype(BF16)
    augment(v_out.r, v, ones_tail(v.shape[0]))
    v_out.send()
    x_own = own_rows(plan, tab, x_s)
    q_out.r[...] = (dg(x_own, w[:, :width], 1, 0).astype(BF16).astype(F32) * 0.125).astype(BF16)
    q_out.send()
    qf_own = own_rows(plan, tab, qf.r)
    tri = jnp.where(
        lax.broadcasted_iota(jnp.int32, (QB, QB), 1) <= lax.broadcasted_iota(jnp.int32, (QB, QB), 0),
        0.0,
        OFF,
    )

    def attend(core):
        sizes = (QB * (core + 1), QB * (4 - core))
        for h in range(heads):
            at = 0
            for i, keys in enumerate(sizes):
                rows = slice(i * QB, (i + 1) * QB)
                q = jnp.concatenate([q_out.r[rows, head_cols(h)], qf_own[rows]], axis=1)
                wide = slice(h * AUG, (h + 1) * AUG)
                e, c, recip = head_forward(q, k_out.r[:keys, wide], v_out.r[:keys, wide], tri)
                e_s[h, :, at : at + keys] = e
                c_out.r[rows, head_cols(h)] = c
                rl_out.r[rows, h : h + 1] = recip
                at += keys
            pltpu.make_async_copy(e_s.at[h], raw_outs[0].at[h], e_sems.at[h]).start()

    for core in range(2):
        pl.when(tab[plan.at["half"]] == core)(functools.partial(attend, core))
    rl_out.send()
    c_out.send()
    y = x_own.astype(F32) + dg(c_out.r[...], wso.r[...], 1, 0)
    normed, recip = norm_forward(y)
    n_out.r[...] = normed
    n_out.send()
    r_out.r[...] = recip
    r_out.send()
    z = (normed * g1.r[...] + b1.r[...]).astype(BF16)
    cq_out.r[...] = (dg(z, wcq.r[...], 1, 0).astype(BF16).astype(F32) * 0.125).astype(BF16)
    for h in range(heads):
        pltpu.make_async_copy(e_s.at[h], raw_outs[0].at[h], e_sems.at[h]).wait()


def cross_forward(plan, heads, tab, raw, ins, outs, raw_outs, m_s, e_s, sems, e_sems):
    wckv, qf, kf, cq, wco, n1, g1, b1 = ins
    k_out, v_out, rl_out, c_out, n_out, r_out = outs
    pieces = gather_rows(tab, plan, row_names(plan), raw, m_s, sems)
    width = heads * HEAD_DIM
    w = wckv.r
    arrive(pieces)
    k = dg(m_s[...], w[:, :width], 1, 0).astype(BF16)
    augment(k_out.r, k, kf.r[...])
    k_out.send()
    v = dg(m_s[...], w[:, width:], 1, 0).astype(BF16)
    augment(v_out.r, v, ones_tail(v.shape[0]))
    v_out.send()
    qf_own = own_rows(plan, tab, qf.r)
    copies = []
    for h in range(heads):
        for i in range(2):
            rows = slice(i * QB, (i + 1) * QB)
            q = jnp.concatenate([cq.r[rows, head_cols(h)], qf_own[rows]], axis=1)
            wide = slice(h * AUG, (h + 1) * AUG)
            e, c, recip = head_forward(q, k_out.r[:, wide], v_out.r[:, wide], None)
            e_s[h, rows] = e
            c_out.r[rows, head_cols(h)] = c
            rl_out.r[rows, h : h + 1] = recip
        copies.append(pltpu.make_async_copy(e_s.at[h], raw_outs[0].at[h], e_sems.at[h]))
        copies[-1].start()
    rl_out.send()
    c_out.send()
    y = n1.r[...] * g1.r[...] + b1.r[...] + dg(c_out.r[...], wco.r[...], 1, 0)
    normed, recip = norm_forward(y)
    n_out.r[...] = normed
    r_out.r[...] = recip
    for cp in copies:
        cp.wait()


def feed(plan, tab, raw, ins, outs, raw_outs, g_s, h_s, sems):
    n2, g2, b2, wup, wdown, g3, b3 = ins
    f_send, f_keep, du_out, dy_out, small_out, *o_out = outs
    n, tok = plan.rows, plan.tok
    grads = gather_rows(tab, plan, ["loc%d" % t for t in range(n)], raw, g_s, sems)
    z2 = n2.r[...] * g2.r[...] + b2.r[...]
    z2b = z2.astype(BF16)
    width = z2.shape[1]
    ff = wup.dst.shape[1]
    half = ff // 2
    fed = jnp.zeros(z2.shape, F32)
    d = du_out.r
    for i in range(0, ff, width):
        cols = slice(i, i + width)
        u = dg(z2b, wup.r[:, cols], 1, 0)
        sig = 0.5 + 0.5 * jnp.tanh(0.5 * u)
        h_s[:, cols] = (u * sig).astype(BF16)
        d[:, cols] = (sig * (1.0 + u * (1.0 - sig))).astype(BF16)
        fed += dg(h_s[:, cols], wdown.r[cols, :], 1, 0)
    n3, r3 = norm_forward(z2 + fed)
    arrive(grads)
    dy3, dg3, db3 = norm_back(g_s[...].astype(F32), n3, r3, g3.r[...])
    g_s[...] = (n3 * g3.r[...] + b3.r[...]).astype(BF16)
    for t in range(n):
        at = pl.multiple_of(tab[plan.at["loc%d" % t]] * tok, tok)
        o_out[t].r[...] = g_s[pl.ds(at, tok)]
        o_out[t].send()
    dy_out.r[...] = dy3
    dy_out.send()
    small_out.r[...] = jnp.concatenate([dg3, db3, jnp.zeros((6, width), F32)], axis=0)
    dfb = dy3.astype(BF16)
    mine = tab[plan.at["half"]]
    sides = ((f_send, 1 - mine), (f_keep, mine))
    for dst, side in sides:
        at = pl.multiple_of(side * half, half)
        dst.r[:half] = dg(h_s[:, pl.ds(at, half)], dfb, 0, 0).astype(BF16)
    for i in range(0, ff, width):
        cols = slice(i, i + width)
        d[:, cols] = (dg(dfb, wdown.r[cols, :], 1, 1) * d[:, cols].astype(F32)).astype(BF16)
    du_out.send()
    for dst, side in sides:
        for i in range(half // width):
            at = pl.multiple_of(side * half + i * width, width)
            rows = slice(half + i * width, half + (i + 1) * width)
            dst.r[rows] = dg(z2b, d[:, pl.ds(at, width)], 0, 0).astype(BF16)
        dst.send()


def feed_inputs(tab, raw, ins, outs, raw_outs):
    du, wup, dy3, n2, r2, g2, small_in = ins
    dy_out, small_out = outs
    dz2 = dy3.r[...] + dg(du.r[...], wup.r[...], 1, 1)
    dy2, dg2, db2 = norm_back(dz2, n2.r[...], r2.r[...], g2.r[...])
    dy_out.r[...] = dy2
    small_out.r[...] = jnp.concatenate([dg2, db2, small_in.r[:6]], axis=0)


def context_grad(dy, w, c, rl, first, heads, dc_s, dd_s):
    group = slice(first * HEAD_DIM, (first + heads) * HEAD_DIM)
    dc = dg(dy[...].astype(BF16), w[group], 1, 1)
    cf = c[:, group].astype(F32)
    for h in range(heads):
        part = dc[:, head_cols(h)] * rl[:, first + h : first + h + 1]
        dc_s[:, head_cols(h)] = part.astype(BF16)
        dd_s[:, h : h + 1] = jnp.sum(part * cf[:, head_cols(h)], axis=1, keepdims=True)
    return group


def head_loads(first, heads, raw, e_s, k_s, v_s, sems):
    wide = pl.ds(first * AUG, heads * AUG)
    e_in, k_in, v_in = raw
    v = Load(v_in.at[:, wide], v_s, sems.at[0])
    e = [Load(e_in.at[first + h], e_s.at[h], sems.at[2 + h]) for h in range(heads)]
    return v, Load(k_in.at[:, wide], k_s, sems.at[1]), e


def cross_heads(first, heads, tab, raw, ins, outs, raw_outs, e_s, k_s, v_s, dc_s, dd_s, sems, ds_s):
    dy, wo, c, rl, q = ins
    kv_out, dq_out = outs
    v, k, e = head_loads(first, heads, raw, e_s, k_s, v_s, sems)
    group = context_grad(dy.r, wo.r, c.r, rl.r, first, heads, dc_s, dd_s)
    dct = dc_s[...].T
    qt = q.r[:, group].T
    half = heads * HEAD_DIM
    for h in range(heads):
        cols = head_cols(h)
        wide = slice(h * AUG, h * AUG + HEAD_DIM)
        for i in range(2):
            rows = slice(i * QB, (i + 1) * QB)
            dp = dg(dc_s[rows, cols], v.r[:, wide], 1, 1)
            e[h].r
            ds_s[rows] = (e_s[h, rows].astype(F32) * (dp - dd_s[rows, h : h + 1])).astype(BF16)
        kv_out.r[half + h * HEAD_DIM : half + (h + 1) * HEAD_DIM] = dg(dct[cols], e_s[h], 1, 0).astype(BF16)
        kv_out.r[cols] = dg(qt[cols], ds_s[...], 1, 0).astype(BF16)
        dq_out.r[:, cols] = (dg(ds_s[...], k.r[:, wide], 1, 0) * 0.125).astype(BF16)


def self_heads(plan, first, heads, tab, raw, ins, outs, raw_outs, e_s, k_s, v_s, dc_s, dd_s, sems):
    dy, wo, c, rl, q = ins
    kv_out, dq_out = outs
    v, k, e = head_loads(first, heads, raw, e_s, k_s, v_s, sems)
    group = context_grad(dy.r, wo.r, c.r, rl.r, first, heads, dc_s, dd_s)
    dct = dc_s[...].T
    qt = q.r[:, group].T
    half = heads * HEAD_DIM
    arrive([v, k] + e)

    def attend(core):
        n_lo, n_hi = QB * (core + 1), QB * (4 - core)
        total = k_s.shape[0]
        for h in range(heads):
            cols = head_cols(h)
            wide = slice(h * AUG, h * AUG + HEAD_DIM)
            sums = []
            at = 0
            for i, keys in enumerate((n_lo, n_hi)):
                rows = slice(i * QB, (i + 1) * QB)
                eh = e_s[h, :, at : at + keys]
                dp = dg(dc_s[rows, cols], v_s[:keys, wide], 1, 1)
                ds = (eh.astype(F32) * (dp - dd_s[rows, h : h + 1])).astype(BF16)
                dq_out.r[rows, cols] = (dg(ds, k_s[:keys, wide], 1, 0) * 0.125).astype(BF16)
                sums.append((dg(qt[cols, rows], ds, 1, 0), dg(dct[cols, rows], eh, 1, 0)))
                at += keys
            for j in range(2):
                low, high = sums[0][j], sums[1][j]
                at = j * half + h * HEAD_DIM
                rows = slice(at, at + HEAD_DIM)
                kv_out.r[rows, :n_lo] = (low + high[:, :n_lo]).astype(BF16)
                kv_out.r[rows, n_lo:n_hi] = high[:, n_lo:].astype(BF16)
                if n_hi < total:
                    kv_out.r[rows, n_hi:] = jnp.zeros((HEAD_DIM, total - n_hi), BF16)

    for core in range(2):
        pl.when(tab[plan.at["half"]] == core)(functools.partial(attend, core))


def stack_heads(parts, dst):
    at = 0
    for j in range(2):
        for p in parts:
            half = p.shape[0] // 2
            dst[at : at + half] = p[j * half : (j + 1) * half]
            at += half


def share_rows(plan, tab, src, send, base, keep):
    n, tok = plan.rows, plan.tok
    for t in range(n):
        for name, dst, at in (("sib%d", send, base), ("own%d", keep, 0)):
            row = pl.multiple_of(tab[plan.at[name % t]] * tok, tok)
            dst[at + t * tok : at + (t + 1) * tok] = src[pl.ds(row, tok)].astype(BF16)


def cross_dense(plan, groups, padded, tab, raw, ins, outs, raw_outs, m_s, kv_s, f_s, z_s, sems):
    dqs, ins = ins[:groups], ins[groups:]
    wcq, dy2, n1, r1, g1, b1, small_in = ins[:7]
    kvs, (c2, c1, wckv) = ins[7 : 7 + groups], ins[7 + groups :]
    dy_out, c_send, c_keep, m_keep = outs
    pieces = gather_rows(tab, plan, row_names(plan), raw, m_s, sems)
    mine = tab[plan.at["half"]]
    dqb = jnp.concatenate([v.r[...] for v in dqs], axis=1)
    dz1 = dy2.r[...] + dg(dqb, wcq.r[...], 1, 1)
    dy1, dg1, db1 = norm_back(dz1, n1.r[...], r1.r[...], g1.r[...])
    width = dy1.shape[1]
    step = width // 2
    dy_out.r[...] = dy1
    dy_out.send()
    da1 = dy1.astype(BF16)
    da2 = dy2.r[...].astype(BF16)
    z_s[...] = (n1.r[...] * g1.r[...] + b1.r[...]).astype(BF16)
    tiny = jnp.concatenate([dg1, db1, small_in.r[:6]], axis=0)
    stack_heads([v.r for v in kvs], kv_s)
    f_s[...] = dg(kv_s[...], wckv.r[...], 0, 1)
    share_rows(plan, tab, f_s, c_send.r, padded, m_keep.r)
    m_keep.send()
    arrive(pieces)
    for store, side in ((c_send, 1 - mine), (c_keep, mine)):
        dst = store.r
        at = pl.multiple_of(side * step, step)
        ckv = dg(m_s[:, pl.ds(at, step)], kv_s[...], 0, 1).astype(BF16)
        dst[:step] = ckv[:, :width]
        dst[step : 2 * step] = ckv[:, width:]
        dst[2 * step : 3 * step] = dg(z_s[:, pl.ds(at, step)], dqb, 0, 0).astype(BF16)
        dst[3 * step : 4 * step] = dg(c2.r[:, pl.ds(at, step)], da2, 0, 0).astype(BF16)
        dst[4 * step : 5 * step] = dg(c1.r[:, pl.ds(at, step)], da1, 0, 0).astype(BF16)
        dst[5 * step : 5 * step + 8] = jnp.where(side == 0, tiny, 0.0).astype(BF16)
        dst[5 * step + 8 : padded] = jnp.zeros((padded - 5 * step - 8, width), BF16)
        store.send()


def self_dense(plan, groups, padded, tab, raw, ins, outs, raw_outs, x_s, kv_s, xo_s, f_s, sems):
    kvs, dqs, (wqkv, dy1) = ins[:groups], ins[groups : 2 * groups], ins[2 * groups :]
    s_send, s_keep, x_keep = outs
    pieces = gather_rows(tab, plan, row_names(plan), raw, x_s, sems)
    lo = pl.multiple_of(tab[plan.at["lo"]] * QB, QB)
    hi = pl.multiple_of(tab[plan.at["hi"]] * QB, QB)
    width = x_s.shape[1]
    step = width // 2
    mine = tab[plan.at["half"]]
    stack_heads([v.r for v in kvs], kv_s)
    dqb = jnp.concatenate([v.r[...] for v in dqs], axis=1)
    arrive(pieces)
    xo_s[:QB] = x_s[pl.ds(lo, QB)]
    xo_s[QB:] = x_s[pl.ds(hi, QB)]
    for store, side in ((s_keep, mine), (s_send, 1 - mine)):
        dst = store.r
        at = pl.multiple_of(side * step, step)
        dst[:step] = dg(xo_s[:, pl.ds(at, step)], dqb, 0, 0).astype(BF16)
        kv = dg(x_s[:, pl.ds(at, step)], kv_s[...], 0, 1).astype(BF16)
        dst[step : 2 * step] = kv[:, :width]
        dst[2 * step : 3 * step] = kv[:, width:]
        if padded > 3 * step:
            dst[3 * step : padded] = jnp.zeros((padded - 3 * step, width), BF16)
    s_keep.send()
    w = wqkv.r
    f_s[...] = dg(kv_s[...], w[:, width:], 0, 1)
    dx = dy1.r[...] + dg(dqb, w[:, :width], 1, 1)
    f_s[pl.ds(lo, QB)] += dx[:QB]
    f_s[pl.ds(hi, QB)] += dx[QB:]
    share_rows(plan, tab, f_s, s_send.r, padded, x_keep.r)


def halve_kernel(cols, tab, ins, outs):
    keep, got = ins[0], ins[1:]
    kept, sends = outs[0], outs[1:]
    half = keep.shape[0] // 2
    size = half // 2
    for i in range(2):
        src, base = (got[0], i * half) if len(got) == 1 else (got[i], 0)
        mine = tab[cols[i]]
        for dst, block in ((kept.at[i * size : (i + 1) * size], mine), (sends[i], 1 - mine)):
            at = pl.multiple_of(i * half + block * size, size)
            there = pl.multiple_of(base + block * size, size)
            dst[...] = (keep[pl.ds(at, size)].astype(F32) + src[pl.ds(there, size)].astype(F32)).astype(BF16)


def split_kernel(col, tab, ins, outs):
    size, me = outs[0].shape[0], tab[col]
    for r, dst in enumerate(outs):
        at = pl.multiple_of((me ^ r) * size, size)
        total = ins[0][pl.ds(at, size)].astype(F32)
        for p in ins[1:]:
            total += p[pl.ds(at, size)].astype(F32)
        dst[...] = total.astype(BF16)


def block_kernel(kinds, names, tab, ins, outs):
    parts = []
    for kind, count in kinds:
        parts.append((kind, ins[:count], ins[0].shape[0]))
        ins = ins[count:]
    me = tab[names] if len(outs) > 1 else 0
    at = 0
    for kind, arrays, rows in parts:
        share = rows // len(outs)
        for r, dst in enumerate(outs):
            cuts = [(0, share, None)]
            if len(outs) > 1:
                start = pl.multiple_of((me ^ r) * share, share)
            else:
                start = 0
            if kind == "halves":
                half = rows // 2
                if len(outs) == 1:
                    cuts = [(0, half, arrays[1]), (half, half, arrays[2])]
                    for base, size, src in cuts:
                        total = arrays[0][base : base + size].astype(F32) + src[...].astype(F32)
                        dst[at + base : at + base + size] = total.astype(BF16)
                    continue
                inner = pl.multiple_of(lax.rem(start, half), share)
                in_b = start >= half
                for flag, src in ((False, arrays[1]), (True, arrays[2])):

                    @pl.when(in_b == flag)
                    def _(src=src, dst=dst, start=start, inner=inner, share=share, at=at):
                        total = arrays[0][pl.ds(start, share)].astype(F32) + src[pl.ds(inner, share)].astype(F32)
                        dst[at : at + share] = total.astype(BF16)

                continue
            total = arrays[0][pl.ds(start, share)].astype(F32)
            for p in arrays[1:]:
                total += p[pl.ds(start, share)].astype(F32)
            dst[at : at + share] = total.astype(BF16)
        at += rows // len(outs)


def unblock_kernel(rows, name, tab, ins, outs):
    me, out = tab[name], outs[0]
    at = to = 0
    for n in rows:
        for r, src in enumerate(ins):
            out[pl.ds(pl.multiple_of(to + (me ^ r) * n, n), n)] = src[at : at + n]
        at += n
        to += n * len(ins)


class Halving:
    def __init__(self, plan, tab, keep, got):
        self.plan, self.tab, self.kept, self.got = plan, tab, keep, [got]

    def halve(self, i, deps=()):
        rows, width = self.kept.shape
        shapes = [((n, width), BF16) for n in (rows // 2, rows // 4, rows // 4)]
        cols = [self.plan.at["step%d%s" % (i, side)] for side in "ab"]
        out = small(functools.partial(halve_kernel, cols), self.tab, [self.kept, *self.got], shapes, deps)
        self.kept = out[0]
        self.got = [swap(v, self.plan, bit) for v, bit in zip(out[1:], self.plan.steps[i])]
        return self.kept

    kind = ("halves", 3)


class Direct:
    def __init__(self, plan, tab, rows, keep, got):
        self.plan, self.tab, self.rows, self.kept, self.got = plan, tab, rows, keep, [got]

    def split(self, i, deps=()):
        stage = self.plan.near[i]
        n = 2 ** len(stage[1])
        self.rows //= n
        shapes = [((self.rows, self.kept.shape[1]), BF16)] * n
        kernel = functools.partial(split_kernel, self.plan.at["near%d" % i])
        out = small(kernel, self.tab, [self.kept, *self.got], shapes, deps)
        self.kept, self.got = out[0], [meet(out[r], stage, r) for r in range(1, n)]
        return self.kept

    @property
    def kind(self):
        return ("sum", 1 + len(self.got))


class Far:
    def __init__(self, plan, tab, chunks):
        self.plan, self.tab = plan, tab
        self.rows = [c.kept.shape[0] for c in chunks]
        self.width = chunks[0].kept.shape[1]
        self.kinds = [c.kind for c in chunks]
        self.parts = [v for c in chunks for v in (c.kept, *c.got)]

    def cut(self, n, name, deps):
        self.rows = [v // n for v in self.rows]
        kernel = functools.partial(block_kernel, self.kinds, name)
        self.kinds = [("sum", n)]
        return small(kernel, self.tab, self.parts, [((sum(self.rows), self.width), BF16)] * n, deps)

    def total(self, deps=()):
        return self.cut(1, 0, deps)[0]

    def scatter(self, i, deps=()):
        stage = self.plan.stages[i]
        n = 2 ** len(stage[1])
        out = self.cut(n, self.plan.at["far%d" % i], deps)
        self.parts = [out[0]] + [meet(out[r], stage, r) for r in range(1, n)]
        return out[0]

    def gather(self, i, own, deps=()):
        stage = self.plan.stages[i]
        n = 2 ** len(stage[1])
        ins = [own] + [meet(own, stage, r) for r in range(1, n)]
        kernel = functools.partial(unblock_kernel, self.rows, self.plan.at["far%d" % i])
        self.rows = [v * n for v in self.rows]
        return small(kernel, self.tab, ins, [((sum(self.rows), self.width), BF16)], deps)[0]


def halves_kernel(tab, ins, outs):
    half = ins[0].shape[0] // 2
    for i, dst in enumerate(outs):
        dst[...] = ins[0][i * half : (i + 1) * half]


def join_kernel(cols, tab, ins, outs):
    own, *got = ins
    size = own.shape[0] // 2
    for i in range(2):
        mine = tab[cols[i]]
        for src, block in ((own.at[i * size : (i + 1) * size], mine), (got[i], 1 - mine)):
            at = pl.multiple_of(block * size, size)
            value = src[...]
            outs[1 + i][pl.ds(at, size)] = value
            outs[0][pl.ds(pl.multiple_of(2 * i * size + at, size), size)] = value


class Doubling:
    def __init__(self, plan, tab, own, deps):
        self.plan, self.tab, self.own = plan, tab, own
        rows, self.width = own.shape
        self.apart = small(halves_kernel, tab, [own], [((rows // 2, self.width), BF16)] * 2, deps)
        self.move(len(plan.steps) - 1)

    def move(self, i):
        self.got = [swap(v, self.plan, bit) for v, bit in zip(self.apart, self.plan.steps[i])]

    def join(self, i, deps=()):
        cols = [self.plan.at["step%d%s" % (i, side)] for side in "ab"]
        rows = self.own.shape[0]
        shapes = [((n, self.width), BF16) for n in (2 * rows, rows, rows)]
        self.own, *self.apart = small(
            functools.partial(join_kernel, cols), self.tab, [self.own, *self.got], shapes, deps
        )
        self.move(i - 1)

    def both(self, after):
        mine, _ = lax.optimization_barrier(([self.own, *self.got], after))
        return mine + [swap(v, self.plan, self.plan.core) for v in mine]


def near_parts(plan, own):
    out = [((), own)]
    for stage in plan.near:
        n = 2 ** len(stage[1])
        out = [(r + (k,), v if k == 0 else meet(v, stage, k)) for k in range(n) for r, v in out]
    return out


def both_cores(plan, parts):
    return [(r, side, v if side == 0 else swap(v, plan, plan.core)) for side in range(2) for r, v in parts]


def halving_at(plan, tab, diff, rows, i):
    size = rows // 2
    at = i * size
    for j in range(len(plan.steps)):
        size //= 2
        axis, shift = plan.steps[j][i]
        flip = 0
        for (_, shifts, _), d in zip(plan.near, diff):
            if shift in shifts:
                flip = (d >> shifts.index(shift)) & 1
        at = at + (tab[plan.at["step%d%s" % (j, "ab"[i])]] ^ flip) * size
    return at, size


def direct_at(plan, tab, diff, rows):
    at, size = 0, rows
    for j, ((_, shifts, _), d) in enumerate(zip(plan.near, diff)):
        size >>= len(shifts)
        at = at + (tab[plan.at["near%d" % j]] ^ d) * size
    return at, size


def feed_final(plan, tab, raw, ins, outs, raw_outs):
    down, up, mark = outs
    mark.r[...] = jnp.zeros(mark.r.shape, F32)
    mine = tab[plan.at["half"]]
    bits = [tab[plan.at["step0" + side]] for side in "ab"]
    half = down.r.shape[0] // 2
    size = half // 2

    def put(far, flip, a, b):
        side = mine ^ far
        at = pl.multiple_of(side * half + (bits[0] ^ flip) * size, size)
        down.r[pl.ds(at, size)] = a.astype(F32)
        at = pl.multiple_of(side * half + (bits[1] ^ flip) * size, size)
        up.r[:, pl.ds(at, size)] = b.astype(F32)

    for far in range(2):
        own, a, b = ins[3 * far : 3 * far + 3]
        put(far, 0, own.r[:size], own.r[size:])
        put(far, 1, a.r[...], b.r[...])


def rest_final(plan, diffs, c_rows, s_rows, tab, raw, ins, outs, raw_outs, c_s, s_s):
    qkv, ckv, cq, co, so, tiny = outs
    width = qkv.r.shape[0]
    step = width // 2
    for (diff, far), load in zip(diffs, ins):
        src = load.r
        base = 0
        for i in range(2):
            at, size = halving_at(plan, tab, diff, c_rows, i)
            c_s[far, pl.ds(pl.multiple_of(at, size), size)] = src[base : base + size]
            base += size
        at, size = direct_at(plan, tab, diff, s_rows)
        s_s[far, pl.ds(pl.multiple_of(at, size), size)] = src[base : base + size]
    mine = tab[plan.at["half"]]
    places = [pl.ds(pl.multiple_of((mine ^ far) * step, step), step) for far in range(2)]
    for i in range(3):
        for far, at in enumerate(places):
            qkv.r[at, i * width : (i + 1) * width] = s_s[far, i * step : (i + 1) * step].astype(F32)
    qkv.send()
    for i in range(2):
        for far, at in enumerate(places):
            ckv.r[at, i * width : (i + 1) * width] = c_s[far, i * step : (i + 1) * step].astype(F32)
    ckv.send()
    for i, dst in enumerate((cq, co, so)):
        for far, at in enumerate(places):
            dst.r[at] = c_s[far, (2 + i) * step : (3 + i) * step].astype(F32)
        dst.send()
    tail = slice(5 * step, 5 * step + 8)
    tiny.r[...] = c_s[0, tail].astype(F32) + c_s[1, tail].astype(F32)


def row_blocks(x, plan, scalar):
    return [lax.dynamic_index_in_dim(x, scalar("row%d" % t), 0, keepdims=False) for t in range(plan.rows)]


def to_rows(blocks, plan):
    return [lax.ppermute(b, AXES, plan.perms[t]) for t, b in enumerate(blocks)]


def send_back(parts, plan):
    return [lax.ppermute(p, AXES, [(d, s) for s, d in plan.perms[t]]) for t, p in enumerate(parts)]


def give_kernel(plan, tab, raw, ins, outs, raw_outs):
    tok = plan.tok
    for t, dst in enumerate(outs):
        rows = slice(t * tok, (t + 1) * tok)
        for i in range(2):
            keep, got = raw[2 * i : 2 * i + 2]
            base = got.shape[0] - plan.rows * tok
            came = got[base + t * tok : base + (t + 1) * tok].astype(F32)
            dst.r[i * tok : (i + 1) * tok] = (keep[rows].astype(F32) + came).astype(BF16)
        dst.send()


def take_kernel(plan, tab, raw, ins, outs, raw_outs):
    *arrays, mark = outs
    tok = plan.tok
    for t, load in enumerate(ins):
        row = tab[plan.at["row%d" % t]]
        for i, dst in enumerate(arrays):
            dst.r[row] = load.r[i * tok : (i + 1) * tok].astype(dst.r.dtype)
    mark.r[...] = jnp.zeros(mark.r.shape, F32)


def body(plan, tokens, memory, tgt_seg, mem_seg, cotangent, w_qkv, w_so, w_cq, w_ckv, w_co, w_up, w_down, *norms):
    n, tok, width = tokens.shape
    length = tgt_seg.shape[1]
    heads = width // HEAD_DIM
    ff = w_up.shape[1]
    own = length // 2
    g1, b1, g2, b2, g3, b3 = (v.reshape(1, width) for v in norms)
    known = plan.scalars()
    scalar = lambda name: known[name]
    tab = jnp.stack([known[name] for name in plan.at])

    segs = jnp.stack([tgt_seg, mem_seg])
    if plan.pair_in_dp:
        far = swap(segs, plan, plan.core)
        segs = jnp.where(scalar("seg_far") == 1, far, segs)
    segs = lax.dynamic_index_in_dim(segs, scalar("seg_row"), 1, keepdims=False)
    lane = jnp.arange(HEAD_DIM)[None, :]
    qf = (segs[0][:, None] == lane).astype(BF16)
    kf, mf = (jnp.where((s[:, None] != lane) & (lane < 3), OFF, 0.0).astype(BF16) for s in segs)

    def both(parts):
        return parts + [swap(p, plan, plan.core) for p in parts]

    x_own = to_rows(row_blocks(tokens, plan, scalar), plan)
    x_parts = both(x_own)
    blocks, x_own = lax.optimization_barrier((row_blocks(memory, plan, scalar), x_own))
    m_own = to_rows(blocks, plan)
    blocks, x_parts = lax.optimization_barrier((row_blocks(cotangent, plan, scalar), x_parts))
    g_parts = to_rows(blocks, plan)

    arr = lambda r, c, d=F32: ((r, c), d)
    low = lambda r, c: ((r, c), BF16)
    vs = lambda r, c, d=BF16: pltpu.VMEM((r, c), d)
    sem = lambda k: pltpu.SemaphoreType.DMA((k,))
    wide = heads * AUG
    e_self, e_cross = (heads, QB, 5 * QB), (heads, own, length)

    q1, k1, v1, rl1, c1, n1, r1, cq, e1 = big(
        functools.partial(self_forward, plan, heads),
        tab,
        x_parts,
        [w_qkv, qf, kf, w_so, g1, b1, w_cq],
        [
            low(own, width),
            low(length, wide),
            low(length, wide),
            arr(own, heads),
            low(own, width),
            arr(own, width),
            arr(own, 1),
            low(own, width),
        ],
        [vs(length, width), pltpu.VMEM(e_self, BF16), sem(2 * n), sem(heads)],
        14,
        raw_outs=[(e_self, BF16)],
    )
    m_own, cq = lax.optimization_barrier((m_own, cq))
    m_parts = both(m_own)
    k2, v2, rl2, c2, n2, r2, e2 = big(
        functools.partial(cross_forward, plan, heads),
        tab,
        m_parts,
        [w_ckv, qf, mf, cq, w_co, n1, g1, b1],
        [low(length, wide), low(length, wide), arr(own, heads), low(own, width), arr(own, width), arr(own, 1)],
        [vs(length, width), pltpu.VMEM(e_cross, BF16), sem(2 * n), sem(heads)],
        15,
        raw_outs=[(e_cross, BF16)],
    )
    f_send, f_keep, du, dy3, tiny, *o_rows = big(
        functools.partial(feed, plan),
        tab,
        g_parts,
        [n2, g2, b2, w_up, w_down, g3, b3],
        [low(ff, width), low(ff, width), low(own, ff), arr(own, width), arr(8, width)]
        + [low(tok, width)] * n,
        [vs(own, width), vs(own, ff), sem(n)],
        12,
    )
    f = Halving(plan, tab, f_keep, swap(f_send, plan, plan.core))
    dy2, tiny = big(
        feed_inputs, tab, [], [du, w_up, dy3, n2, r2, g2, tiny], [arr(own, width), arr(8, width)], [], 4, mib=20
    )
    steps = len(plan.steps)
    kept = f.halve(0, [dy2])
    groups = 2
    some = heads // groups

    def backward(first, some, kernel, raw, ins, extra, us, deps):
        cols = some * HEAD_DIM
        return big(
            functools.partial(kernel, first, some),
            tab,
            raw,
            ins,
            [low(2 * cols, length), low(own, cols)],
            [
                pltpu.VMEM((some,) + raw[0].shape[1:], BF16),
                vs(length, some * AUG),
                vs(length, some * AUG),
                vs(own, cols),
                vs(own, some, F32),
                sem(2 + some),
            ]
            + extra,
            us,
            deps=deps,
            raw_spec=HB,
        )

    cross_part = lambda i, deps: backward(
        i * some, some, cross_heads, [e2, k2, v2], [dy2, w_co, c2, rl2, cq], [vs(own, length)], 9, deps
    )
    kv_a, dq_a = cross_part(0, [kept])
    for i in range(1, steps):
        kept = f.halve(i, [dq_a])
    out_back = send_back(o_rows, plan)
    kv_b, dq_b = cross_part(1, [kept, dq_a])
    f = Far(plan, tab, [f])
    kept = f.scatter(0, [dq_b])
    c_rows, s_rows = plan.padded(3 * width), plan.padded(3 * width // 2)
    dy1, c_send, c_keep, m_keep = big(
        functools.partial(cross_dense, plan, groups, c_rows),
        tab,
        m_parts,
        [dq_a, dq_b, w_cq, dy2, n1, r1, g1, b1, tiny, kv_a, kv_b, c2, c1, w_ckv],
        [arr(own, width), low(c_rows + own, width), low(c_rows, width), low(own, width)],
        [vs(length, width), vs(2 * width, length), vs(length, width, F32), vs(own, width), sem(2 * n)],
        11,
        deps=[kept, *out_back],
    )
    for i in range(1, len(plan.stages)):
        f.scatter(i, [dy1])
    f_own = f.total([dy1])
    for i in reversed(range(1, len(plan.stages))):
        f_own = f.gather(i, f_own)
    c_send, f_own = lax.optimization_barrier((c_send, f_own))
    c_got = swap(c_send, plan, plan.core)
    c = Halving(plan, tab, c_keep, c_got)
    kept = c.halve(0)
    kv_c, dq_c = backward(
        0, heads, functools.partial(self_heads, plan), [e1, k1, v1], [dy1, w_so, c1, rl1, q1], [], 13, [f_own, kept]
    )
    f_own = f.gather(0, f_own, [dq_c])
    for i in range(1, steps):
        kept = c.halve(i, [dq_c])
    s_send, s_keep, x_keep = big(
        functools.partial(self_dense, plan, 1, s_rows),
        tab,
        x_parts,
        [kv_c, dq_c, w_qkv, dy1],
        [low(s_rows + own, width), low(s_rows, width), low(own, width)],
        [vs(length, width), vs(2 * width, length), vs(own, width), vs(length, width, F32), sem(2 * n)],
        7,
        deps=[f_own, kept],
    )
    s_got = swap(s_send, plan, plan.core)
    s = Direct(plan, tab, s_rows, s_keep, s_got)
    for i in range(len(plan.near)):
        s.split(i)
    rest = Far(plan, tab, [c, s])
    for i in range(len(plan.stages)):
        kept = rest.scatter(i)
    f = Doubling(plan, tab, f_own, [kept])
    rest_own = rest.total()
    for i in reversed(range(1, steps)):
        f.join(i, [rest_own])
    for i in reversed(range(1, len(plan.stages))):
        rest_own = rest.gather(i, rest_own)

    def finish(kernel, arrays, outs, scratch, more=(), deps=()):
        diffs = [(diff, far) for diff, far, _ in arrays]
        return big(
            functools.partial(kernel, plan, diffs, *more), tab, [], [v for _, _, v in arrays], outs, scratch, 5, deps=deps
        )

    def take(parts, kinds):
        outs = [((n, tok, width), d) for d in kinds] + [arr(8, 128)]
        return big(functools.partial(take_kernel, plan), tab, [], parts, outs, [], 2)

    output, mark = take(out_back, [BF16])
    rest_own = rest.gather(0, rest_own, [mark, *f.got])
    rest_near = near_parts(plan, rest_own)
    turns = big(
        functools.partial(give_kernel, plan),
        tab,
        [m_keep, c_got, x_keep, s_got],
        [],
        [low(2 * tok, width)] * n,
        [],
        2,
        deps=[rest_own],
        raw_spec=VM,
    )
    back = send_back(turns, plan)
    down, up, late = big(
        functools.partial(feed_final, plan),
        tab,
        [],
        f.both(turns[0]),
        [arr(ff, width), arr(width, ff), arr(8, 128)],
        [],
        5,
    )
    arrays, late, back = lax.optimization_barrier(([v for _, v in rest_near], late, back))
    all_rest = both_cores(plan, [(d, v) for (d, _), v in zip(rest_near, arrays)])
    grad_memory, grad_tokens, mark = take(back, [F32, F32])
    qkv, ckv, d_cq, d_co, d_so, tiny = finish(
        rest_final,
        all_rest,
        [arr(width, 3 * width), arr(width, 2 * width)] + [arr(width, width)] * 3 + [arr(8, width)],
        [pltpu.VMEM((2, c_rows, width), BF16), pltpu.VMEM((2, s_rows, width), BF16)],
        (c_rows, s_rows),
        [late],
    )
    return (output, grad_tokens, grad_memory, qkv, d_so, d_cq, ckv, d_co, up, down) + tuple(
        tiny[i] for i in range(6)
    )


def solution(mesh):
    def whole(*args):
        rows = args[0].shape[0] // mesh.shape["dp"]
        tok = args[0].shape[1] // mesh.shape["seq"]
        plan = Plan(mesh, rows, tok)
        split, copied = P("dp", "seq", None), P()
        return jax.shard_map(
            functools.partial(body, plan),
            mesh=mesh,
            in_specs=(split, split, P("dp", None), P("dp", None), split) + (copied,) * 13,
            out_specs=(split,) * 3 + (copied,) * 13,
            check_vma=False,
        )(*args)

    return whole
```

```python
import functools

import jax
import jax.numpy as jnp
import numpy as np
from jax import lax
from jax.experimental import pallas as pl
from jax.experimental.pallas import tpu as pltpu
from jax.sharding import PartitionSpec as P

F32 = jnp.float32
BF16 = jnp.bfloat16
HEAD_DIM = 64
AUG = 2 * HEAD_DIM
QB = 256
OFF = -1e9
AXES = ("dp", "seq")
COST = 3e8
VM = pl.BlockSpec(memory_space=pltpu.VMEM)
SM = pl.BlockSpec(memory_space=pltpu.SMEM)
HB = pl.BlockSpec(memory_space=pltpu.HBM)
ANY = pl.BlockSpec(memory_space=pl.ANY)


def dg(a, b, ca, cb):
    return lax.dot_general(a, b, (((ca,), (cb,)), ((), ())), preferred_element_type=F32)


class Plan:
    def __init__(self, mesh, rows, tok):
        dp, seq = mesh.shape["dp"], mesh.shape["seq"]
        self.dp, self.seq, self.rows, self.tok = dp, seq, rows, tok
        self.pair_in_dp = seq == 4
        assert rows * 2 == seq and seq in (4, 8)
        if self.pair_in_dp:
            dev = lambda k, c, h: (2 * k + h) * seq + c
            team_row = lambda h, j: 2 * h + j
            start = lambda c, h: c
            teams = dp // 2
            self.core = ("dp", 0)
            chips, line = self.bits("dp", 1, dp), self.bits("seq", 0, seq)
        else:
            dev = lambda k, c, h: k * seq + 2 * c + h
            team_row = lambda h, j: j
            start = lambda c, h: 2 * c + h
            teams = dp
            self.core = ("seq", 0)
            chips, line = self.bits("dp", 0, dp), self.bits("seq", 1, seq)
        count = dp * seq
        own = {0: (0, 3), 1: (1, 2)}
        half_of = {0: 0, 3: 0, 1: 1, 2: 1}
        todo = []
        for c in range(4):
            for h in range(2):
                for j in range(rows):
                    block = start(c, h) * tok // QB
                    todo.append(((c, h), (team_row(h, j), half_of[block]), j, start(c, h)))
        self.perms = []
        self.send_row = np.zeros((count, rows), np.int32)
        self.recv_at = np.zeros((count, rows), np.int32)
        nodes = [(c, h) for c in range(4) for h in range(2)]
        for turn in range(rows):
            match = {}

            def grow(src, seen):
                for e in todo:
                    if e[0] == src and e[1] not in seen:
                        seen.add(e[1])
                        if e[1] not in match or grow(match[e[1]][0], seen):
                            match[e[1]] = e
                            return True
                return False

            for src in nodes:
                assert grow(src, set())
            pairs = []
            for e in match.values():
                todo.remove(e)
                for k in range(teams):
                    s, d = dev(k, *e[0]), dev(k, *e[1])
                    pairs.append((s, d))
                    self.send_row[s, turn] = e[2]
                    self.recv_at[d, turn] = e[3]
            self.perms.append(sorted(pairs))
        place = np.zeros(count, np.int32)
        half, chip = np.zeros(count, np.int32), np.zeros(count, np.int32)
        sibling = np.zeros(count, np.int32)
        for k in range(teams):
            for c in range(4):
                for h in range(2):
                    d = dev(k, c, h)
                    half[d], chip[d], place[d] = h, c, 2 * c + h
                    sibling[d] = dev(k, c, 1 - h)
        self.codes = {}

        def add(name, values):
            by_place = [int(np.asarray(values)[place == p][0]) for p in range(8)]
            assert all(by_place[p] == v for p, v in zip(place, values))
            self.codes[name] = by_place

        add("half", half)
        add("lo", half)
        add("hi", 3 - half)
        if self.pair_in_dp:
            add("seg_far", (chip // 2 != half).astype(np.int32))
            add("seg_row", chip % 2)
        else:
            add("seg_far", np.zeros(count, np.int32))
            add("seg_row", chip)
        for t in range(rows):
            pos = self.recv_at[:, t] * tok
            add("own%d" % t, self.recv_at[:, t])
            add("sib%d" % t, self.recv_at[sibling, t])
            add("loc%d" % t, (np.where(pos // QB == half, 0, QB) + pos % QB) // tok)
            add("row%d" % t, self.send_row[:, t])
        far = len(chips) // 2
        self.steps = []
        for p, q in zip(chips[:far], chips[far:]):
            self.steps += [(p, q), (q, p)]
        near = [b for p, q in zip(chips[:far], chips[far:]) for b in (p, q)]
        self.near = self.groups("dp", sorted(near), dp)
        self.stages = self.groups("dp", chips[2 * far :], dp) + self.groups("seq", line, seq)
        self.bit_names = {}
        for i, step in enumerate(self.steps):
            for side, bit in zip("ab", step):
                self.bit_names["step%d%s" % (i, side)] = (bit[0], bit[1], 1)
        for i, (axis, shifts, _) in enumerate(self.near):
            self.bit_names["near%d" % i] = (axis, shifts[0], 2 ** len(shifts) - 1)
        for i, (axis, shifts, _) in enumerate(self.stages):
            self.bit_names["far%d" % i] = (axis, shifts[0], 2 ** len(shifts) - 1)
        self.at = {name: i for i, name in enumerate([*self.codes, *self.bit_names])}

    def padded(self, rows):
        unit = 16 * 2 ** len(self.steps)
        for _, bits, _ in self.stages:
            unit *= 2 ** len(bits)
        return -(-rows // unit) * unit

    def scalars(self):
        dp, seq = lax.axis_index("dp"), lax.axis_index("seq")
        place = 2 * seq + (dp & 1) if self.pair_in_dp else seq
        out = {}
        for name, by_place in self.codes.items():
            code = sum(v << (3 * p) for p, v in enumerate(by_place))
            out[name] = (jnp.int32(code) >> (3 * place)) & 7
        for name, (axis, shift, mask) in self.bit_names.items():
            out[name] = ((dp if axis == "dp" else seq) >> shift) & mask
        return out

    @staticmethod
    def bits(axis, shift, size):
        return [(axis, i) for i in range(shift, size.bit_length() - 1)]


    @staticmethod
    def groups(axis, bits, size):
        out = []
        bits = [shift for _, shift in bits]
        while bits:
            now, bits = bits[:2], bits[2:]
            mask = sum(1 << b for b in now)
            rest = [i for i in range(size) if not i & mask]
            steps = [0]
            for b in now:
                steps += [v + (1 << b) for v in steps]
            out.append((axis, now, [[i + v for v in steps] for i in rest]))
        return out


def meet(x, stage, r):
    axis, _, groups = stage
    pairs = [(g[k], g[k ^ r]) for g in groups for k in range(len(g))]
    return lax.ppermute(x, axis, pairs)


def swap(x, plan, bit):
    axis, shift = bit
    n = plan.dp if axis == "dp" else plan.seq
    return lax.ppermute(x, axis, [(i, i ^ (1 << shift)) for i in range(n)])


def norm_forward(y):
    centre = y - jnp.mean(y, axis=-1, keepdims=True)
    recip = lax.rsqrt(jnp.mean(centre * centre, axis=-1, keepdims=True) + 1e-05)
    return centre * recip, recip


def norm_back(grad, normed, recip, gain):
    d_gain = jnp.sum(grad * normed, axis=0, keepdims=True)
    d_bias = jnp.sum(grad, axis=0, keepdims=True)
    scaled = grad * gain
    d_in = recip * (
        scaled
        - jnp.mean(scaled, axis=-1, keepdims=True)
        - normed * jnp.mean(scaled * normed, axis=-1, keepdims=True)
    )
    return d_in, d_gain, d_bias


def augment(dst, x, tail):
    for h in range(x.shape[1] // HEAD_DIM):
        dst[:, h * AUG : (h + 1) * AUG] = jnp.concatenate(
            [x[:, h * HEAD_DIM : (h + 1) * HEAD_DIM], tail], axis=1
        )


def ones_tail(n):
    return (lax.broadcasted_iota(jnp.int32, (n, HEAD_DIM), 1) == 0).astype(BF16)


def head_forward(q, k, v, tri):
    s = dg(q, k, 1, 1)
    n = k.shape[0]
    if tri is not None:
        edge = s[:, n - QB :] + tri
        s = edge if n == QB else jnp.concatenate([s[:, : n - QB], edge], axis=1)
    e = jnp.exp(s - jnp.max(s, axis=1, keepdims=True)).astype(BF16)
    cv = dg(e, v, 1, 0)
    recip = 1.0 / cv[:, HEAD_DIM : HEAD_DIM + 1]
    return e, (cv[:, :HEAD_DIM] * recip).astype(BF16), recip


class Load:
    def __init__(self, src, dst, sem):
        self.dst, self.copy = dst, pltpu.make_async_copy(src, dst, sem)
        self.copy.start()
        self.here = False

    @property
    def r(self):
        if not self.here:
            self.copy.wait()
            self.here = True
        return self.dst


class Store:
    def __init__(self, src, dst, sem):
        self.r, self.copy, self.sent = src, pltpu.make_async_copy(src, dst, sem), False

    def send(self):
        self.copy.start()
        self.sent = True

    def done(self):
        if not self.sent:
            self.send()
        self.copy.wait()


def gather_rows(tab, plan, names, parts, dst, sems):
    out = []
    for i, (name, ref) in enumerate(zip(names, parts)):
        at = pl.multiple_of(tab[plan.at[name]] * plan.tok, plan.tok)
        out.append(Load(ref, dst.at[pl.ds(at, plan.tok)], sems.at[i]))
    return out


def row_names(plan):
    return ["own%d" % t for t in range(plan.rows)] + ["sib%d" % t for t in range(plan.rows)]


def arrive(loads):
    for v in loads:
        v.r


def big(kernel, tab, raw, ins, outs, scratch, us, raw_outs=(), deps=(), mib=44, free=(), raw_spec=HB):
    n_raw, n_in, n_dep, n_out, n_ro = len(raw), len(ins), len(deps), len(outs), len(raw_outs)

    def run(tab, *refs):
        raws, refs = refs[:n_raw], refs[n_raw:]
        srcs, refs = refs[:n_in], refs[n_in + n_dep :]
        dsts, refs = refs[:n_out], refs[n_out:]
        raw_dsts, refs = refs[:n_ro], refs[n_ro:]
        in_room, refs = refs[:n_in], refs[n_in:]
        out_room, refs = refs[:n_out], refs[n_out:]
        sems, refs = refs[0], refs[1:]
        loads = [Load(s, d, sems.at[i]) for i, (s, d) in enumerate(zip(srcs, in_room))]
        stores = [Store(s, d, sems.at[n_in + i]) for i, (s, d) in enumerate(zip(out_room, dsts))]
        kernel(tab, raws, loads, stores, raw_dsts, *refs)
        arrive(loads)
        for v in stores:
            v.done()

    room = [pltpu.VMEM(v.shape, v.dtype) for v in ins] + [pltpu.VMEM(s, d) for s, d in outs]
    return pl.pallas_call(
        run,
        out_shape=[jax.ShapeDtypeStruct(s, d) for s, d in [*outs, *raw_outs]],
        in_specs=[SM] + [raw_spec] * n_raw + [HB] * n_in + [ANY] * n_dep,
        out_specs=[ANY if i in free else HB for i in range(n_out)] + [HB] * n_ro,
        scratch_shapes=room + [pltpu.SemaphoreType.DMA((n_in + n_out,))] + scratch,
        compiler_params=pltpu.CompilerParams(vmem_limit_bytes=mib * 2**20),
        cost_estimate=pl.CostEstimate(flops=int(us * COST), bytes_accessed=2**20, transcendentals=0),
    )(tab, *raw, *ins, *deps)


def small(kernel, tab, ins, outs, deps=(), mib=16):
    n_in, n_dep = len(ins), len(deps)

    def run(tab, *refs):
        kernel(tab, refs[:n_in], refs[n_in + n_dep :])

    return pl.pallas_call(
        run,
        out_shape=[jax.ShapeDtypeStruct(s, d) for s, d in outs],
        in_specs=[SM] + [VM] * n_in + [ANY] * n_dep,
        out_specs=[VM] * len(outs),
        compiler_params=pltpu.CompilerParams(vmem_limit_bytes=mib * 2**20),
        cost_estimate=pl.CostEstimate(flops=int(2 * COST), bytes_accessed=2**20, transcendentals=0),
    )(tab, *ins, *deps)


def own_rows(plan, tab, ref):
    lo = pl.multiple_of(tab[plan.at["lo"]] * QB, QB)
    hi = pl.multiple_of(tab[plan.at["hi"]] * QB, QB)
    return jnp.concatenate([ref[pl.ds(lo, QB)], ref[pl.ds(hi, QB)]], axis=0)


def head_cols(h):
    return slice(h * HEAD_DIM, (h + 1) * HEAD_DIM)


def self_forward(plan, heads, tab, raw, ins, outs, raw_outs, x_s, e_s, sems, e_sems):
    wqkv, qf, kf, wso, g1, b1, wcq = ins
    q_out, k_out, v_out, rl_out, c_out, n_out, r_out, cq_out = outs
    pieces = gather_rows(tab, plan, row_names(plan), raw, x_s, sems)
    width = heads * HEAD_DIM
    w = wqkv.r
    arrive(pieces)
    k = dg(x_s[...], w[:, width : 2 * width], 1, 0).astype(BF16)
    augment(k_out.r, k, kf.r[...])
    k_out.send()
    v = dg(x_s[...], w[:, 2 * width :], 1, 0).astype(BF16)
    augment(v_out.r, v, ones_tail(v.shape[0]))
    v_out.send()
    x_own = own_rows(plan, tab, x_s)
    q_out.r[...] = (dg(x_own, w[:, :width], 1, 0).astype(BF16).astype(F32) * 0.125).astype(BF16)
    q_out.send()
    qf_own = own_rows(plan, tab, qf.r)
    tri = jnp.where(
        lax.broadcasted_iota(jnp.int32, (QB, QB), 1) <= lax.broadcasted_iota(jnp.int32, (QB, QB), 0),
        0.0,
        OFF,
    )

    def attend(core):
        sizes = (QB * (core + 1), QB * (4 - core))
        for h in range(heads):
            at = 0
            for i, keys in enumerate(sizes):
                rows = slice(i * QB, (i + 1) * QB)
                q = jnp.concatenate([q_out.r[rows, head_cols(h)], qf_own[rows]], axis=1)
                wide = slice(h * AUG, (h + 1) * AUG)
                e, c, recip = head_forward(q, k_out.r[:keys, wide], v_out.r[:keys, wide], tri)
                e_s[h, :, at : at + keys] = e
                c_out.r[rows, head_cols(h)] = c
                rl_out.r[rows, h : h + 1] = recip
                at += keys
            pltpu.make_async_copy(e_s.at[h], raw_outs[0].at[h], e_sems.at[h]).start()

    for core in range(2):
        pl.when(tab[plan.at["half"]] == core)(functools.partial(attend, core))
    rl_out.send()
    c_out.send()
    y = x_own.astype(F32) + dg(c_out.r[...], wso.r[...], 1, 0)
    normed, recip = norm_forward(y)
    n_out.r[...] = normed
    n_out.send()
    r_out.r[...] = recip
    r_out.send()
    z = (normed * g1.r[...] + b1.r[...]).astype(BF16)
    cq_out.r[...] = (dg(z, wcq.r[...], 1, 0).astype(BF16).astype(F32) * 0.125).astype(BF16)
    for h in range(heads):
        pltpu.make_async_copy(e_s.at[h], raw_outs[0].at[h], e_sems.at[h]).wait()


def cross_forward(plan, heads, tab, raw, ins, outs, raw_outs, m_s, e_s, sems, e_sems):
    wckv, qf, kf, cq, wco, n1, g1, b1 = ins
    k_out, v_out, rl_out, c_out, n_out, r_out = outs
    pieces = gather_rows(tab, plan, row_names(plan), raw, m_s, sems)
    width = heads * HEAD_DIM
    w = wckv.r
    arrive(pieces)
    k = dg(m_s[...], w[:, :width], 1, 0).astype(BF16)
    augment(k_out.r, k, kf.r[...])
    k_out.send()
    v = dg(m_s[...], w[:, width:], 1, 0).astype(BF16)
    augment(v_out.r, v, ones_tail(v.shape[0]))
    v_out.send()
    qf_own = own_rows(plan, tab, qf.r)
    copies = []
    for h in range(heads):
        for i in range(2):
            rows = slice(i * QB, (i + 1) * QB)
            q = jnp.concatenate([cq.r[rows, head_cols(h)], qf_own[rows]], axis=1)
            wide = slice(h * AUG, (h + 1) * AUG)
            e, c, recip = head_forward(q, k_out.r[:, wide], v_out.r[:, wide], None)
            e_s[h, rows] = e
            c_out.r[rows, head_cols(h)] = c
            rl_out.r[rows, h : h + 1] = recip
        copies.append(pltpu.make_async_copy(e_s.at[h], raw_outs[0].at[h], e_sems.at[h]))
        copies[-1].start()
    rl_out.send()
    c_out.send()
    y = n1.r[...] * g1.r[...] + b1.r[...] + dg(c_out.r[...], wco.r[...], 1, 0)
    normed, recip = norm_forward(y)
    n_out.r[...] = normed
    r_out.r[...] = recip
    for cp in copies:
        cp.wait()


def feed(plan, tab, raw, ins, outs, raw_outs, g_s, h_s, sems):
    n2, g2, b2, wup, wdown, g3, b3 = ins
    f_send, f_keep, du_out, dy_out, small_out, *o_out = outs
    n, tok = plan.rows, plan.tok
    grads = gather_rows(tab, plan, ["loc%d" % t for t in range(n)], raw, g_s, sems)
    z2 = n2.r[...] * g2.r[...] + b2.r[...]
    z2b = z2.astype(BF16)
    width = z2.shape[1]
    ff = wup.dst.shape[1]
    half = ff // 2
    fed = jnp.zeros(z2.shape, F32)
    d = du_out.r
    for i in range(0, ff, width):
        cols = slice(i, i + width)
        u = dg(z2b, wup.r[:, cols], 1, 0)
        sig = 0.5 + 0.5 * jnp.tanh(0.5 * u)
        h_s[:, cols] = (u * sig).astype(BF16)
        d[:, cols] = (sig * (1.0 + u * (1.0 - sig))).astype(BF16)
        fed += dg(h_s[:, cols], wdown.r[cols, :], 1, 0)
    n3, r3 = norm_forward(z2 + fed)
    arrive(grads)
    dy3, dg3, db3 = norm_back(g_s[...].astype(F32), n3, r3, g3.r[...])
    g_s[...] = (n3 * g3.r[...] + b3.r[...]).astype(BF16)
    for t in range(n):
        at = pl.multiple_of(tab[plan.at["loc%d" % t]] * tok, tok)
        o_out[t].r[...] = g_s[pl.ds(at, tok)]
        o_out[t].send()
    dy_out.r[...] = dy3
    dy_out.send()
    small_out.r[...] = jnp.concatenate([dg3, db3, jnp.zeros((6, width), F32)], axis=0)
    dfb = dy3.astype(BF16)
    mine = tab[plan.at["half"]]
    sides = ((f_send, 1 - mine), (f_keep, mine))
    for dst, side in sides:
        at = pl.multiple_of(side * half, half)
        dst.r[:half] = dg(h_s[:, pl.ds(at, half)], dfb, 0, 0).astype(BF16)
    for i in range(0, ff, width):
        cols = slice(i, i + width)
        d[:, cols] = (dg(dfb, wdown.r[cols, :], 1, 1) * d[:, cols].astype(F32)).astype(BF16)
    du_out.send()
    for dst, side in sides:
        for i in range(half // width):
            at = pl.multiple_of(side * half + i * width, width)
            rows = slice(half + i * width, half + (i + 1) * width)
            dst.r[rows] = dg(z2b, d[:, pl.ds(at, width)], 0, 0).astype(BF16)
        dst.send()


def feed_inputs(tab, raw, ins, outs, raw_outs):
    du, wup, dy3, n2, r2, g2, small_in = ins
    dy_out, small_out = outs
    dz2 = dy3.r[...] + dg(du.r[...], wup.r[...], 1, 1)
    dy2, dg2, db2 = norm_back(dz2, n2.r[...], r2.r[...], g2.r[...])
    dy_out.r[...] = dy2
    small_out.r[...] = jnp.concatenate([dg2, db2, small_in.r[:6]], axis=0)


def context_grad(dy, w, c, rl, first, heads, dc_s, dd_s):
    group = slice(first * HEAD_DIM, (first + heads) * HEAD_DIM)
    dc = dg(dy[...].astype(BF16), w[group], 1, 1)
    cf = c[:, group].astype(F32)
    for h in range(heads):
        part = dc[:, head_cols(h)] * rl[:, first + h : first + h + 1]
        dc_s[:, head_cols(h)] = part.astype(BF16)
        dd_s[:, h : h + 1] = jnp.sum(part * cf[:, head_cols(h)], axis=1, keepdims=True)
    return group


def head_loads(first, heads, raw, e_s, k_s, v_s, sems):
    wide = pl.ds(first * AUG, heads * AUG)
    e_in, k_in, v_in = raw
    v = Load(v_in.at[:, wide], v_s, sems.at[0])
    e = [Load(e_in.at[first + h], e_s.at[h], sems.at[2 + h]) for h in range(heads)]
    return v, Load(k_in.at[:, wide], k_s, sems.at[1]), e


def cross_heads(first, heads, tab, raw, ins, outs, raw_outs, e_s, k_s, v_s, dc_s, dd_s, sems, ds_s):
    dy, wo, c, rl, q = ins
    kv_out, dq_out = outs
    v, k, e = head_loads(first, heads, raw, e_s, k_s, v_s, sems)
    group = context_grad(dy.r, wo.r, c.r, rl.r, first, heads, dc_s, dd_s)
    dct = dc_s[...].T
    qt = q.r[:, group].T
    half = heads * HEAD_DIM
    for h in range(heads):
        cols = head_cols(h)
        wide = slice(h * AUG, h * AUG + HEAD_DIM)
        for i in range(2):
            rows = slice(i * QB, (i + 1) * QB)
            dp = dg(dc_s[rows, cols], v.r[:, wide], 1, 1)
            e[h].r
            ds_s[rows] = (e_s[h, rows].astype(F32) * (dp - dd_s[rows, h : h + 1])).astype(BF16)
        kv_out.r[half + h * HEAD_DIM : half + (h + 1) * HEAD_DIM] = dg(dct[cols], e_s[h], 1, 0).astype(BF16)
        kv_out.r[cols] = dg(qt[cols], ds_s[...], 1, 0).astype(BF16)
        dq_out.r[:, cols] = (dg(ds_s[...], k.r[:, wide], 1, 0) * 0.125).astype(BF16)


def self_heads(plan, first, heads, tab, raw, ins, outs, raw_outs, e_s, k_s, v_s, dc_s, dd_s, sems):
    dy, wo, c, rl, q = ins
    kv_out, dq_out = outs
    v, k, e = head_loads(first, heads, raw, e_s, k_s, v_s, sems)
    group = context_grad(dy.r, wo.r, c.r, rl.r, first, heads, dc_s, dd_s)
    dct = dc_s[...].T
    qt = q.r[:, group].T
    half = heads * HEAD_DIM
    arrive([v, k] + e)

    def attend(core):
        n_lo, n_hi = QB * (core + 1), QB * (4 - core)
        total = k_s.shape[0]
        for h in range(heads):
            cols = head_cols(h)
            wide = slice(h * AUG, h * AUG + HEAD_DIM)
            sums = []
            at = 0
            for i, keys in enumerate((n_lo, n_hi)):
                rows = slice(i * QB, (i + 1) * QB)
                eh = e_s[h, :, at : at + keys]
                dp = dg(dc_s[rows, cols], v_s[:keys, wide], 1, 1)
                ds = (eh.astype(F32) * (dp - dd_s[rows, h : h + 1])).astype(BF16)
                dq_out.r[rows, cols] = (dg(ds, k_s[:keys, wide], 1, 0) * 0.125).astype(BF16)
                sums.append((dg(qt[cols, rows], ds, 1, 0), dg(dct[cols, rows], eh, 1, 0)))
                at += keys
            for j in range(2):
                low, high = sums[0][j], sums[1][j]
                at = j * half + h * HEAD_DIM
                rows = slice(at, at + HEAD_DIM)
                kv_out.r[rows, :n_lo] = (low + high[:, :n_lo]).astype(BF16)
                kv_out.r[rows, n_lo:n_hi] = high[:, n_lo:].astype(BF16)
                if n_hi < total:
                    kv_out.r[rows, n_hi:] = jnp.zeros((HEAD_DIM, total - n_hi), BF16)

    for core in range(2):
        pl.when(tab[plan.at["half"]] == core)(functools.partial(attend, core))


def stack_heads(parts, dst):
    at = 0
    for j in range(2):
        for p in parts:
            half = p.shape[0] // 2
            dst[at : at + half] = p[j * half : (j + 1) * half]
            at += half


def share_rows(plan, tab, src, send, base, keep):
    n, tok = plan.rows, plan.tok
    for t in range(n):
        for name, dst, at in (("sib%d", send, base), ("own%d", keep, 0)):
            row = pl.multiple_of(tab[plan.at[name % t]] * tok, tok)
            dst[at + t * tok : at + (t + 1) * tok] = src[pl.ds(row, tok)].astype(BF16)


def cross_dense(plan, groups, padded, tab, raw, ins, outs, raw_outs, m_s, kv_s, f_s, z_s, sems):
    dqs, ins = ins[:groups], ins[groups:]
    wcq, dy2, n1, r1, g1, b1, small_in = ins[:7]
    kvs, (c2, c1, wckv) = ins[7 : 7 + groups], ins[7 + groups :]
    dy_out, c_send, c_keep, m_keep = outs
    pieces = gather_rows(tab, plan, row_names(plan), raw, m_s, sems)
    mine = tab[plan.at["half"]]
    dqb = jnp.concatenate([v.r[...] for v in dqs], axis=1)
    dz1 = dy2.r[...] + dg(dqb, wcq.r[...], 1, 1)
    dy1, dg1, db1 = norm_back(dz1, n1.r[...], r1.r[...], g1.r[...])
    width = dy1.shape[1]
    step = width // 2
    dy_out.r[...] = dy1
    dy_out.send()
    da1 = dy1.astype(BF16)
    da2 = dy2.r[...].astype(BF16)
    z_s[...] = (n1.r[...] * g1.r[...] + b1.r[...]).astype(BF16)
    tiny = jnp.concatenate([dg1, db1, small_in.r[:6]], axis=0)
    stack_heads([v.r for v in kvs], kv_s)
    f_s[...] = dg(kv_s[...], wckv.r[...], 0, 1)
    share_rows(plan, tab, f_s, c_send.r, padded, m_keep.r)
    m_keep.send()
    arrive(pieces)
    for store, side in ((c_send, 1 - mine), (c_keep, mine)):
        dst = store.r
        at = pl.multiple_of(side * step, step)
        ckv = dg(m_s[:, pl.ds(at, step)], kv_s[...], 0, 1).astype(BF16)
        dst[:step] = ckv[:, :width]
        dst[step : 2 * step] = ckv[:, width:]
        dst[2 * step : 3 * step] = dg(z_s[:, pl.ds(at, step)], dqb, 0, 0).astype(BF16)
        dst[3 * step : 4 * step] = dg(c2.r[:, pl.ds(at, step)], da2, 0, 0).astype(BF16)
        dst[4 * step : 5 * step] = dg(c1.r[:, pl.ds(at, step)], da1, 0, 0).astype(BF16)
        dst[5 * step : 5 * step + 8] = jnp.where(side == 0, tiny, 0.0).astype(BF16)
        dst[5 * step + 8 : padded] = jnp.zeros((padded - 5 * step - 8, width), BF16)
        store.send()


def self_dense(plan, groups, padded, tab, raw, ins, outs, raw_outs, x_s, kv_s, xo_s, f_s, sems):
    kvs, dqs, (wqkv, dy1) = ins[:groups], ins[groups : 2 * groups], ins[2 * groups :]
    s_send, s_keep, x_keep = outs
    pieces = gather_rows(tab, plan, row_names(plan), raw, x_s, sems)
    lo = pl.multiple_of(tab[plan.at["lo"]] * QB, QB)
    hi = pl.multiple_of(tab[plan.at["hi"]] * QB, QB)
    width = x_s.shape[1]
    step = width // 2
    mine = tab[plan.at["half"]]
    stack_heads([v.r for v in kvs], kv_s)
    dqb = jnp.concatenate([v.r[...] for v in dqs], axis=1)
    arrive(pieces)
    xo_s[:QB] = x_s[pl.ds(lo, QB)]
    xo_s[QB:] = x_s[pl.ds(hi, QB)]
    for store, side in ((s_keep, mine), (s_send, 1 - mine)):
        dst = store.r
        at = pl.multiple_of(side * step, step)
        dst[:step] = dg(xo_s[:, pl.ds(at, step)], dqb, 0, 0).astype(BF16)
        kv = dg(x_s[:, pl.ds(at, step)], kv_s[...], 0, 1).astype(BF16)
        dst[step : 2 * step] = kv[:, :width]
        dst[2 * step : 3 * step] = kv[:, width:]
        if padded > 3 * step:
            dst[3 * step : padded] = jnp.zeros((padded - 3 * step, width), BF16)
    s_keep.send()
    w = wqkv.r
    f_s[...] = dg(kv_s[...], w[:, width:], 0, 1)
    dx = dy1.r[...] + dg(dqb, w[:, :width], 1, 1)
    f_s[pl.ds(lo, QB)] += dx[:QB]
    f_s[pl.ds(hi, QB)] += dx[QB:]
    share_rows(plan, tab, f_s, s_send.r, padded, x_keep.r)


def halve_kernel(cols, tab, ins, outs):
    keep, got = ins[0], ins[1:]
    kept, sends = outs[0], outs[1:]
    half = keep.shape[0] // 2
    size = half // 2
    for i in range(2):
        src, base = (got[0], i * half) if len(got) == 1 else (got[i], 0)
        mine = tab[cols[i]]
        for dst, block in ((kept.at[i * size : (i + 1) * size], mine), (sends[i], 1 - mine)):
            at = pl.multiple_of(i * half + block * size, size)
            there = pl.multiple_of(base + block * size, size)
            dst[...] = (keep[pl.ds(at, size)].astype(F32) + src[pl.ds(there, size)].astype(F32)).astype(BF16)


def split_kernel(col, tab, ins, outs):
    size, me = outs[0].shape[0], tab[col]
    for r, dst in enumerate(outs):
        at = pl.multiple_of((me ^ r) * size, size)
        total = ins[0][pl.ds(at, size)].astype(F32)
        for p in ins[1:]:
            total += p[pl.ds(at, size)].astype(F32)
        dst[...] = total.astype(BF16)


def block_kernel(kinds, names, tab, ins, outs):
    parts = []
    for kind, count in kinds:
        parts.append((kind, ins[:count], ins[0].shape[0]))
        ins = ins[count:]
    me = tab[names] if len(outs) > 1 else 0
    at = 0
    for kind, arrays, rows in parts:
        share = rows // len(outs)
        for r, dst in enumerate(outs):
            cuts = [(0, share, None)]
            if len(outs) > 1:
                start = pl.multiple_of((me ^ r) * share, share)
            else:
                start = 0
            if kind == "halves":
                half = rows // 2
                if len(outs) == 1:
                    cuts = [(0, half, arrays[1]), (half, half, arrays[2])]
                    for base, size, src in cuts:
                        total = arrays[0][base : base + size].astype(F32) + src[...].astype(F32)
                        dst[at + base : at + base + size] = total.astype(BF16)
                    continue
                inner = pl.multiple_of(lax.rem(start, half), share)
                in_b = start >= half
                for flag, src in ((False, arrays[1]), (True, arrays[2])):

                    @pl.when(in_b == flag)
                    def _(src=src, dst=dst, start=start, inner=inner, share=share, at=at):
                        total = arrays[0][pl.ds(start, share)].astype(F32) + src[pl.ds(inner, share)].astype(F32)
                        dst[at : at + share] = total.astype(BF16)

                continue
            total = arrays[0][pl.ds(start, share)].astype(F32)
            for p in arrays[1:]:
                total += p[pl.ds(start, share)].astype(F32)
            dst[at : at + share] = total.astype(BF16)
        at += rows // len(outs)


def unblock_kernel(rows, name, tab, ins, outs):
    me, out = tab[name], outs[0]
    at = to = 0
    for n in rows:
        for r, src in enumerate(ins):
            out[pl.ds(pl.multiple_of(to + (me ^ r) * n, n), n)] = src[at : at + n]
        at += n
        to += n * len(ins)


class Halving:
    def __init__(self, plan, tab, keep, got):
        self.plan, self.tab, self.kept, self.got = plan, tab, keep, [got]

    def halve(self, i, deps=()):
        rows, width = self.kept.shape
        shapes = [((n, width), BF16) for n in (rows // 2, rows // 4, rows // 4)]
        cols = [self.plan.at["step%d%s" % (i, side)] for side in "ab"]
        out = small(functools.partial(halve_kernel, cols), self.tab, [self.kept, *self.got], shapes, deps)
        self.kept = out[0]
        self.got = [swap(v, self.plan, bit) for v, bit in zip(out[1:], self.plan.steps[i])]
        return self.kept

    kind = ("halves", 3)


class Direct:
    def __init__(self, plan, tab, rows, keep, got):
        self.plan, self.tab, self.rows, self.kept, self.got = plan, tab, rows, keep, [got]

    def split(self, i, deps=()):
        stage = self.plan.near[i]
        n = 2 ** len(stage[1])
        self.rows //= n
        shapes = [((self.rows, self.kept.shape[1]), BF16)] * n
        kernel = functools.partial(split_kernel, self.plan.at["near%d" % i])
        out = small(kernel, self.tab, [self.kept, *self.got], shapes, deps)
        self.kept, self.got = out[0], [meet(out[r], stage, r) for r in range(1, n)]
        return self.kept

    @property
    def kind(self):
        return ("sum", 1 + len(self.got))


class Far:
    def __init__(self, plan, tab, chunks):
        self.plan, self.tab = plan, tab
        self.rows = [c.kept.shape[0] for c in chunks]
        self.width = chunks[0].kept.shape[1]
        self.kinds = [c.kind for c in chunks]
        self.parts = [v for c in chunks for v in (c.kept, *c.got)]

    def cut(self, n, name, deps):
        self.rows = [v // n for v in self.rows]
        kernel = functools.partial(block_kernel, self.kinds, name)
        self.kinds = [("sum", n)]
        return small(kernel, self.tab, self.parts, [((sum(self.rows), self.width), BF16)] * n, deps)

    def total(self, deps=()):
        return self.cut(1, 0, deps)[0]

    def scatter(self, i, deps=()):
        stage = self.plan.stages[i]
        n = 2 ** len(stage[1])
        out = self.cut(n, self.plan.at["far%d" % i], deps)
        self.parts = [out[0]] + [meet(out[r], stage, r) for r in range(1, n)]
        return out[0]

    def gather(self, i, own, deps=()):
        stage = self.plan.stages[i]
        n = 2 ** len(stage[1])
        ins = [own] + [meet(own, stage, r) for r in range(1, n)]
        kernel = functools.partial(unblock_kernel, self.rows, self.plan.at["far%d" % i])
        self.rows = [v * n for v in self.rows]
        return small(kernel, self.tab, ins, [((sum(self.rows), self.width), BF16)], deps)[0]


def halves_kernel(tab, ins, outs):
    half = ins[0].shape[0] // 2
    for i, dst in enumerate(outs):
        dst[...] = ins[0][i * half : (i + 1) * half]


def join_kernel(cols, tab, ins, outs):
    own, *got = ins
    size = own.shape[0] // 2
    for i in range(2):
        mine = tab[cols[i]]
        for src, block in ((own.at[i * size : (i + 1) * size], mine), (got[i], 1 - mine)):
            at = pl.multiple_of(block * size, size)
            value = src[...]
            outs[1 + i][pl.ds(at, size)] = value
            outs[0][pl.ds(pl.multiple_of(2 * i * size + at, size), size)] = value


class Doubling:
    def __init__(self, plan, tab, own, deps):
        self.plan, self.tab, self.own = plan, tab, own
        rows, self.width = own.shape
        self.apart = small(halves_kernel, tab, [own], [((rows // 2, self.width), BF16)] * 2, deps)
        self.move(len(plan.steps) - 1)

    def move(self, i):
        self.got = [swap(v, self.plan, bit) for v, bit in zip(self.apart, self.plan.steps[i])]

    def join(self, i, deps=()):
        cols = [self.plan.at["step%d%s" % (i, side)] for side in "ab"]
        rows = self.own.shape[0]
        shapes = [((n, self.width), BF16) for n in (2 * rows, rows, rows)]
        self.own, *self.apart = small(
            functools.partial(join_kernel, cols), self.tab, [self.own, *self.got], shapes, deps
        )
        self.move(i - 1)

    def both(self, after):
        mine, _ = lax.optimization_barrier(([self.own, *self.got], after))
        return mine + [swap(v, self.plan, self.plan.core) for v in mine]


def near_parts(plan, own):
    out = [((), own)]
    for stage in plan.near:
        n = 2 ** len(stage[1])
        out = [(r + (k,), v if k == 0 else meet(v, stage, k)) for k in range(n) for r, v in out]
    return out


def both_cores(plan, parts):
    return [(r, side, v if side == 0 else swap(v, plan, plan.core)) for side in range(2) for r, v in parts]


def halving_at(plan, tab, diff, rows, i):
    size = rows // 2
    at = i * size
    for j in range(len(plan.steps)):
        size //= 2
        axis, shift = plan.steps[j][i]
        flip = 0
        for (_, shifts, _), d in zip(plan.near, diff):
            if shift in shifts:
                flip = (d >> shifts.index(shift)) & 1
        at = at + (tab[plan.at["step%d%s" % (j, "ab"[i])]] ^ flip) * size
    return at, size


def direct_at(plan, tab, diff, rows):
    at, size = 0, rows
    for j, ((_, shifts, _), d) in enumerate(zip(plan.near, diff)):
        size >>= len(shifts)
        at = at + (tab[plan.at["near%d" % j]] ^ d) * size
    return at, size


def feed_final(plan, tab, raw, ins, outs, raw_outs):
    down, up, mark = outs
    mark.r[...] = jnp.zeros(mark.r.shape, F32)
    mine = tab[plan.at["half"]]
    bits = [tab[plan.at["step0" + side]] for side in "ab"]
    half = down.r.shape[0] // 2
    size = half // 2

    def put(far, flip, a, b):
        side = mine ^ far
        at = pl.multiple_of(side * half + (bits[0] ^ flip) * size, size)
        down.r[pl.ds(at, size)] = a.astype(F32)
        at = pl.multiple_of(side * half + (bits[1] ^ flip) * size, size)
        up.r[:, pl.ds(at, size)] = b.astype(F32)

    for far in range(2):
        own, a, b = ins[3 * far : 3 * far + 3]
        put(far, 0, own.r[:size], own.r[size:])
        put(far, 1, a.r[...], b.r[...])


def rest_final(plan, diffs, c_rows, s_rows, tab, raw, ins, outs, raw_outs, c_s, s_s):
    qkv, ckv, cq, co, so, tiny = outs
    width = qkv.r.shape[0]
    step = width // 2
    for (diff, far), load in zip(diffs, ins):
        src = load.r
        base = 0
        for i in range(2):
            at, size = halving_at(plan, tab, diff, c_rows, i)
            c_s[far, pl.ds(pl.multiple_of(at, size), size)] = src[base : base + size]
            base += size
        at, size = direct_at(plan, tab, diff, s_rows)
        s_s[far, pl.ds(pl.multiple_of(at, size), size)] = src[base : base + size]
    mine = tab[plan.at["half"]]
    places = [pl.ds(pl.multiple_of((mine ^ far) * step, step), step) for far in range(2)]
    for i in range(3):
        for far, at in enumerate(places):
            qkv.r[at, i * width : (i + 1) * width] = s_s[far, i * step : (i + 1) * step].astype(F32)
    qkv.send()
    for i in range(2):
        for far, at in enumerate(places):
            ckv.r[at, i * width : (i + 1) * width] = c_s[far, i * step : (i + 1) * step].astype(F32)
    ckv.send()
    for i, dst in enumerate((cq, co, so)):
        for far, at in enumerate(places):
            dst.r[at] = c_s[far, (2 + i) * step : (3 + i) * step].astype(F32)
        dst.send()
    tail = slice(5 * step, 5 * step + 8)
    tiny.r[...] = c_s[0, tail].astype(F32) + c_s[1, tail].astype(F32)


def row_blocks(x, plan, scalar):
    return [lax.dynamic_index_in_dim(x, scalar("row%d" % t), 0, keepdims=False) for t in range(plan.rows)]


def to_rows(blocks, plan):
    return [lax.ppermute(b, AXES, plan.perms[t]) for t, b in enumerate(blocks)]


def send_back(parts, plan):
    return [lax.ppermute(p, AXES, [(d, s) for s, d in plan.perms[t]]) for t, p in enumerate(parts)]


def give_kernel(plan, tab, raw, ins, outs, raw_outs):
    tok = plan.tok
    for t, dst in enumerate(outs):
        rows = slice(t * tok, (t + 1) * tok)
        for i in range(2):
            keep, got = raw[2 * i : 2 * i + 2]
            base = got.shape[0] - plan.rows * tok
            came = got[base + t * tok : base + (t + 1) * tok].astype(F32)
            dst.r[i * tok : (i + 1) * tok] = (keep[rows].astype(F32) + came).astype(BF16)
        dst.send()


def take_kernel(plan, tab, raw, ins, outs, raw_outs):
    *arrays, mark = outs
    tok = plan.tok
    for t, load in enumerate(ins):
        row = tab[plan.at["row%d" % t]]
        for i, dst in enumerate(arrays):
            dst.r[row] = load.r[i * tok : (i + 1) * tok].astype(dst.r.dtype)
    mark.r[...] = jnp.zeros(mark.r.shape, F32)


def body(plan, tokens, memory, tgt_seg, mem_seg, cotangent, w_qkv, w_so, w_cq, w_ckv, w_co, w_up, w_down, *norms):
    n, tok, width = tokens.shape
    length = tgt_seg.shape[1]
    heads = width // HEAD_DIM
    ff = w_up.shape[1]
    own = length // 2
    g1, b1, g2, b2, g3, b3 = (v.reshape(1, width) for v in norms)
    known = plan.scalars()
    scalar = lambda name: known[name]
    tab = jnp.stack([known[name] for name in plan.at])

    segs = jnp.stack([tgt_seg, mem_seg])
    if plan.pair_in_dp:
        far = swap(segs, plan, plan.core)
        segs = jnp.where(scalar("seg_far") == 1, far, segs)
    segs = lax.dynamic_index_in_dim(segs, scalar("seg_row"), 1, keepdims=False)
    lane = jnp.arange(HEAD_DIM)[None, :]
    qf = (segs[0][:, None] == lane).astype(BF16)
    kf, mf = (jnp.where((s[:, None] != lane) & (lane < 3), OFF, 0.0).astype(BF16) for s in segs)

    def both(parts):
        return parts + [swap(p, plan, plan.core) for p in parts]

    x_own = to_rows(row_blocks(tokens, plan, scalar), plan)
    x_parts = both(x_own)
    blocks, x_own = lax.optimization_barrier((row_blocks(memory, plan, scalar), x_own))
    m_own = to_rows(blocks, plan)
    blocks, x_parts = lax.optimization_barrier((row_blocks(cotangent, plan, scalar), x_parts))
    g_parts = to_rows(blocks, plan)

    arr = lambda r, c, d=F32: ((r, c), d)
    low = lambda r, c: ((r, c), BF16)
    vs = lambda r, c, d=BF16: pltpu.VMEM((r, c), d)
    sem = lambda k: pltpu.SemaphoreType.DMA((k,))
    wide = heads * AUG
    e_self, e_cross = (heads, QB, 5 * QB), (heads, own, length)

    q1, k1, v1, rl1, c1, n1, r1, cq, e1 = big(
        functools.partial(self_forward, plan, heads),
        tab,
        x_parts,
        [w_qkv, qf, kf, w_so, g1, b1, w_cq],
        [
            low(own, width),
            low(length, wide),
            low(length, wide),
            arr(own, heads),
            low(own, width),
            arr(own, width),
            arr(own, 1),
            low(own, width),
        ],
        [vs(length, width), pltpu.VMEM(e_self, BF16), sem(2 * n), sem(heads)],
        14,
        raw_outs=[(e_self, BF16)],
    )
    m_own, cq = lax.optimization_barrier((m_own, cq))
    m_parts = both(m_own)
    k2, v2, rl2, c2, n2, r2, e2 = big(
        functools.partial(cross_forward, plan, heads),
        tab,
        m_parts,
        [w_ckv, qf, mf, cq, w_co, n1, g1, b1],
        [low(length, wide), low(length, wide), arr(own, heads), low(own, width), arr(own, width), arr(own, 1)],
        [vs(length, width), pltpu.VMEM(e_cross, BF16), sem(2 * n), sem(heads)],
        15,
        raw_outs=[(e_cross, BF16)],
    )
    f_send, f_keep, du, dy3, tiny, *o_rows = big(
        functools.partial(feed, plan),
        tab,
        g_parts,
        [n2, g2, b2, w_up, w_down, g3, b3],
        [low(ff, width), low(ff, width), low(own, ff), arr(own, width), arr(8, width)]
        + [low(tok, width)] * n,
        [vs(own, width), vs(own, ff), sem(n)],
        12,
    )
    f = Halving(plan, tab, f_keep, swap(f_send, plan, plan.core))
    dy2, tiny = big(
        feed_inputs, tab, [], [du, w_up, dy3, n2, r2, g2, tiny], [arr(own, width), arr(8, width)], [], 4, mib=20
    )
    steps = len(plan.steps)
    kept = f.halve(0, [dy2])
    groups = 2

    def backward(first, some, kernel, raw, ins, extra, us, deps):
        cols = some * HEAD_DIM
        return big(
            functools.partial(kernel, first, some),
            tab,
            raw,
            ins,
            [low(2 * cols, length), low(own, cols)],
            [
                pltpu.VMEM((some,) + raw[0].shape[1:], BF16),
                vs(length, some * AUG),
                vs(length, some * AUG),
                vs(own, cols),
                vs(own, some, F32),
                sem(2 + some),
            ]
            + extra,
            us,
            deps=deps,
            raw_spec=HB,
        )

    early = heads * 3 // 4
    cross_part = lambda i, deps: backward(
        i * early, (early, heads - early)[i], cross_heads, [e2, k2, v2], [dy2, w_co, c2, rl2, cq], [vs(own, length)], 9, deps
    )
    kv_a, dq_a = cross_part(0, [kept])
    for i in range(1, steps):
        kept = f.halve(i, [dq_a])
    out_back = send_back(o_rows, plan)
    kv_b, dq_b = cross_part(1, [kept, dq_a])
    f = Far(plan, tab, [f])
    kept = f.scatter(0, [dq_b])
    c_rows, s_rows = plan.padded(3 * width), plan.padded(3 * width // 2)
    dy1, c_send, c_keep, m_keep = big(
        functools.partial(cross_dense, plan, groups, c_rows),
        tab,
        m_parts,
        [dq_a, dq_b, w_cq, dy2, n1, r1, g1, b1, tiny, kv_a, kv_b, c2, c1, w_ckv],
        [arr(own, width), low(c_rows + own, width), low(c_rows, width), low(own, width)],
        [vs(length, width), vs(2 * width, length), vs(length, width, F32), vs(own, width), sem(2 * n)],
        11,
        deps=[kept, *out_back],
    )
    for i in range(1, len(plan.stages)):
        f.scatter(i, [dy1])
    f_own = f.total([dy1])
    for i in reversed(range(1, len(plan.stages))):
        f_own = f.gather(i, f_own)
    c_send, f_own = lax.optimization_barrier((c_send, f_own))
    c_got = swap(c_send, plan, plan.core)
    c = Halving(plan, tab, c_keep, c_got)
    kept = c.halve(0)
    kv_c, dq_c = backward(
        0, heads, functools.partial(self_heads, plan), [e1, k1, v1], [dy1, w_so, c1, rl1, q1], [], 13, [f_own, kept]
    )
    f_own = f.gather(0, f_own, [dq_c])
    for i in range(1, steps):
        kept = c.halve(i, [dq_c])
    s_send, s_keep, x_keep = big(
        functools.partial(self_dense, plan, 1, s_rows),
        tab,
        x_parts,
        [kv_c, dq_c, w_qkv, dy1],
        [low(s_rows + own, width), low(s_rows, width), low(own, width)],
        [vs(length, width), vs(2 * width, length), vs(own, width), vs(length, width, F32), sem(2 * n)],
        7,
        deps=[f_own, kept],
    )
    s_got = swap(s_send, plan, plan.core)
    s = Direct(plan, tab, s_rows, s_keep, s_got)
    for i in range(len(plan.near)):
        s.split(i)
    rest = Far(plan, tab, [c, s])
    for i in range(len(plan.stages)):
        kept = rest.scatter(i)
    f = Doubling(plan, tab, f_own, [kept])
    rest_own = rest.total()
    for i in reversed(range(1, steps)):
        f.join(i, [rest_own])
    for i in reversed(range(1, len(plan.stages))):
        rest_own = rest.gather(i, rest_own)

    def finish(kernel, arrays, outs, scratch, more=(), deps=()):
        diffs = [(diff, far) for diff, far, _ in arrays]
        return big(
            functools.partial(kernel, plan, diffs, *more), tab, [], [v for _, _, v in arrays], outs, scratch, 5, deps=deps
        )

    def take(parts, kinds):
        outs = [((n, tok, width), d) for d in kinds] + [arr(8, 128)]
        return big(functools.partial(take_kernel, plan), tab, [], parts, outs, [], 2)

    output, mark = take(out_back, [BF16])
    rest_own = rest.gather(0, rest_own, [mark, *f.got])
    rest_near = near_parts(plan, rest_own)
    turns = big(
        functools.partial(give_kernel, plan),
        tab,
        [m_keep, c_got, x_keep, s_got],
        [],
        [low(2 * tok, width)] * n,
        [],
        2,
        deps=[rest_own],
        raw_spec=VM,
    )
    back = send_back(turns, plan)
    down, up, late = big(
        functools.partial(feed_final, plan),
        tab,
        [],
        f.both(turns[0]),
        [arr(ff, width), arr(width, ff), arr(8, 128)],
        [],
        5,
    )
    arrays, late, back = lax.optimization_barrier(([v for _, v in rest_near], late, back))
    all_rest = both_cores(plan, [(d, v) for (d, _), v in zip(rest_near, arrays)])
    grad_memory, grad_tokens, mark = take(back, [F32, F32])
    qkv, ckv, d_cq, d_co, d_so, tiny = finish(
        rest_final,
        all_rest,
        [arr(width, 3 * width), arr(width, 2 * width)] + [arr(width, width)] * 3 + [arr(8, width)],
        [pltpu.VMEM((2, c_rows, width), BF16), pltpu.VMEM((2, s_rows, width), BF16)],
        (c_rows, s_rows),
        [late],
    )
    return (output, grad_tokens, grad_memory, qkv, d_so, d_cq, ckv, d_co, up, down) + tuple(
        tiny[i] for i in range(6)
    )


def solution(mesh):
    def whole(*args):
        rows = args[0].shape[0] // mesh.shape["dp"]
        tok = args[0].shape[1] // mesh.shape["seq"]
        plan = Plan(mesh, rows, tok)
        split, copied = P("dp", "seq", None), P()
        return jax.shard_map(
            functools.partial(body, plan),
            mesh=mesh,
            in_specs=(split, split, P("dp", None), P("dp", None), split) + (copied,) * 13,
            out_specs=(split,) * 3 + (copied,) * 13,
            check_vma=False,
        )(*args)

    return whole
```
